512 devices in a mesh: dp: 2 (over z_lo), row: 8 (over x, core), col: 32 (over y, z_hi).
Axes of the slice: x: 4, y: 8, z: 8 (z_hi: 4, z_lo: 2; z = z_hi * 2 + z_lo), core: 2. Of those that a mesh axis runs over, the one named last changes fastest.
Arguments:
- features: bfloat16 [2, 64, 64, 16, 256], P('dp', 'col', 'row'), may hold values from -10.5 to 10.5
- w_qkv: bfloat16 [256, 768], replicated, may hold values from -0.375 to 0.375
- w_out: bfloat16 [256, 256], replicated, may hold values from -0.375 to 0.375
- cotangent: bfloat16 [2, 64, 64, 16, 256], P('dp', 'col', 'row'), may hold values from -6 to 6
Outputs:
- update: bfloat16 [2, 64, 64, 16, 256], P('dp', 'col', 'row')
- grad_in: bfloat16 [2, 64, 64, 16, 256], P('dp', 'col', 'row')
- grad_qkv: float32 [256, 768], replicated
- grad_out: float32 [256, 256], replicated
The draws below stay inside these ranges and needn't reach their ends.
All inputs are finite; a program needn't handle non-finite values.
Results may differ from the reference program's by a relative error of at most 0.017.
The reference program's roundings to bfloat16 on the way count: a program that leaves them out, or rounds other values in their place, can miss the bound.
Values may be sent and summed in bfloat16 or wider, within the bound.
No kernel may reach another device: no remote copies, remote signals or barrier semaphores. Data moves between devices by JAX's collectives and lax.ppermute only.
A program may use at most 64 MiB of HBM per device.

```python
import math
import jax
import jax.numpy as jnp
from jax import lax

C = 256
HEADS = 8
Z = 16
PATCHES = 2
Y = 64
X = 64


def draw_features(key, part):
    key = jax.random.fold_in(key, 11)
    shape = (PATCHES, Y, X, Z, C)
    first = jax.random.fold_in(key, 0)
    base = jnp.clip(jax.random.normal(first, shape, jnp.float32), -4.0, 4.0)
    return base.astype(jnp.bfloat16)


def shard_levels(own_key, dims, cuts, least, top_value):
    gain, own = 1.0, jax.random.fold_in(own_key, 6)
    for axis_at, blocks in cuts:
        steps = jnp.exp(jax.random.uniform(jax.random.fold_in(own, axis_at), (blocks,), jnp.float32, least / len(cuts), top_value / len(cuts)))
        gain = gain * jnp.repeat(steps, dims[axis_at] // blocks).reshape([-1 if axis == axis_at else 1 for axis in range(len(dims))])
    return gain


def noise(stream_key, extent, scale, most, cuts=(), held_as=jnp.bfloat16):
    gain = shard_levels(stream_key, extent, cuts, -0.22, 0.18) if cuts else 1.0
    values = jax.random.normal(stream_key, extent, jnp.float32) * scale * gain
    return jnp.minimum(jnp.maximum(values, -most), most).astype(held_as)


def setup_inputs(seed: int = 0) -> dict:
    streams_of = jax.random.split(jax.random.key(seed), 5)
    return {
        "features": draw_features(jax.random.fold_in(streams_of[4], 71), 0),
        "w_qkv": noise(streams_of[1], (C, 3 * C), C ** -0.5, 0.375),
        "w_out": noise(streams_of[2], (C, C), C ** -0.5, 0.375),
        "cotangent": noise(streams_of[3], (PATCHES, Y, X, Z, C), 1.0, 6.0, ((0, 2), (1, 32), (2, 8))),
    }


def split_heads(line_block):
    leading = line_block.shape[:3]
    model_width = line_block.shape[3] // 3
    parts = line_block.reshape(leading + (3, HEADS, model_width // HEADS)).astype(jnp.float32)
    return (parts[:, :, :, 0], parts[:, :, :, 1], parts[:, :, :, 2], model_width)

def weights_of(queries, key_heads):
    score_scale = 1.0 / math.sqrt(queries.shape[-1])
    scores = jnp.einsum('albhd,ambhd->abhlm', queries, key_heads) * score_scale
    return jax.nn.softmax(scores, axis=-1)

def attend(line_block):
    queries, key_heads, values, model_width = split_heads(line_block)
    rounded = weights_of(queries, key_heads).astype(jnp.bfloat16).astype(jnp.float32)
    mixed = jnp.einsum('abhlm,ambhd->albhd', rounded, values)
    return mixed.reshape(line_block.shape[:3] + (model_width,)).astype(jnp.bfloat16)

def attend_back(line_block, upstream):
    queries, key_heads, values, model_width = split_heads(line_block)
    score_scale = 1.0 / math.sqrt(queries.shape[-1])
    weights_full = weights_of(queries, key_heads)
    rounded = weights_full.astype(jnp.bfloat16).astype(jnp.float32)
    upstream_heads = upstream.reshape(queries.shape).astype(jnp.float32)
    dprobs = jnp.einsum('albhd,ambhd->abhlm', upstream_heads, values)
    dvalues = jnp.einsum('abhlm,albhd->ambhd', rounded, upstream_heads)
    dscores = weights_full * (dprobs - lax.optimization_barrier(jnp.sum(dprobs * weights_full, axis=-1, keepdims=True))) * score_scale
    dround = dscores.astype(jnp.bfloat16).astype(jnp.float32)
    dqueries = jnp.einsum('abhlm,ambhd->albhd', dround, key_heads)
    dkeys = jnp.einsum('abhlm,albhd->ambhd', dround, queries)
    stacked = jnp.stack([dqueries, dkeys, dvalues], axis=3)
    return stacked.reshape(line_block.shape[:3] + (3 * model_width,)).astype(jnp.bfloat16)

def along_lines(func, arrays, axis):
    moved = [jnp.moveaxis(array_in, axis, 3) for array_in in arrays]
    inner = moved[0].shape[:4]
    length = inner[3]
    count = inner[0] * inner[1] * inner[2]
    lines_per = math.gcd(count, 64)
    blocks = tuple((m.reshape(count // lines_per, lines_per, length, 1, m.shape[-1]) for m in moved))
    result = lax.map(lambda pieces: func(*pieces), blocks)
    result = result.reshape(inner + (result.shape[-1],))
    return jnp.moveaxis(result, 3, axis)

def reference(features, w_qkv, w_out, cotangent):
    model_width = features.shape[-1]
    full_shape = features.shape
    feat_rows = features.reshape(-1, model_width)
    proj = jnp.dot(feat_rows, w_qkv, preferred_element_type=jnp.float32).astype(jnp.bfloat16)
    proj = proj.reshape(full_shape[:4] + (3 * model_width,))
    outs = [along_lines(attend, (proj,), axis) for axis in (3, 1, 2)]
    mix = (outs[0].astype(jnp.float32) + outs[1].astype(jnp.float32) + outs[2].astype(jnp.float32)).astype(jnp.bfloat16)
    mix_rows = mix.reshape(-1, model_width)
    update = jnp.dot(mix_rows, w_out, preferred_element_type=jnp.float32).astype(jnp.bfloat16)
    grad_rows = cotangent.reshape(-1, model_width)
    factor = 1.0 / math.sqrt(feat_rows.shape[0])
    grad_out = jnp.dot(mix_rows.T, grad_rows, preferred_element_type=jnp.float32) * factor
    grad_mix = jnp.dot(grad_rows, w_out.T, preferred_element_type=jnp.float32).astype(jnp.bfloat16)
    grad_mix = grad_mix.reshape(full_shape)
    input_total = jnp.zeros((feat_rows.shape[0], model_width), jnp.float32)
    qkv_total = jnp.zeros((model_width, 3 * model_width), jnp.float32)
    for axis in (3, 1, 2):
        dproj = along_lines(attend_back, (proj, grad_mix), axis).reshape(-1, 3 * model_width)
        dfeat = jnp.dot(dproj, w_qkv.T, preferred_element_type=jnp.float32).astype(jnp.bfloat16)
        dfeat = lax.optimization_barrier(dfeat)
        input_total = input_total + dfeat.astype(jnp.float32)
        qkv_total = qkv_total + jnp.dot(feat_rows.T, dproj, preferred_element_type=jnp.float32)
    grad_in = input_total.astype(jnp.bfloat16).reshape(full_shape)
    return (update.reshape(full_shape), grad_in, qkv_total * factor, grad_out)
```

```python
import functools
import math

import jax
import jax.numpy as jnp
from jax import lax
from jax.experimental import pallas as pl
from jax.experimental.pallas import tpu as pltpu
from jax.sharding import PartitionSpec as P

HEADS = 8
DEPTH = 32
C = 256
T = 256
PATCHES = 2
LINES = 4
NEG = -1e30

BF = jnp.bfloat16
F32 = jnp.float32


def nn(a, b):
    return lax.dot_general(a, b, (((1,), (0,)), ((), ())), preferred_element_type=F32)


def nt(a, b):
    return lax.dot_general(a, b, (((1,), (1,)), ((), ())), preferred_element_type=F32)


def iota(axis, shape=(T, T)):
    return lax.broadcasted_iota(jnp.int32, shape, axis)


def y_source(r):
    return ((r // LINES) % 2) * 128 + (r // 8) * LINES + r % LINES


def x_source(r):
    peer = r // 32
    return (peer // 4) * 128 + (r % 8) * 16 + (peer % 4) * LINES + (r // 8) % LINES


def z_line(r):
    return r // 16


def y_line(r):
    return r % LINES


def x_line(r):
    return (r // 8) % LINES


def onehot(hit):
    return jnp.where(hit, 1.0, 0.0).astype(BF)


def pack_body(feat, cot, send_x, send_y):
    for source, out in ((x_source, send_x), (y_source, send_y)):
        pick = onehot(source(iota(0)) == iota(1))
        out[:, :C] = nn(pick, feat[...]).astype(BF)
        out[:, C:] = nn(pick, cot[...]).astype(BF)


def axis_math(line, feat, cot, w_qkv, w_qkv_t, w_out):
    scale = 1.0 / math.sqrt(DEPTH)
    eye = onehot(iota(0) == iota(1))
    feat_t = nt(eye, feat).astype(BF)
    cot_t = nt(eye, cot).astype(BF)
    proj = nn(feat, w_qkv[...]).astype(BF)
    proj_t = nn(w_qkv_t[...], feat_t).astype(BF)
    gmix = nt(cot, w_out[...]).astype(BF)
    gmix_t = nn(w_out[...], cot_t).astype(BF)
    q, k, v = proj[:, :C], proj[:, C : 2 * C], proj[:, 2 * C :]
    q_t, k_t, v_t = proj_t[:C], proj_t[C : 2 * C], proj_t[2 * C :]
    bias = jnp.where(line(iota(0)) == line(iota(1)), 0.0, NEG)
    head_of_row = iota(0) // DEPTH
    head_of_lane = iota(1) // DEPTH
    zero = jnp.zeros((T, C), BF)
    out_t = []
    dq_t = []
    dk = jnp.zeros((T, C), F32)
    dv = jnp.zeros((T, C), F32)
    for h in range(HEADS):
        rows = slice(h * DEPTH, (h + 1) * DEPTH)
        on_row = head_of_row == h
        on_lane = head_of_lane == h
        scores = nn(k, jnp.where(on_row, q_t, zero)) + bias
        top = jnp.max(scores, axis=0, keepdims=True)
        e = jnp.exp((scores - top) * scale)
        probs = e * (1.0 / jnp.sum(e, axis=0, keepdims=True))
        rounded = probs.astype(BF)
        out_t.append(nn(v_t[rows], rounded))
        dv += nn(rounded, jnp.where(on_lane, gmix, zero))
        dprobs = nn(v, jnp.where(on_row, gmix_t, zero))
        mean = jnp.sum(dprobs * probs, axis=0, keepdims=True)
        dround = (probs * (dprobs - mean) * scale).astype(BF)
        dq_t.append(nn(k_t[rows], dround))
        dk += nn(dround, jnp.where(on_lane, q, zero))
    out_t = jnp.concatenate(out_t, axis=0).astype(BF)
    dq_t = jnp.concatenate(dq_t, axis=0).astype(BF)
    out = nt(eye, out_t).astype(BF)
    dq = nt(eye, dq_t).astype(BF)
    dk = dk.astype(BF)
    dv = dv.astype(BF)
    dfeat = (
        nn(dq, w_qkv_t[:C]) + nn(dk, w_qkv_t[C : 2 * C]) + nn(dv, w_qkv_t[2 * C :])
    ).astype(BF)
    return out, dfeat, (nn(feat_t, dq), nn(feat_t, dk), nn(feat_t, dv), nn(out_t, cot))


def z_body(feat, cot, w_qkv, w_qkv_t, w_out, back, grad):
    back[:, :C], back[:, C:], terms = axis_math(z_line, feat[...], cot[...], w_qkv, w_qkv_t, w_out)
    for at, term in enumerate(terms):
        grad[:, at * C : (at + 1) * C] = term


def x_body(got, w_qkv, w_qkv_t, w_out, grad_so_far, back, grad):
    back[:, :C], back[:, C:], terms = axis_math(
        x_line, got[:, :C], got[:, C:], w_qkv, w_qkv_t, w_out
    )
    for at, term in enumerate(terms):
        cols = slice(at * C, (at + 1) * C)
        grad[:, cols] = grad_so_far[:, cols] + term


def y_body(got, w_qkv, w_qkv_t, w_out, grad_so_far, back_x, back, send_row):
    back[:, :C], back[:, C:], terms = axis_math(
        y_line, got[:, :C], got[:, C:], w_qkv, w_qkv_t, w_out
    )
    send_row[:, : 2 * C] = back_x[...]
    for at, term in enumerate(terms):
        cols = slice(at * C, (at + 1) * C)
        send_row[:, 2 * C + at * C : 3 * C + at * C] = (grad_so_far[:, cols] + term).astype(BF)


def row_sum_body(got_row, back_y, send_col):
    send_col[:, : 2 * C] = back_y[...]
    total = jnp.zeros((32, 4 * C), F32)
    for peer in range(8):
        total += got_row[peer * 32 : (peer + 1) * 32, 2 * C :].astype(F32)
    tiles = jnp.concatenate([total[:, j * 128 : (j + 1) * 128] for j in range(8)], axis=0)
    r = iota(0)
    pick = onehot(iota(1) == (r % 8) * 32 + r // 8)
    send_col[:, 2 * C :] = nn(pick, tiles.astype(BF)).astype(BF)


def col_sum_body(got_col, send):
    total = jnp.zeros((8, 128), F32)
    for peer in range(32):
        total += got_col[peer * 8 : (peer + 1) * 8, 2 * C :].astype(F32)
    send[...] = jnp.concatenate([total] * 64, axis=0).astype(BF)


def dp_sum_body(factor, got, send):
    total = ((got[:256].astype(F32) + got[256:].astype(F32)) * factor).astype(BF)
    r = iota(0)
    pick = onehot(iota(1) == (r % 32) * 8 + r // 32)
    tiles = nn(pick, total)
    rows = jnp.concatenate([tiles[j * 32 : (j + 1) * 32] for j in range(8)], axis=1).astype(BF)
    for peer in range(8):
        send[peer * 32 : (peer + 1) * 32] = rows


def final_body(back_z, back_y, back_x, w_out, update, grad_in):
    put_y = onehot(iota(0) == y_source(iota(1)))
    put_x = onehot(iota(0) == x_source(iota(1)))
    total = (
        back_z[...].astype(F32) + nn(put_y, back_y[:, : 2 * C]) + nn(put_x, back_x[:, : 2 * C])
    ).astype(BF)
    update[...] = nn(total[:, :C], w_out[...]).astype(BF)
    grad_in[...] = total[:, C:]


def call(body, outs, flops, *args):
    vmem = pl.BlockSpec(memory_space=pltpu.VMEM)
    return pl.pallas_call(
        body,
        out_shape=outs,
        in_specs=[vmem] * len(args),
        out_specs=[vmem] * len(outs),
        compiler_params=pltpu.CompilerParams(vmem_limit_bytes=40 * 2**20),
        cost_estimate=pl.CostEstimate(flops=flops, bytes_accessed=2**20, transcendentals=2**19),
    )(*args)


def shape(rows, cols, dtype):
    return jax.ShapeDtypeStruct((rows, cols), dtype)


def exchange(rows, axis):
    return lax.all_to_all(rows, axis, split_axis=0, concat_axis=0, tiled=True)


def body(features, w_qkv, w_out, cotangent):
    local_shape = features.shape
    feat = features.reshape(T, C)
    cot = cotangent.reshape(T, C)
    weights = (w_qkv, w_qkv.T, w_out)
    cube = 2 * T * T * C
    back_shape = shape(T, 2 * C, BF)
    grad_shape = shape(C, 4 * C, F32)
    send_x, send_y = call(pack_body, [back_shape] * 2, cube * 4, feat, cot)
    got_x = exchange(send_x, "row")
    back_z, grad = call(z_body, [back_shape, grad_shape], cube * 70, feat, cot, *weights)
    got_y = exchange(send_y, "col")
    back_x, grad = call(x_body, [back_shape, grad_shape], cube * 70, got_x, *weights, grad)
    back_y, send_row = call(
        y_body, [back_shape, shape(T, 6 * C, BF)], cube * 70, got_y, *weights, grad, back_x
    )
    got_row = exchange(send_row, "row")
    (send_col,) = call(row_sum_body, [shape(T, 2 * C + 128, BF)], cube, got_row, back_y)
    got_col = exchange(send_col, "col")
    (send_rest,) = call(col_sum_body, [shape(512, 128, BF)], 2**20, got_col)
    got_rest = exchange(send_rest, ("dp", "col"))
    update, grad_in = call(
        final_body, [shape(T, C, BF)] * 2, cube * 6, back_z, got_col, got_row, w_out
    )
    factor = 1.0 / math.sqrt(PATCHES * 64 * 64 * 16)
    (send_last,) = call(
        functools.partial(dp_sum_body, factor), [shape(C, 4 * C, BF)], cube, got_rest
    )
    whole = exchange(send_last, "row")
    return (
        update.reshape(local_shape),
        grad_in.reshape(local_shape),
        whole[:, : 3 * C].astype(F32),
        whole[:, 3 * C :].astype(F32),
    )


def solution(mesh):
    placed = (P("dp", "col", "row", None, None), P(), P(), P("dp", "col", "row", None, None))
    return jax.shard_map(
        body,
        mesh=mesh,
        in_specs=placed,
        out_specs=(P("dp", "col", "row", None, None), P("dp", "col", "row", None, None), P(), P()),
        check_vma=False,
    )
```

```python
import functools
import math

import jax
import jax.numpy as jnp
from jax import lax
from jax.experimental import pallas as pl
from jax.experimental.pallas import tpu as pltpu
from jax.sharding import PartitionSpec as P

HEADS = 8
DEPTH = 32
C = 256
T = 256
PATCHES = 2
Z = 16
HALF = 128
QUAD = 4
LINES = 4
NEG = -1e30

BF = jnp.bfloat16
F32 = jnp.float32


def nn(a, b):
    return lax.dot_general(a, b, (((1,), (0,)), ((), ())), preferred_element_type=F32)


def nt(a, b):
    return lax.dot_general(a, b, (((1,), (1,)), ((), ())), preferred_element_type=F32)


def iota(axis, shape=(T, T)):
    return lax.broadcasted_iota(jnp.int32, shape, axis)


def y_source(r):
    return ((r // LINES) % 2) * 128 + (r // 8) * LINES + r % LINES


def x_source(r):
    peer = r // 32
    return (peer // 4) * 128 + (r % 8) * 16 + (peer % 4) * LINES + (r // 8) % LINES


def y_sorted(r):
    return (r % 64) * LINES + r // 64


def x_sorted(r):
    return (r % 64) // 8 * 32 + r // 64 * 8 + r % 8


def z_line(r):
    return r // Z


def long_line(r):
    return r // 64


def onehot(hit):
    return jnp.where(hit, 1.0, 0.0).astype(BF)


def send(source, feat, cot, out):
    pick = onehot(source(iota(0)) == iota(1))
    out[:, :C] = nn(pick, feat).astype(BF)
    out[:, C:] = nn(pick, cot).astype(BF)


def pack_body(feat_hbm, cot_hbm, send_x, feat, cot, sem):
    copies = [
        pltpu.make_async_copy(feat_hbm, feat, sem.at[0]),
        pltpu.make_async_copy(cot_hbm, cot, sem.at[1]),
    ]
    for copy in copies:
        copy.start()
    for copy in copies:
        copy.wait()
    send(x_source, feat[...], cot[...], send_x)


def axis_math(source, line, feat, cot, w_qkv, w_qkv_t, w_out):
    scale = 1.0 / math.sqrt(DEPTH)
    eye = onehot(iota(0) == iota(1))
    if source is None:
        unsort = eye
    else:
        sort = onehot(source(iota(0)) == iota(1))
        unsort = onehot(iota(0) == source(iota(1)))
        feat = nn(sort, feat).astype(BF)
        cot = nn(sort, cot).astype(BF)
    feat_t = nt(eye, feat).astype(BF)
    cot_t = nt(eye, cot).astype(BF)
    proj = nn(feat, w_qkv[...]).astype(BF)
    proj_t = nn(w_qkv_t[...], feat_t).astype(BF)
    gmix = nt(cot, w_out[...]).astype(BF)
    gmix_t = nn(w_out[...], cot_t).astype(BF)
    q, k, v = proj[:, :C], proj[:, C : 2 * C], proj[:, 2 * C :]
    q_t, k_t, v_t = proj_t[:C], proj_t[C : 2 * C], proj_t[2 * C :]
    wide = (HALF, QUAD * HALF)
    bias = jnp.where(line(iota(0, wide)) == line(iota(1, wide) % HALF), 0.0, NEG)
    head_of_lane = iota(1, (HALF, HALF)) // DEPTH
    blank = jnp.zeros((HALF, HALF), BF)
    strip = jnp.zeros((DEPTH, HALF), BF)

    def spread(a_t):
        return jnp.concatenate(
            [
                jnp.concatenate(
                    [a_t[i * DEPTH : (i + 1) * DEPTH] if i == j else strip for i in range(QUAD)],
                    axis=0,
                )
                for j in range(QUAD)
            ],
            axis=1,
        )

    def stack(a):
        return jnp.concatenate(
            [jnp.where(head_of_lane == j, a, blank) for j in range(QUAD)], axis=0
        )

    def per_head(a_t, m):
        return jnp.concatenate(
            [
                nn(a_t[j * DEPTH : (j + 1) * DEPTH], m[:, j * HALF : (j + 1) * HALF])
                for j in range(QUAD)
            ],
            axis=0,
        )

    parts = []
    for half in range(2):
        toks = slice(half * HALF, (half + 1) * HALF)
        for quad in range(2):
            chans = slice(quad * HALF, (quad + 1) * HALF)
            scores = nn(k[toks, chans], spread(q_t[chans, toks])) + bias
            top = jnp.max(scores, axis=0, keepdims=True)
            e = jnp.exp((scores - top) * scale)
            probs = e * (1.0 / jnp.sum(e, axis=0, keepdims=True))
            rounded = probs.astype(BF)
            out_t = per_head(v_t[chans, toks], rounded)
            dv = nn(rounded, stack(gmix[toks, chans]))
            dprobs = nn(v[toks, chans], spread(gmix_t[chans, toks]))
            mean = jnp.sum(dprobs * probs, axis=0, keepdims=True)
            dround = (probs * (dprobs - mean) * scale).astype(BF)
            dq_t = per_head(k_t[chans, toks], dround)
            dk = nn(dround, stack(q[toks, chans]))
            parts.append([m.astype(BF) for m in (out_t, dq_t, dk, dv)])

    def whole(at, transposed):
        p = [[parts[2 * half + quad][at] for quad in range(2)] for half in range(2)]
        if transposed:
            p = [[p[j][i] for j in range(2)] for i in range(2)]
        return jnp.concatenate([jnp.concatenate(r, axis=1) for r in p], axis=0)

    out_t, dq_t = whole(0, True), whole(1, True)
    dk, dv = whole(2, False), whole(3, False)
    out = nt(unsort, out_t).astype(BF)
    dq = nt(eye, dq_t).astype(BF)
    dfeat = (
        nn(dq, w_qkv_t[:C]) + nn(dk, w_qkv_t[C : 2 * C]) + nn(dv, w_qkv_t[2 * C :])
    ).astype(BF)
    if source is not None:
        dfeat = nn(unsort, dfeat).astype(BF)
    return out, dfeat, (nn(feat_t, dq), nn(feat_t, dk), nn(feat_t, dv), nn(out_t, cot))


def z_body(feat, cot, w_qkv, w_qkv_t, w_out, back, grad, send_y):
    send(y_source, feat[...], cot[...], send_y)
    back[:, :C], back[:, C:], terms = axis_math(None, z_line, feat[...], cot[...], w_qkv, w_qkv_t, w_out)
    for at, term in enumerate(terms):
        grad[:, at * C : (at + 1) * C] = term


def x_body(got, w_qkv, w_qkv_t, w_out, grad_so_far, back, grad):
    back[:, :C], back[:, C:], terms = axis_math(
        x_sorted, long_line, got[:, :C], got[:, C:], w_qkv, w_qkv_t, w_out
    )
    for at, term in enumerate(terms):
        cols = slice(at * C, (at + 1) * C)
        grad[:, cols] = grad_so_far[:, cols] + term


def y_body(got, w_qkv, w_qkv_t, w_out, grad_so_far, back_x, back, send_row):
    back[:, :C], back[:, C:], terms = axis_math(
        y_sorted, long_line, got[:, :C], got[:, C:], w_qkv, w_qkv_t, w_out
    )
    send_row[:, : 2 * C] = back_x[...]
    for at, term in enumerate(terms):
        cols = slice(at * C, (at + 1) * C)
        send_row[:, 2 * C + at * C : 3 * C + at * C] = (grad_so_far[:, cols] + term).astype(BF)


def row_sum_body(got_row, back_y, send_col):
    send_col[:, : 2 * C] = back_y[...]
    total = jnp.zeros((32, 4 * C), F32)
    for peer in range(8):
        total += got_row[peer * 32 : (peer + 1) * 32, 2 * C :].astype(F32)
    tiles = jnp.concatenate([total[:, j * 128 : (j + 1) * 128] for j in range(8)], axis=0)
    r = iota(0)
    pick = onehot(iota(1) == (r % 8) * 32 + r // 8)
    send_col[:, 2 * C :] = nn(pick, tiles.astype(BF)).astype(BF)


def col_sum_body(got_col, send):
    total = jnp.zeros((8, 128), F32)
    for peer in range(32):
        total += got_col[peer * 8 : (peer + 1) * 8, 2 * C :].astype(F32)
    send[...] = jnp.concatenate([total] * 64, axis=0).astype(BF)


def dp_sum_body(factor, got, send):
    total = ((got[:256].astype(F32) + got[256:].astype(F32)) * factor).astype(BF)
    r = iota(0)
    pick = onehot(iota(1) == (r % 32) * 8 + r // 32)
    tiles = nn(pick, total)
    rows = jnp.concatenate([tiles[j * 32 : (j + 1) * 32] for j in range(8)], axis=1).astype(BF)
    for peer in range(8):
        send[peer * 32 : (peer + 1) * 32] = rows


def final_body(back_z, back_y, back_x, w_out, update, grad_in):
    put_y = onehot(iota(0) == y_source(iota(1)))
    put_x = onehot(iota(0) == x_source(iota(1)))
    total = (
        back_z[...].astype(F32) + nn(put_y, back_y[:, : 2 * C]) + nn(put_x, back_x[:, : 2 * C])
    ).astype(BF)
    update[...] = nn(total[:, :C], w_out[...]).astype(BF)
    grad_in[...] = total[:, C:]


def unpack_body(got, grad_qkv, grad_out):
    grad_qkv[...] = got[:, : 3 * C].astype(F32)
    grad_out[...] = got[:, 3 * C :].astype(F32)


def call(body, outs, flops, *args, space=pltpu.VMEM, scratch=(), grant=40 * 2**20):
    vmem = pl.BlockSpec(memory_space=pltpu.VMEM)
    return pl.pallas_call(
        body,
        out_shape=outs,
        in_specs=[pl.BlockSpec(memory_space=space)] * len(args),
        scratch_shapes=scratch,
        out_specs=[vmem] * len(outs),
        compiler_params=pltpu.CompilerParams(vmem_limit_bytes=grant),
        cost_estimate=pl.CostEstimate(flops=flops, bytes_accessed=2**20, transcendentals=2**19),
    )(*args)


def shape(rows, cols, dtype):
    return jax.ShapeDtypeStruct((rows, cols), dtype)


def exchange(rows, axis):
    return lax.all_to_all(rows, axis, split_axis=0, concat_axis=0, tiled=True)


def body(features, w_qkv, w_out, cotangent):
    local_shape = features.shape
    feat = features.reshape(T, C)
    cot = cotangent.reshape(T, C)
    weights = (w_qkv, w_qkv.T, w_out)
    cube = 2 * T * T * C
    back_shape = shape(T, 2 * C, BF)
    grad_shape = shape(C, 4 * C, F32)
    (send_x,) = call(
        pack_body,
        [back_shape],
        cube * 2,
        feat,
        cot,
        space=pltpu.HBM,
        scratch=[pltpu.VMEM((T, C), BF), pltpu.VMEM((T, C), BF), pltpu.SemaphoreType.DMA((2,))],
        grant=None,
    )
    got_x = exchange(send_x, "row")
    back_z, grad, send_y = call(
        z_body, [back_shape, grad_shape, back_shape], cube * 70, feat, cot, *weights
    )
    got_y = exchange(send_y, "col")
    back_x, grad = call(x_body, [back_shape, grad_shape], cube * 70, got_x, *weights, grad)
    back_y, send_row = call(
        y_body, [back_shape, shape(T, 6 * C, BF)], cube * 70, got_y, *weights, grad, back_x
    )
    got_row = exchange(send_row, "row")
    (send_col,) = call(row_sum_body, [shape(T, 2 * C + 128, BF)], cube, got_row, back_y)
    got_col = exchange(send_col, "col")
    (send_rest,) = call(col_sum_body, [shape(512, 128, BF)], 2**20, got_col)
    got_rest = exchange(send_rest, ("dp", "col"))
    update, grad_in = call(
        final_body, [shape(T, C, BF)] * 2, cube * 6, back_z, got_col, got_row, w_out
    )
    factor = 1.0 / math.sqrt(PATCHES * 64 * 64 * 16)
    (send_last,) = call(
        functools.partial(dp_sum_body, factor), [shape(C, 4 * C, BF)], cube, got_rest
    )
    whole = exchange(send_last, "row")
    grad_qkv, grad_out = call(
        unpack_body, [shape(C, 3 * C, F32), shape(C, C, F32)], 2**20, whole
    )
    return (update.reshape(local_shape), grad_in.reshape(local_shape), grad_qkv, grad_out)


def solution(mesh):
    placed = (P("dp", "col", "row", None, None), P(), P(), P("dp", "col", "row", None, None))
    return jax.shard_map(
        body,
        mesh=mesh,
        in_specs=placed,
        out_specs=(P("dp", "col", "row", None, None), P("dp", "col", "row", None, None), P(), P()),
        check_vma=False,
    )
```

```python
import functools
import math

import jax
import jax.numpy as jnp
from jax import lax
from jax.experimental import pallas as pl
from jax.experimental.pallas import tpu as pltpu
from jax.sharding import PartitionSpec as P

HEADS = 8
DEPTH = 32
C = 256
T = 256
PATCHES = 2
Z = 16
HALF = 128
QUAD = 4
LINES = 4
NEG = -1e30

BF = jnp.bfloat16
F32 = jnp.float32


def nn(a, b):
    return lax.dot_general(a, b, (((1,), (0,)), ((), ())), preferred_element_type=F32)


def nt(a, b):
    return lax.dot_general(a, b, (((1,), (1,)), ((), ())), preferred_element_type=F32)


def iota(axis, shape=(T, T)):
    return lax.broadcasted_iota(jnp.int32, shape, axis)


def y_source(r):
    return ((r // LINES) % 2) * 128 + (r // 8) * LINES + r % LINES


def x_source(r):
    peer = r // 16
    return (peer // 8) * 128 + (r % 8) * 16 + (peer % 8) * 2 + (r // 8) % 2


def y_sorted(r):
    return (r % 64) * LINES + r // 64


def x_sorted(r):
    return r // 128 * 128 + (r % 64) // 8 * 16 + (r // 64) % 2 * 8 + r % 8


def z_line(r):
    return r // Z


def long_line(r):
    return r // 64


def onehot(hit):
    return jnp.where(hit, 1.0, 0.0).astype(BF)


def send(source, feat, cot, out):
    pick = onehot(source(iota(0)) == iota(1))
    out[:, :C] = nn(pick, feat).astype(BF)
    out[:, C:] = nn(pick, cot).astype(BF)


def pack_body(feat_hbm, cot_hbm, send_x, feat, cot, sem):
    copies = [
        pltpu.make_async_copy(feat_hbm, feat, sem.at[0]),
        pltpu.make_async_copy(cot_hbm, cot, sem.at[1]),
    ]
    for copy in copies:
        copy.start()
    for copy in copies:
        copy.wait()
    send(x_source, feat[...], cot[...], send_x)


def axis_math(source, line, feat, cot, w_qkv, w_qkv_t, w_out):
    scale = 1.0 / math.sqrt(DEPTH)
    eye = onehot(iota(0) == iota(1))
    if source is None:
        unsort = eye
    else:
        sort = onehot(source(iota(0)) == iota(1))
        unsort = onehot(iota(0) == source(iota(1)))
        feat = nn(sort, feat).astype(BF)
        cot = nn(sort, cot).astype(BF)
    feat_t = nt(eye, feat).astype(BF)
    cot_t = nt(eye, cot).astype(BF)
    proj = nn(feat, w_qkv[...]).astype(BF)
    proj_t = nn(w_qkv_t[...], feat_t).astype(BF)
    gmix = nt(cot, w_out[...]).astype(BF)
    gmix_t = nn(w_out[...], cot_t).astype(BF)
    q, k, v = proj[:, :C], proj[:, C : 2 * C], proj[:, 2 * C :]
    q_t, k_t, v_t = proj_t[:C], proj_t[C : 2 * C], proj_t[2 * C :]
    wide = (HALF, QUAD * HALF)
    bias = jnp.where(line(iota(0, wide)) == line(iota(1, wide) % HALF), 0.0, NEG)
    head_of_lane = iota(1, (HALF, HALF)) // DEPTH
    blank = jnp.zeros((HALF, HALF), BF)
    strip = jnp.zeros((DEPTH, HALF), BF)

    def spread(a_t):
        return jnp.concatenate(
            [
                jnp.concatenate(
                    [a_t[i * DEPTH : (i + 1) * DEPTH] if i == j else strip for i in range(QUAD)],
                    axis=0,
                )
                for j in range(QUAD)
            ],
            axis=1,
        )

    def stack(a):
        return jnp.concatenate(
            [jnp.where(head_of_lane == j, a, blank) for j in range(QUAD)], axis=0
        )

    def per_head(a_t, m):
        return jnp.concatenate(
            [
                nn(a_t[j * DEPTH : (j + 1) * DEPTH], m[:, j * HALF : (j + 1) * HALF])
                for j in range(QUAD)
            ],
            axis=0,
        )

    blocks = [
        (slice(half * HALF, (half + 1) * HALF), slice(quad * HALF, (quad + 1) * HALF))
        for half in range(2)
        for quad in range(2)
    ]
    all_scores = [nn(k[t, c], spread(q_t[c, t])) + bias for t, c in blocks]
    all_dprobs = [nn(v[t, c], spread(gmix_t[c, t])) for t, c in blocks]
    soft = []
    for scores, dprobs in zip(all_scores, all_dprobs):
        top = jnp.max(scores, axis=0, keepdims=True)
        e = jnp.exp((scores - top) * scale)
        probs = e * (1.0 / jnp.sum(e, axis=0, keepdims=True))
        mean = jnp.sum(dprobs * probs, axis=0, keepdims=True)
        soft.append((probs.astype(BF), (probs * (dprobs - mean) * scale).astype(BF)))
    parts = []
    for (t, c), (rounded, dround) in zip(blocks, soft):
        out_t = per_head(v_t[c, t], rounded)
        dv = nn(rounded, stack(gmix[t, c]))
        dq_t = per_head(k_t[c, t], dround)
        dk = nn(dround, stack(q[t, c]))
        parts.append([m.astype(BF) for m in (out_t, dq_t, dk, dv)])

    def whole(at, transposed):
        p = [[parts[2 * half + quad][at] for quad in range(2)] for half in range(2)]
        if transposed:
            p = [[p[j][i] for j in range(2)] for i in range(2)]
        return jnp.concatenate([jnp.concatenate(r, axis=1) for r in p], axis=0)

    out_t, dq_t = whole(0, True), whole(1, True)
    dk, dv = whole(2, False), whole(3, False)
    out = nt(unsort, out_t).astype(BF)
    dq = nt(eye, dq_t).astype(BF)
    dfeat = (
        nn(dq, w_qkv_t[:C]) + nn(dk, w_qkv_t[C : 2 * C]) + nn(dv, w_qkv_t[2 * C :])
    ).astype(BF)
    if source is not None:
        dfeat = nn(unsort, dfeat).astype(BF)
    return out, dfeat, (nn(feat_t, dq), nn(feat_t, dk), nn(feat_t, dv), nn(out_t, cot))


def z_body(feat, cot, w_qkv, w_qkv_t, w_out, back, grad, send_y):
    send(y_source, feat[...], cot[...], send_y)
    back[:, :C], back[:, C:], terms = axis_math(None, z_line, feat[...], cot[...], w_qkv, w_qkv_t, w_out)
    for at, term in enumerate(terms):
        grad[:, at * C : (at + 1) * C] = term.astype(BF)


def x_body(got, w_qkv, w_qkv_t, w_out, grad_so_far, back, grad):
    back[:, :C], back[:, C:], terms = axis_math(
        x_sorted, long_line, got[:, :C], got[:, C:], w_qkv, w_qkv_t, w_out
    )
    for at, term in enumerate(terms):
        cols = slice(at * C, (at + 1) * C)
        grad[:, cols] = (grad_so_far[:, cols].astype(F32) + term).astype(BF)


def core():
    return lax.rem(lax.axis_index("row"), 2)


def y_body(got, w_qkv, w_qkv_t, w_out, grad_so_far, back, keep, give, total):
    back[:, :C], back[:, C:], terms = axis_math(
        y_sorted, long_line, got[:, :C], got[:, C:], w_qkv, w_qkv_t, w_out
    )
    for at, term in enumerate(terms):
        cols = slice(at * C, (at + 1) * C)
        total[:, cols] = grad_so_far[:, cols].astype(F32) + term
    mine = core()
    keep[...] = total[pl.ds(pl.multiple_of(mine * 128, 128), 128)]
    give[...] = total[pl.ds(pl.multiple_of((1 - mine) * 128, 128), 128)].astype(BF)


def col_pack_body(back_y, keep, took, send_col):
    send_col[:, : 2 * C] = back_y[...]
    half = (keep[...] + took[...].astype(F32)).astype(BF)
    send_col[:128, 2 * C :] = half[:, : 2 * C]
    send_col[128:, 2 * C :] = half[:, 2 * C :]


def row_pack_body(got_col, back_x, send_row):
    send_row[:, : 2 * C] = back_x[...]
    block = jnp.sum(got_col[:, 2 * C :].astype(F32).reshape(32, 8, 2 * C), axis=0)
    block = jnp.concatenate([block[:, :C], block[:, C:]], axis=0)
    send_row[:, 2 * C :] = jnp.concatenate([block] * 16, axis=0).astype(BF)


def last_pack_body(factor, got_row, send):
    mine = core()
    block = jnp.zeros((16, C), F32)
    for peer in range(8):
        at = pl.multiple_of((2 * peer + mine) * 16, 16)
        block += got_row[pl.ds(at, 16), 2 * C :].astype(F32)
    send[...] = jnp.concatenate([block * factor] * 32, axis=0).astype(BF)


def final_body(back_z, back_y, back_x, w_out, update, grad_in):
    put_y = onehot(iota(0) == y_source(iota(1)))
    put_x = onehot(iota(0) == x_source(iota(1)))
    total = (
        back_z[...].astype(F32) + nn(put_y, back_y[:, : 2 * C]) + nn(put_x, back_x[:, : 2 * C])
    ).astype(BF)
    update[...] = nn(total[:, :C], w_out[...]).astype(BF)
    grad_in[...] = total[:, C:]


def unpack_body(mine, other, grad_qkv, grad_out):
    for src, half in ((mine, core()), (other, 1 - core())):
        rows = pl.ds(pl.multiple_of(half * 128, 128), 128)
        tiles = src[...].astype(F32).reshape(2, 16, 2, 8, C)
        for at in range(4):
            block = tiles[at // 2, :, at % 2].reshape(128, C)
            if at < 3:
                grad_qkv[rows, at * C : (at + 1) * C] = block
            else:
                grad_out[rows, :] = block


def call(body, outs, flops, *args, space=pltpu.VMEM, scratch=(), grant=40 * 2**20):
    vmem = pl.BlockSpec(memory_space=pltpu.VMEM)
    return pl.pallas_call(
        body,
        out_shape=outs,
        in_specs=[pl.BlockSpec(memory_space=space)] * len(args),
        scratch_shapes=scratch,
        out_specs=[vmem] * len(outs),
        compiler_params=pltpu.CompilerParams(vmem_limit_bytes=grant),
        cost_estimate=pl.CostEstimate(flops=flops, bytes_accessed=2**20, transcendentals=2**19),
    )(*args)


def shape(rows, cols, dtype):
    return jax.ShapeDtypeStruct((rows, cols), dtype)


def exchange(rows, axis):
    return lax.all_to_all(rows, axis, split_axis=0, concat_axis=0, tiled=True)


def swap(rows):
    return lax.ppermute(rows, "row", [(i, i ^ 1) for i in range(8)])


def body(features, w_qkv, w_out, cotangent):
    local_shape = features.shape
    feat = features.reshape(T, C)
    cot = cotangent.reshape(T, C)
    weights = (w_qkv, w_qkv.T, w_out)
    cube = 2 * T * T * C
    back_shape = shape(T, 2 * C, BF)
    grad_shape = shape(C, 4 * C, BF)
    (send_x,) = call(
        pack_body,
        [back_shape],
        cube * 2,
        feat,
        cot,
        space=pltpu.HBM,
        scratch=[pltpu.VMEM((T, C), BF), pltpu.VMEM((T, C), BF), pltpu.SemaphoreType.DMA((2,))],
        grant=None,
    )
    got_x = exchange(send_x, ("dp", "row"))
    back_z, grad, send_y = call(
        z_body, [back_shape, grad_shape, back_shape], cube * 70, feat, cot, *weights
    )
    got_y = exchange(send_y, "col")
    back_x, grad = call(x_body, [back_shape, grad_shape], cube * 70, got_x, *weights, grad)
    back_y, keep, give = call(
        y_body,
        [back_shape, shape(128, 4 * C, F32), shape(128, 4 * C, BF)],
        cube * 70,
        got_y,
        *weights,
        grad,
        scratch=[pltpu.VMEM((C, 4 * C), F32)],
    )
    took = swap(give)
    (send_col,) = call(col_pack_body, [shape(T, 4 * C, BF)], 2**20, back_y, keep, took)
    got_col = exchange(send_col, "col")
    (send_row,) = call(row_pack_body, [shape(T, 3 * C, BF)], 2**20, got_col, back_x)
    got_row = exchange(send_row, ("dp", "row"))
    factor = 1.0 / math.sqrt(PATCHES * 64 * 64 * 16)
    (send_last,) = call(
        functools.partial(last_pack_body, factor), [shape(512, C, BF)], 2**20, got_row
    )
    mine = exchange(send_last, "col")
    update, grad_in = call(
        final_body, [shape(T, C, BF)] * 2, cube * 6, back_z, got_col, got_row, w_out
    )
    grad_qkv, grad_out = call(
        unpack_body, [shape(C, 3 * C, F32), shape(C, C, F32)], 2**20, mine, swap(mine)
    )
    return (update.reshape(local_shape), grad_in.reshape(local_shape), grad_qkv, grad_out)


def solution(mesh):
    placed = (P("dp", "col", "row", None, None), P(), P(), P("dp", "col", "row", None, None))
    return jax.shard_map(
        body,
        mesh=mesh,
        in_specs=placed,
        out_specs=(P("dp", "col", "row", None, None), P("dp", "col", "row", None, None), P(), P()),
        check_vma=False,
    )
```

```python
import functools
import math

import jax
import jax.numpy as jnp
from jax import lax
from jax.experimental import pallas as pl
from jax.experimental.pallas import tpu as pltpu
from jax.sharding import PartitionSpec as P

HEADS = 8
DEPTH = 32
C = 256
T = 256
PATCHES = 2
Z = 16
HALF = 128
QUAD = 4
LINES = 4
NEG = -1e30

BF = jnp.bfloat16
F32 = jnp.float32


def nn(a, b):
    return lax.dot_general(a, b, (((1,), (0,)), ((), ())), preferred_element_type=F32)


def nt(a, b):
    return lax.dot_general(a, b, (((1,), (1,)), ((), ())), preferred_element_type=F32)


def iota(axis, shape=(T, T)):
    return lax.broadcasted_iota(jnp.int32, shape, axis)


def y_source(r):
    return ((r // LINES) % 2) * 128 + (r // 8) * LINES + r % LINES


def x_source(r):
    peer = r // 16
    return (peer // 8) * 128 + (r % 8) * 16 + (peer % 8) * 2 + (r // 8) % 2


def y_sorted(r):
    return (r % 64) * LINES + r // 64


def x_sorted(r):
    return r // 128 * 128 + (r % 64) // 8 * 16 + (r // 64) % 2 * 8 + r % 8


def z_line(r):
    return r // Z


def long_line(r):
    return r // 64


def onehot(hit):
    return jnp.where(hit, 1.0, 0.0).astype(BF)


def send(source, feat, cot, out):
    pick = onehot(source(iota(0)) == iota(1))
    out[:, :C] = nn(pick, feat).astype(BF)
    out[:, C:] = nn(pick, cot).astype(BF)


def pack_body(feat_hbm, cot_hbm, send_x, feat, cot, sorted_rows, sem):
    copies = [
        pltpu.make_async_copy(feat_hbm, feat, sem.at[0]),
        pltpu.make_async_copy(cot_hbm, cot, sem.at[1]),
    ]
    for copy in copies:
        copy.start()
    pick = onehot(x_source(iota(0)) == iota(1))
    outs = []
    for at, (copy, rows) in enumerate(zip(copies, (feat, cot))):
        copy.wait()
        cols = slice(at * C, (at + 1) * C)
        sorted_rows[:, cols] = nn(pick, rows[...]).astype(BF)
        outs.append(
            pltpu.make_async_copy(sorted_rows.at[:, cols], send_x.at[:, cols], sem.at[2 + at])
        )
        outs[at].start()
    for out in outs:
        out.wait()


def axis_math(source, line, feat, cot, w_qkv, w_qkv_t, w_out):
    scale = 1.0 / math.sqrt(DEPTH)
    eye = onehot(iota(0) == iota(1))
    if source is not None:
        sort = onehot(source(iota(0)) == iota(1))
        feat = nn(sort, feat).astype(BF)
        cot = nn(sort, cot).astype(BF)
    feat_t = nt(eye, feat).astype(BF)
    cot_t = nt(eye, cot).astype(BF)
    proj = nn(feat, w_qkv[...]).astype(BF)
    proj_t = nn(w_qkv_t[...], feat_t).astype(BF)
    gmix = nt(cot, w_out[...]).astype(BF)
    gmix_t = nn(w_out[...], cot_t).astype(BF)
    q, k, v = proj[:, :C], proj[:, C : 2 * C], proj[:, 2 * C :]
    q_t, k_t, v_t = proj_t[:C], proj_t[C : 2 * C], proj_t[2 * C :]
    wide = (HALF, QUAD * HALF)
    bias = jnp.where(line(iota(0, wide)) == line(iota(1, wide) % HALF), 0.0, NEG)
    head_of_lane = iota(1, (HALF, HALF)) // DEPTH
    blank = jnp.zeros((HALF, HALF), BF)
    strip = jnp.zeros((DEPTH, HALF), BF)

    def spread(a_t):
        return jnp.concatenate(
            [
                jnp.concatenate(
                    [a_t[i * DEPTH : (i + 1) * DEPTH] if i == j else strip for i in range(QUAD)],
                    axis=0,
                )
                for j in range(QUAD)
            ],
            axis=1,
        )

    def stack(a):
        return jnp.concatenate(
            [jnp.where(head_of_lane == j, a, blank) for j in range(QUAD)], axis=0
        )

    def per_head(a_t, m):
        return jnp.concatenate(
            [
                nn(a_t[j * DEPTH : (j + 1) * DEPTH], m[:, j * HALF : (j + 1) * HALF])
                for j in range(QUAD)
            ],
            axis=0,
        )

    blocks = [
        (slice(half * HALF, (half + 1) * HALF), slice(quad * HALF, (quad + 1) * HALF))
        for half in range(2)
        for quad in range(2)
    ]
    all_scores = [nn(k[t, c], spread(q_t[c, t])) + bias for t, c in blocks]
    all_dprobs = [nn(v[t, c], spread(gmix_t[c, t])) for t, c in blocks]
    soft = []
    for scores, dprobs in zip(all_scores, all_dprobs):
        top = jnp.max(scores, axis=0, keepdims=True)
        e = jnp.exp((scores - top) * scale)
        probs = e * (1.0 / jnp.sum(e, axis=0, keepdims=True))
        mean = jnp.sum(dprobs * probs, axis=0, keepdims=True)
        soft.append((probs.astype(BF), (probs * (dprobs - mean) * scale).astype(BF)))
    parts = []
    for (t, c), (rounded, dround) in zip(blocks, soft):
        out_t = per_head(v_t[c, t], rounded)
        dv = nn(rounded, stack(gmix[t, c]))
        dq_t = per_head(k_t[c, t], dround)
        dk = nn(dround, stack(q[t, c]))
        parts.append([m.astype(BF) for m in (out_t, dq_t, dk, dv)])

    def whole(at, transposed):
        p = [[parts[2 * half + quad][at] for quad in range(2)] for half in range(2)]
        if transposed:
            p = [[p[j][i] for j in range(2)] for i in range(2)]
        return jnp.concatenate([jnp.concatenate(r, axis=1) for r in p], axis=0)

    out_t, dq_t = whole(0, True), whole(1, True)
    dk, dv = whole(2, False), whole(3, False)
    grads = (nt(feat_t, dq_t), nn(feat_t, dk), nn(feat_t, dv), nn(out_t, cot))
    return (out_t, dq_t, dk, dv), grads


def results(source, out_t, dq_t, dk, dv, w_qkv):
    unsort = onehot(iota(0) == (iota(1) if source is None else source(iota(1))))
    out = nt(unsort, out_t).astype(BF)
    dfeat_t = (
        nn(w_qkv[:, :C], dq_t) + nt(w_qkv[:, C : 2 * C], dk) + nt(w_qkv[:, 2 * C :], dv)
    ).astype(BF)
    return out, nt(unsort, dfeat_t).astype(BF)


def z_body(feat, cot, w_qkv, w_qkv_t, w_out, back, grad, send_y):
    send(y_source, feat[...], cot[...], send_y)
    parts, terms = axis_math(None, z_line, feat[...], cot[...], w_qkv, w_qkv_t, w_out)
    back[:, :C], back[:, C:] = results(None, *parts, w_qkv)
    for at, term in enumerate(terms):
        grad[:, at * C : (at + 1) * C] = term.astype(BF)


def x_body(got, w_qkv, w_qkv_t, w_out, grad_so_far, back, grad):
    parts, terms = axis_math(
        x_sorted, long_line, got[:, :C], got[:, C:], w_qkv, w_qkv_t, w_out
    )
    back[:, :C], back[:, C:] = results(x_sorted, *parts, w_qkv)
    for at, term in enumerate(terms):
        cols = slice(at * C, (at + 1) * C)
        grad[:, cols] = (grad_so_far[:, cols].astype(F32) + term).astype(BF)


def core():
    return lax.rem(lax.axis_index("row"), 2)


def y_body(got, w_qkv, w_qkv_t, w_out, grad_so_far, out_t, dq_t, dk, dv, keep, give, total):
    parts, terms = axis_math(
        y_sorted, long_line, got[:, :C], got[:, C:], w_qkv, w_qkv_t, w_out
    )
    for ref, part in zip((out_t, dq_t, dk, dv), parts):
        ref[...] = part
    for at, term in enumerate(terms):
        cols = slice(at * C, (at + 1) * C)
        total[:, cols] = grad_so_far[:, cols].astype(F32) + term
    mine = core()
    keep[...] = total[pl.ds(pl.multiple_of(mine * 128, 128), 128)]
    give[...] = total[pl.ds(pl.multiple_of((1 - mine) * 128, 128), 128)].astype(BF)


def y_back_body(out_t, dq_t, dk, dv, w_qkv, back):
    back[:, :C], back[:, C:] = results(
        y_sorted, out_t[...], dq_t[...], dk[...], dv[...], w_qkv
    )


def col_pack_body(back_y, keep, took, send_col):
    send_col[:, : 2 * C] = back_y[...]
    half = (keep[...] + took[...].astype(F32)).astype(BF)
    send_col[:128, 2 * C :] = half[:, : 2 * C]
    send_col[128:, 2 * C :] = half[:, 2 * C :]


def row_pack_body(got_col, back_x, send_row):
    send_row[:, : 2 * C] = back_x[...]
    block = jnp.sum(got_col[:, 2 * C :].astype(F32).reshape(32, 8, 2 * C), axis=0)
    block = jnp.concatenate([block[:, :C], block[:, C:]], axis=0)
    send_row[:, 2 * C :] = jnp.concatenate([block] * 16, axis=0).astype(BF)


def last_pack_body(factor, got_row, send):
    mine = core()
    block = jnp.zeros((16, C), F32)
    for peer in range(8):
        at = pl.multiple_of((2 * peer + mine) * 16, 16)
        block += got_row[pl.ds(at, 16), 2 * C :].astype(F32)
    send[...] = jnp.concatenate([block * factor] * 32, axis=0).astype(BF)


def final_body(back_z, back_y, back_x, w_out, update, grad_in):
    put_y = onehot(iota(0) == y_source(iota(1)))
    put_x = onehot(iota(0) == x_source(iota(1)))
    total = (
        back_z[...].astype(F32) + nn(put_y, back_y[:, : 2 * C]) + nn(put_x, back_x[:, : 2 * C])
    ).astype(BF)
    update[...] = nn(total[:, :C], w_out[...]).astype(BF)
    grad_in[...] = total[:, C:]


def unpack_body(mine, other, grad_qkv, grad_out):
    for src, half in ((mine, core()), (other, 1 - core())):
        rows = pl.ds(pl.multiple_of(half * 128, 128), 128)
        tiles = src[...].astype(F32).reshape(2, 16, 2, 8, C)
        for at in range(4):
            block = tiles[at // 2, :, at % 2].reshape(128, C)
            if at < 3:
                grad_qkv[rows, at * C : (at + 1) * C] = block
            else:
                grad_out[rows, :] = block


def call(body, outs, flops, *args, space=pltpu.VMEM, scratch=(), grant=40 * 2**20):
    return pl.pallas_call(
        body,
        out_shape=outs,
        in_specs=[pl.BlockSpec(memory_space=space)] * len(args),
        scratch_shapes=scratch,
        out_specs=[pl.BlockSpec(memory_space=space)] * len(outs),
        compiler_params=pltpu.CompilerParams(vmem_limit_bytes=grant),
        cost_estimate=pl.CostEstimate(flops=flops, bytes_accessed=2**20, transcendentals=2**19),
    )(*args)


def shape(rows, cols, dtype):
    return jax.ShapeDtypeStruct((rows, cols), dtype)


def exchange(rows, axis):
    return lax.all_to_all(rows, axis, split_axis=0, concat_axis=0, tiled=True)


def swap(rows):
    return lax.ppermute(rows, "row", [(i, i ^ 1) for i in range(8)])


def body(features, w_qkv, w_out, cotangent):
    local_shape = features.shape
    feat = features.reshape(T, C)
    cot = cotangent.reshape(T, C)
    weights = (w_qkv, w_qkv.T, w_out)
    cube = 2 * T * T * C
    back_shape = shape(T, 2 * C, BF)
    grad_shape = shape(C, 4 * C, BF)
    (send_x,) = call(
        pack_body,
        [back_shape],
        cube * 2,
        feat,
        cot,
        space=pltpu.HBM,
        scratch=[
            pltpu.VMEM((T, C), BF),
            pltpu.VMEM((T, C), BF),
            pltpu.VMEM((T, 2 * C), BF),
            pltpu.SemaphoreType.DMA((4,)),
        ],
        grant=None,
    )
    got_x = exchange(send_x, ("dp", "row"))
    back_z, grad, send_y = call(
        z_body, [back_shape, grad_shape, back_shape], cube * 70, feat, cot, *weights
    )
    got_y = exchange(send_y, "col")
    back_x, grad = call(x_body, [back_shape, grad_shape], cube * 70, got_x, *weights, grad)
    *parts, keep, give = call(
        y_body,
        [shape(T, C, BF)] * 4 + [shape(128, 4 * C, F32), shape(128, 4 * C, BF)],
        cube * 70,
        got_y,
        *weights,
        grad,
        scratch=[pltpu.VMEM((C, 4 * C), F32)],
    )
    took = swap(give)
    (back_y,) = call(y_back_body, [back_shape], cube * 6, *parts, w_qkv)
    (send_col,) = call(col_pack_body, [shape(T, 4 * C, BF)], 2**20, back_y, keep, took)
    got_col = exchange(send_col, "col")
    (send_row,) = call(row_pack_body, [shape(T, 3 * C, BF)], 2**20, got_col, back_x)
    got_row = exchange(send_row, ("dp", "row"))
    factor = 1.0 / math.sqrt(PATCHES * 64 * 64 * 16)
    (send_last,) = call(
        functools.partial(last_pack_body, factor), [shape(512, C, BF)], 2**20, got_row
    )
    mine = exchange(send_last, "col")
    update, grad_in = call(
        final_body, [shape(T, C, BF)] * 2, cube * 6, back_z, got_col, got_row, w_out
    )
    grad_qkv, grad_out = call(
        unpack_body, [shape(C, 3 * C, F32), shape(C, C, F32)], 2**20, mine, swap(mine)
    )
    return (update.reshape(local_shape), grad_in.reshape(local_shape), grad_qkv, grad_out)


def solution(mesh):
    placed = (P("dp", "col", "row", None, None), P(), P(), P("dp", "col", "row", None, None))
    return jax.shard_map(
        body,
        mesh=mesh,
        in_specs=placed,
        out_specs=(P("dp", "col", "row", None, None), P("dp", "col", "row", None, None), P(), P()),
        check_vma=False,
    )
```

```python
import functools
import math

import jax
import jax.numpy as jnp
from jax import lax
from jax.experimental import pallas as pl
from jax.experimental.pallas import tpu as pltpu
from jax.sharding import PartitionSpec as P

HEADS = 8
DEPTH = 32
C = 256
T = 256
PATCHES = 2
Z = 16
HALF = 128
QUAD = 4
LINES = 4
NEG = -1e30

BF = jnp.bfloat16
F32 = jnp.float32


def nn(a, b):
    return lax.dot_general(a, b, (((1,), (0,)), ((), ())), preferred_element_type=F32)


def nt(a, b):
    return lax.dot_general(a, b, (((1,), (1,)), ((), ())), preferred_element_type=F32)


def iota(axis, shape=(T, T)):
    return lax.broadcasted_iota(jnp.int32, shape, axis)


def x_source(r):
    peer = r // 32
    return (peer // 4) * 128 + (r % 8) * Z + (peer % 4) * LINES + (r // 8) % LINES


def x_sorted(t):
    return (t % 64) // 8 * 32 + t // 64 * 8 + t % 8


def y_row(t):
    at = t % 128
    return at // 2 * 8 + t // 128 * 2 + at % 2


def y_sorted(t):
    at = t % 64
    return t // 128 * 256 + at // 2 * 8 + at % 2 * 2 + t // 64 % 2


def z_line(r):
    return r // Z


def long_line(r):
    return r // 64


def onehot(hit):
    return jnp.where(hit, 1.0, 0.0).astype(BF)


def pack_body(feat_hbm, cot_hbm, send_x, feat, cot, sorted_rows, sem):
    copies = [
        pltpu.make_async_copy(feat_hbm, feat, sem.at[0]),
        pltpu.make_async_copy(cot_hbm, cot, sem.at[1]),
    ]
    for copy in copies:
        copy.start()
    pick = onehot(x_source(iota(0)) == iota(1))
    outs = []
    for at, (copy, rows) in enumerate(zip(copies, (feat, cot))):
        copy.wait()
        cols = slice(at * C, (at + 1) * C)
        sorted_rows[:, cols] = nn(pick, rows[...]).astype(BF)
        outs.append(
            pltpu.make_async_copy(sorted_rows.at[:, cols], send_x.at[:, cols], sem.at[2 + at])
        )
        outs[at].start()
    for out in outs:
        out.wait()


def axis_math(line, feat, cot, w_qkv, w_qkv_t, w_out):
    scale = 1.0 / math.sqrt(DEPTH)
    feat_t = nt(onehot(iota(0) == iota(1)), feat).astype(BF)
    proj = nn(feat, w_qkv[...]).astype(BF)
    proj_t = nt(w_qkv_t[...], feat).astype(BF)
    gmix = nt(cot, w_out[...]).astype(BF)
    gmix_t = nt(w_out[...], cot).astype(BF)
    q, k, v = proj[:, :C], proj[:, C : 2 * C], proj[:, 2 * C :]
    q_t, k_t, v_t = proj_t[:C], proj_t[C : 2 * C], proj_t[2 * C :]
    wide = (HALF, QUAD * HALF)
    bias = jnp.where(line(iota(0, wide)) == line(iota(1, wide) % HALF), 0.0, NEG)
    head_of_lane = iota(1, (HALF, HALF)) // DEPTH
    blank = jnp.zeros((HALF, HALF), BF)
    strip = jnp.zeros((DEPTH, HALF), BF)

    def spread(a_t):
        return jnp.concatenate(
            [
                jnp.concatenate(
                    [a_t[i * DEPTH : (i + 1) * DEPTH] if i == j else strip for i in range(QUAD)],
                    axis=0,
                )
                for j in range(QUAD)
            ],
            axis=1,
        )

    def stack(a):
        return jnp.concatenate(
            [jnp.where(head_of_lane == j, a, blank) for j in range(QUAD)], axis=0
        )

    def per_head(a_t, m):
        return jnp.concatenate(
            [
                nn(a_t[j * DEPTH : (j + 1) * DEPTH], m[:, j * HALF : (j + 1) * HALF])
                for j in range(QUAD)
            ],
            axis=0,
        )

    blocks = [
        (slice(half * HALF, (half + 1) * HALF), slice(quad * HALF, (quad + 1) * HALF))
        for half in range(2)
        for quad in range(2)
    ]
    all_scores = [nn(k[t, c], spread(q_t[c, t])) + bias for t, c in blocks]
    all_dprobs = [nn(v[t, c], spread(gmix_t[c, t])) for t, c in blocks]
    soft = []
    for scores, dprobs in zip(all_scores, all_dprobs):
        top = jnp.max(scores, axis=0, keepdims=True)
        e = jnp.exp((scores - top) * scale)
        probs = e * (1.0 / jnp.sum(e, axis=0, keepdims=True))
        mean = jnp.sum(dprobs * probs, axis=0, keepdims=True)
        soft.append((probs.astype(BF), (probs * (dprobs - mean) * scale).astype(BF)))
    parts = []
    for (t, c), (rounded, dround) in zip(blocks, soft):
        out_t = per_head(v_t[c, t], rounded)
        dv = nn(rounded, stack(gmix[t, c]))
        dq_t = per_head(k_t[c, t], dround)
        dk = nn(dround, stack(q[t, c]))
        parts.append([m.astype(BF) for m in (out_t, dq_t, dk, dv)])

    def whole(at, transposed):
        p = [[parts[2 * half + quad][at] for quad in range(2)] for half in range(2)]
        if transposed:
            p = [[p[j][i] for j in range(2)] for i in range(2)]
        return jnp.concatenate([jnp.concatenate(r, axis=1) for r in p], axis=0)

    out_t, dq_t = whole(0, True), whole(1, True)
    dk, dv = whole(2, False), whole(3, False)
    grads = (nt(feat_t, dq_t), nn(feat_t, dk), nn(feat_t, dv), nn(out_t, cot))
    return (out_t, dq_t, dk, dv), grads


def results(out_t, dq_t, dk, dv, w_qkv):
    dfeat_t = nn(w_qkv[:, :C], dq_t) + nt(w_qkv[:, C : 2 * C], dk) + nt(w_qkv[:, 2 * C :], dv)
    return out_t, dfeat_t.astype(BF)


def z_body(feat, cot, w_qkv, w_qkv_t, w_out, back, grad, send_y):
    wide = (2 * T, T)
    row = y_row(iota(1, wide))
    send_y[...] = (
        nn(onehot(iota(0, wide) == row), feat[...]) + nn(onehot(iota(0, wide) == row + 4), cot[...])
    ).astype(BF)
    parts, terms = axis_math(z_line, feat[...], cot[...], w_qkv, w_qkv_t, w_out)
    eye = onehot(iota(0) == iota(1))
    for at, part_t in enumerate(results(*parts, w_qkv)):
        back[:, at * C : (at + 1) * C] = nt(eye, part_t).astype(BF)
    for at, term in enumerate(terms):
        grad[:, at * C : (at + 1) * C] = term.astype(BF)


def x_body(got, w_qkv, w_qkv_t, w_out, grad_so_far, back, grad):
    sort = onehot(x_sorted(iota(0)) == iota(1))
    feat = nn(sort, got[:, :C]).astype(BF)
    cot = nn(sort, got[:, C:]).astype(BF)
    parts, terms = axis_math(long_line, feat, cot, w_qkv, w_qkv_t, w_out)
    unsort = onehot(iota(0) == x_sorted(iota(1)))
    for at, part_t in enumerate(results(*parts, w_qkv)):
        back[:, at * C : (at + 1) * C] = nt(unsort, part_t).astype(BF)
    for at, term in enumerate(terms):
        cols = slice(at * C, (at + 1) * C)
        grad[:, cols] = (grad_so_far[:, cols].astype(F32) + term).astype(BF)


def core():
    return lax.rem(lax.axis_index("row"), 2)


def y_body(got, w_qkv, w_qkv_t, w_out, grad_so_far, out_t, dq_t, dk, dv, keep, give, total):
    wide = (T, 2 * T)
    row = y_sorted(iota(0, wide))
    feat = nn(onehot(row == iota(1, wide)), got[...]).astype(BF)
    cot = nn(onehot(row + 4 == iota(1, wide)), got[...]).astype(BF)
    parts, terms = axis_math(long_line, feat, cot, w_qkv, w_qkv_t, w_out)
    for ref, part in zip((out_t, dq_t, dk, dv), parts):
        ref[...] = part
    for at, term in enumerate(terms):
        cols = slice(at * C, (at + 1) * C)
        total[:, cols] = grad_so_far[:, cols].astype(F32) + term
    mine = core()
    keep[...] = total[pl.ds(pl.multiple_of(mine * 128, 128), 128)]
    give[...] = total[pl.ds(pl.multiple_of((1 - mine) * 128, 128), 128)].astype(BF)


def y_back_body(out_t, dq_t, dk, dv, w_qkv, back):
    out_t, dfeat_t = results(out_t[...], dq_t[...], dk[...], dv[...], w_qkv)
    wide = (2 * T, T)
    row = y_sorted(iota(1, wide))
    back[...] = (
        nt(onehot(iota(0, wide) == row), out_t) + nt(onehot(iota(0, wide) == row + 4), dfeat_t)
    ).astype(BF)


def col_pack_body(back_y, keep, took, send_col):
    send_col[:, :C] = back_y[...]
    half = (keep[...] + took[...].astype(F32)).astype(BF)
    for at in range(4):
        send_col[at * 128 : (at + 1) * 128, C:] = half[:, at * C : (at + 1) * C]


def row_pack_body(got_col, back_x, send_row):
    send_row[:, : 2 * C] = back_x[...]
    block = jnp.sum(got_col[:, C:].astype(F32).reshape(64, 8, C), axis=0)
    block = jnp.concatenate([block[:, :128], block[:, 128:]], axis=0)
    send_row[:, 2 * C :] = jnp.concatenate([block] * 16, axis=0).astype(BF)


def last_pack_body(factor, got_row, send):
    mine = core()
    block = jnp.zeros((16, 128), F32)
    for peer in range(4):
        at = pl.multiple_of((2 * peer + mine) * 32, 32)
        block += got_row[pl.ds(at, 16), 2 * C :].astype(F32)
    block = jnp.concatenate([block[:8], block[8:]], axis=1) * factor
    send[...] = jnp.concatenate([block] * 64, axis=0).astype(BF)


def final_body(back_z, got_col, got_row, w_out, update, grad_in):
    wide = (T, 2 * T)
    row = y_row(iota(0, wide))
    back_y = got_col[:, :C]
    put_x = onehot(iota(0) == x_source(iota(1)))
    mix = (
        back_z[:, :C].astype(F32)
        + nn(onehot(row == iota(1, wide)), back_y)
        + nn(put_x, got_row[:, :C])
    ).astype(BF)
    update[...] = nn(mix, w_out[...]).astype(BF)
    grad_in[...] = (
        back_z[:, C:].astype(F32)
        + nn(onehot(row + 4 == iota(1, wide)), back_y)
        + nn(put_x, got_row[:, C : 2 * C])
    ).astype(BF)


def unpack_body(mine, other, grad_qkv, grad_out):
    for src, half in ((mine, core()), (other, 1 - core())):
        rows = pl.ds(pl.multiple_of(half * 128, 128), 128)
        for at in range(3):
            grad_qkv[rows, at * C : (at + 1) * C] = src[at * 128 : (at + 1) * 128].astype(F32)
        grad_out[rows, :] = src[3 * 128 :].astype(F32)


def call(body, outs, flops, *args, space=pltpu.VMEM, scratch=(), grant=40 * 2**20):
    return pl.pallas_call(
        body,
        out_shape=outs,
        in_specs=[pl.BlockSpec(memory_space=space)] * len(args),
        scratch_shapes=scratch,
        out_specs=[pl.BlockSpec(memory_space=space)] * len(outs),
        compiler_params=pltpu.CompilerParams(vmem_limit_bytes=grant),
        cost_estimate=pl.CostEstimate(flops=flops, bytes_accessed=2**20, transcendentals=2**19),
    )(*args)


def shape(rows, cols, dtype):
    return jax.ShapeDtypeStruct((rows, cols), dtype)


def exchange(rows, axis):
    return lax.all_to_all(rows, axis, split_axis=0, concat_axis=0, tiled=True)


def swap(rows):
    return lax.ppermute(rows, "row", [(i, i ^ 1) for i in range(8)])


def body(features, w_qkv, w_out, cotangent):
    local_shape = features.shape
    feat = features.reshape(T, C)
    cot = cotangent.reshape(T, C)
    weights = (w_qkv, w_qkv.T, w_out)
    cube = 2 * T * T * C
    back_shape = shape(T, 2 * C, BF)
    grad_shape = shape(C, 4 * C, BF)
    (send_x,) = call(
        pack_body,
        [back_shape],
        cube * 2,
        feat,
        cot,
        space=pltpu.HBM,
        scratch=[
            pltpu.VMEM((T, C), BF),
            pltpu.VMEM((T, C), BF),
            pltpu.VMEM((T, 2 * C), BF),
            pltpu.SemaphoreType.DMA((4,)),
        ],
        grant=None,
    )
    got_x = exchange(send_x, "row")
    back_z, grad, send_y = call(
        z_body, [back_shape, grad_shape, shape(2 * T, C, BF)], cube * 70, feat, cot, *weights
    )
    got_y = exchange(send_y, ("dp", "col"))
    back_x, grad = call(x_body, [back_shape, grad_shape], cube * 70, got_x, *weights, grad)
    *parts, keep, give = call(
        y_body,
        [shape(T, C, BF)] * 4 + [shape(128, 4 * C, F32), shape(128, 4 * C, BF)],
        cube * 70,
        got_y,
        *weights,
        grad,
        scratch=[pltpu.VMEM((C, 4 * C), F32)],
    )
    took = swap(give)
    (back_y,) = call(y_back_body, [shape(2 * T, C, BF)], cube * 8, *parts, w_qkv)
    (send_col,) = call(col_pack_body, [shape(2 * T, 2 * C, BF)], 2**20, back_y, keep, took)
    got_col = exchange(send_col, ("dp", "col"))
    (send_row,) = call(row_pack_body, [shape(T, 2 * C + 128, BF)], 2**20, got_col, back_x)
    got_row = exchange(send_row, "row")
    factor = 1.0 / math.sqrt(PATCHES * 64 * 64 * 16)
    (send_last,) = call(
        functools.partial(last_pack_body, factor), [shape(512, C, BF)], 2**20, got_row
    )
    mine = exchange(send_last, ("dp", "col"))
    update, grad_in = call(
        final_body, [shape(T, C, BF)] * 2, cube * 6, back_z, got_col, got_row, w_out
    )
    grad_qkv, grad_out = call(
        unpack_body, [shape(C, 3 * C, F32), shape(C, C, F32)], 2**20, mine, swap(mine)
    )
    return (update.reshape(local_shape), grad_in.reshape(local_shape), grad_qkv, grad_out)


def solution(mesh):
    placed = (P("dp", "col", "row", None, None), P(), P(), P("dp", "col", "row", None, None))
    return jax.shard_map(
        body,
        mesh=mesh,
        in_specs=placed,
        out_specs=(P("dp", "col", "row", None, None), P("dp", "col", "row", None, None), P(), P()),
        check_vma=False,
    )
```

```python
import functools
import math

import jax
import jax.numpy as jnp
from jax import lax
from jax.experimental import pallas as pl
from jax.experimental.pallas import tpu as pltpu
from jax.sharding import PartitionSpec as P

HEADS = 8
DEPTH = 32
C = 256
T = 256
PATCHES = 2
Z = 16
HALF = 128
QUAD = 4
LINES = 4
NEG = -1e30

BF = jnp.bfloat16
F32 = jnp.float32


def nn(a, b):
    return lax.dot_general(a, b, (((1,), (0,)), ((), ())), preferred_element_type=F32)


def nt(a, b):
    return lax.dot_general(a, b, (((1,), (1,)), ((), ())), preferred_element_type=F32)


def iota(axis, shape=(T, T)):
    return lax.broadcasted_iota(jnp.int32, shape, axis)


def x_source(r):
    peer = r // 32
    return (peer // 4) * 128 + (r % 8) * Z + (peer % 4) * LINES + (r // 8) % LINES


def x_sorted(t):
    return (t % 64) // 8 * 32 + t // 64 * 8 + t % 8


def y_row(t):
    at = t % 128
    return at // 2 * 8 + t // 128 * 2 + at % 2


def y_sorted(t):
    at = t % 64
    return t // 128 * 256 + at // 2 * 8 + at % 2 * 2 + t // 64 % 2


def z_line(r):
    return r // Z


def long_line(r):
    return r // 64


def onehot(hit):
    return jnp.where(hit, 1.0, 0.0).astype(BF)


def pack_body(feat_hbm, cot_hbm, send_x, feat, cot, sorted_rows, sem):
    copies = [
        pltpu.make_async_copy(feat_hbm, feat, sem.at[0]),
        pltpu.make_async_copy(cot_hbm, cot, sem.at[1]),
    ]
    for copy in copies:
        copy.start()
    pick = onehot(x_source(iota(0)) == iota(1))
    outs = []
    for at, (copy, rows) in enumerate(zip(copies, (feat, cot))):
        copy.wait()
        cols = slice(at * C, (at + 1) * C)
        sorted_rows[:, cols] = nn(pick, rows[...]).astype(BF)
        outs.append(
            pltpu.make_async_copy(sorted_rows.at[:, cols], send_x.at[:, cols], sem.at[2 + at])
        )
        outs[at].start()
    for out in outs:
        out.wait()


def axis_math(line, feat, cot, w_qkv, w_qkv_t, w_out):
    scale = 1.0 / math.sqrt(DEPTH)
    feat_t = nt(onehot(iota(0) == iota(1)), feat).astype(BF)
    proj = nn(feat, w_qkv[...]).astype(BF)
    proj_t = nt(w_qkv_t[...], feat).astype(BF)
    gmix = nt(cot, w_out[...]).astype(BF)
    gmix_t = nt(w_out[...], cot).astype(BF)
    q, k, v = proj[:, :C], proj[:, C : 2 * C], proj[:, 2 * C :]
    q_t, k_t, v_t = proj_t[:C], proj_t[C : 2 * C], proj_t[2 * C :]
    wide = (HALF, QUAD * HALF)
    bias = jnp.where(line(iota(0, wide)) == line(iota(1, wide) % HALF), 0.0, NEG)
    head_of_lane = iota(1, (HALF, HALF)) // DEPTH
    blank = jnp.zeros((HALF, HALF), BF)
    strip = jnp.zeros((DEPTH, HALF), BF)

    def spread(a_t):
        return jnp.concatenate(
            [
                jnp.concatenate(
                    [a_t[i * DEPTH : (i + 1) * DEPTH] if i == j else strip for i in range(QUAD)],
                    axis=0,
                )
                for j in range(QUAD)
            ],
            axis=1,
        )

    def stack(a):
        return jnp.concatenate(
            [jnp.where(head_of_lane == j, a, blank) for j in range(QUAD)], axis=0
        )

    def per_head(a_t, m):
        return jnp.concatenate(
            [
                nn(a_t[j * DEPTH : (j + 1) * DEPTH], m[:, j * HALF : (j + 1) * HALF])
                for j in range(QUAD)
            ],
            axis=0,
        )

    blocks = [
        (slice(half * HALF, (half + 1) * HALF), slice(quad * HALF, (quad + 1) * HALF))
        for half in range(2)
        for quad in range(2)
    ]
    all_scores = [nn(k[t, c], spread(q_t[c, t])) + bias for t, c in blocks]
    all_dprobs = [nn(v[t, c], spread(gmix_t[c, t])) for t, c in blocks]
    soft = []
    for scores, dprobs in zip(all_scores, all_dprobs):
        top = jnp.max(scores, axis=0, keepdims=True)
        e = jnp.exp((scores - top) * scale)
        probs = e * (1.0 / jnp.sum(e, axis=0, keepdims=True))
        mean = jnp.sum(dprobs * probs, axis=0, keepdims=True)
        soft.append((probs.astype(BF), (probs * (dprobs - mean) * scale).astype(BF)))
    parts = []
    for (t, c), (rounded, dround) in zip(blocks, soft):
        out_t = per_head(v_t[c, t], rounded)
        dv = nn(rounded, stack(gmix[t, c]))
        dq_t = per_head(k_t[c, t], dround)
        dk = nn(dround, stack(q[t, c]))
        parts.append([m.astype(BF) for m in (out_t, dq_t, dk, dv)])

    def whole(at, transposed):
        p = [[parts[2 * half + quad][at] for quad in range(2)] for half in range(2)]
        if transposed:
            p = [[p[j][i] for j in range(2)] for i in range(2)]
        return jnp.concatenate([jnp.concatenate(r, axis=1) for r in p], axis=0)

    out_t, dq_t = whole(0, True), whole(1, True)
    dk, dv = whole(2, False), whole(3, False)
    grads = (nt(feat_t, dq_t), nn(feat_t, dk), nn(feat_t, dv), nn(out_t, cot))
    return (out_t, dq_t, dk, dv), grads


def results(out_t, dq_t, dk, dv, w_qkv):
    dfeat_t = nn(w_qkv[:, :C], dq_t) + nt(w_qkv[:, C : 2 * C], dk) + nt(w_qkv[:, 2 * C :], dv)
    return out_t, dfeat_t.astype(BF)


def z_body(feat, cot, w_qkv, w_qkv_t, w_out, back, grad, send_y):
    wide = (2 * T, T)
    row = y_row(iota(1, wide))
    send_y[...] = (
        nn(onehot(iota(0, wide) == row), feat[...]) + nn(onehot(iota(0, wide) == row + 4), cot[...])
    ).astype(BF)
    parts, terms = axis_math(z_line, feat[...], cot[...], w_qkv, w_qkv_t, w_out)
    eye = onehot(iota(0) == iota(1))
    for at, part_t in enumerate(results(*parts, w_qkv)):
        back[:, at * C : (at + 1) * C] = nt(eye, part_t).astype(BF)
    for at, term in enumerate(terms):
        grad[:, at * C : (at + 1) * C] = term.astype(BF)


def x_body(got, w_qkv, w_qkv_t, w_out, grad_so_far, back, grad):
    sort = onehot(x_sorted(iota(0)) == iota(1))
    feat = nn(sort, got[:, :C]).astype(BF)
    cot = nn(sort, got[:, C:]).astype(BF)
    parts, terms = axis_math(long_line, feat, cot, w_qkv, w_qkv_t, w_out)
    unsort = onehot(iota(0) == x_sorted(iota(1)))
    for at, part_t in enumerate(results(*parts, w_qkv)):
        back[:, at * C : (at + 1) * C] = nt(unsort, part_t).astype(BF)
    for at, term in enumerate(terms):
        cols = slice(at * C, (at + 1) * C)
        grad[:, cols] = (grad_so_far[:, cols].astype(F32) + term).astype(BF)


def core():
    return lax.rem(lax.axis_index("row"), 2)


def y_body(got, w_qkv, w_qkv_t, w_out, grad_so_far, out_t, dq_t, dk, dv, keep, give, total):
    wide = (T, 2 * T)
    row = y_sorted(iota(0, wide))
    feat = nn(onehot(row == iota(1, wide)), got[...]).astype(BF)
    cot = nn(onehot(row + 4 == iota(1, wide)), got[...]).astype(BF)
    parts, terms = axis_math(long_line, feat, cot, w_qkv, w_qkv_t, w_out)
    for ref, part in zip((out_t, dq_t, dk, dv), parts):
        ref[...] = part
    for at, term in enumerate(terms):
        cols = slice(at * C, (at + 1) * C)
        total[:, cols] = grad_so_far[:, cols].astype(F32) + term
    mine = core()
    keep[...] = total[pl.ds(pl.multiple_of(mine * 128, 128), 128)]
    give[...] = total[pl.ds(pl.multiple_of((1 - mine) * 128, 128), 128)].astype(BF)


def y_back_body(out_t, dq_t, dk, dv, w_qkv, back):
    wide = (2 * T, T)
    row = y_sorted(iota(1, wide))
    low, high = onehot(iota(0, wide) == row), onehot(iota(0, wide) == row + 4)
    for at, part_t in enumerate(results(out_t[...], dq_t[...], dk[...], dv[...], w_qkv)):
        back[:, at * 128 : (at + 1) * 128] = (
            nt(low, part_t[:128]) + nt(high, part_t[128:])
        ).astype(BF)


def col_pack_body(back_y, keep, took, send_col):
    send_col[:, :128] = back_y[:, :128]
    half = (keep[...] + took[...].astype(F32)).astype(BF)
    for at in range(4):
        send_col[at * 128 : (at + 1) * 128, 128:] = half[:, at * C : (at + 1) * C]


def row_pack_body(got_col, back_x, send_row):
    send_row[:, : 2 * C] = back_x[...]
    block = jnp.sum(got_col[:, 128:].astype(F32).reshape(64, 8, C), axis=0)
    block = jnp.concatenate([block[:, :128], block[:, 128:]], axis=0)
    send_row[:, 2 * C :] = jnp.concatenate([block] * 16, axis=0).astype(BF)


def last_pack_body(factor, got_row, back_y, send):
    mine = core()
    block = jnp.zeros((16, 128), F32)
    for peer in range(4):
        at = pl.multiple_of((2 * peer + mine) * 32, 32)
        block += got_row[pl.ds(at, 16), 2 * C :].astype(F32)
    block = jnp.concatenate([block[:8], block[8:]], axis=1) * factor
    send[:, :128] = back_y[:, 128:]
    send[:, 128:] = jnp.concatenate([block] * 64, axis=0).astype(BF)


def final_body(back_z, got_col, got_row, got_last, w_out, update, grad_in):
    wide = (T, 2 * T)
    row = y_row(iota(0, wide))
    low, high = onehot(row == iota(1, wide)), onehot(row + 4 == iota(1, wide))
    put_x = onehot(iota(0) == x_source(iota(1)))
    sums = []
    for at, rows in enumerate((got_col[:, :128], got_last[:, :128])):
        cols = slice(at * C, (at + 1) * C)
        from_y = jnp.concatenate([nn(low, rows), nn(high, rows)], axis=1)
        sums.append((back_z[:, cols].astype(F32) + from_y + nn(put_x, got_row[:, cols])).astype(BF))
    update[...] = nn(sums[0], w_out[...]).astype(BF)
    grad_in[...] = sums[1]


def unpack_body(mine, other, grad_qkv, grad_out):
    for src, half in ((mine, core()), (other, 1 - core())):
        rows = pl.ds(pl.multiple_of(half * 128, 128), 128)
        for at in range(3):
            grad_qkv[rows, at * C : (at + 1) * C] = src[at * 128 : (at + 1) * 128, 128:].astype(F32)
        grad_out[rows, :] = src[3 * 128 :, 128:].astype(F32)


def call(body, outs, flops, *args, space=pltpu.VMEM, scratch=(), grant=40 * 2**20):
    return pl.pallas_call(
        body,
        out_shape=outs,
        in_specs=[pl.BlockSpec(memory_space=space)] * len(args),
        scratch_shapes=scratch,
        out_specs=[pl.BlockSpec(memory_space=space)] * len(outs),
        compiler_params=pltpu.CompilerParams(vmem_limit_bytes=grant),
        cost_estimate=pl.CostEstimate(flops=flops, bytes_accessed=2**20, transcendentals=2**19),
    )(*args)


def shape(rows, cols, dtype):
    return jax.ShapeDtypeStruct((rows, cols), dtype)


def exchange(rows, axis):
    return lax.all_to_all(rows, axis, split_axis=0, concat_axis=0, tiled=True)


def swap(rows):
    return lax.ppermute(rows, "row", [(i, i ^ 1) for i in range(8)])


def body(features, w_qkv, w_out, cotangent):
    local_shape = features.shape
    feat = features.reshape(T, C)
    cot = cotangent.reshape(T, C)
    weights = (w_qkv, w_qkv.T, w_out)
    cube = 2 * T * T * C
    back_shape = shape(T, 2 * C, BF)
    grad_shape = shape(C, 4 * C, BF)
    (send_x,) = call(
        pack_body,
        [back_shape],
        cube * 2,
        feat,
        cot,
        space=pltpu.HBM,
        scratch=[
            pltpu.VMEM((T, C), BF),
            pltpu.VMEM((T, C), BF),
            pltpu.VMEM((T, 2 * C), BF),
            pltpu.SemaphoreType.DMA((4,)),
        ],
        grant=None,
    )
    got_x = exchange(send_x, "row")
    back_z, grad, send_y = call(
        z_body, [back_shape, grad_shape, shape(2 * T, C, BF)], cube * 70, feat, cot, *weights
    )
    got_y = exchange(send_y, ("dp", "col"))
    back_x, grad = call(x_body, [back_shape, grad_shape], cube * 70, got_x, *weights, grad)
    *parts, keep, give = call(
        y_body,
        [shape(T, C, BF)] * 4 + [shape(128, 4 * C, F32), shape(128, 4 * C, BF)],
        cube * 70,
        got_y,
        *weights,
        grad,
        scratch=[pltpu.VMEM((C, 4 * C), F32)],
    )
    took = swap(give)
    (back_y,) = call(y_back_body, [shape(2 * T, C, BF)], cube * 8, *parts, w_qkv)
    (send_col,) = call(col_pack_body, [shape(2 * T, 3 * 128, BF)], 2**20, back_y, keep, took)
    got_col = exchange(send_col, ("dp", "col"))
    (send_row,) = call(row_pack_body, [shape(T, 2 * C + 128, BF)], 2**20, got_col, back_x)
    got_row = exchange(send_row, "row")
    factor = 1.0 / math.sqrt(PATCHES * 64 * 64 * 16)
    (send_last,) = call(
        functools.partial(last_pack_body, factor),
        [shape(2 * T, 3 * 128, BF)],
        2**20,
        got_row,
        back_y,
    )
    mine = exchange(send_last, ("dp", "col"))
    update, grad_in = call(
        final_body, [shape(T, C, BF)] * 2, cube * 6, back_z, got_col, got_row, mine, w_out
    )
    grad_qkv, grad_out = call(
        unpack_body, [shape(C, 3 * C, F32), shape(C, C, F32)], 2**20, mine, swap(mine)
    )
    return (update.reshape(local_shape), grad_in.reshape(local_shape), grad_qkv, grad_out)


def solution(mesh):
    placed = (P("dp", "col", "row", None, None), P(), P(), P("dp", "col", "row", None, None))
    return jax.shard_map(
        body,
        mesh=mesh,
        in_specs=placed,
        out_specs=(P("dp", "col", "row", None, None), P("dp", "col", "row", None, None), P(), P()),
        check_vma=False,
    )
```

```python
import functools
import math

import jax
import jax.numpy as jnp
from jax import lax
from jax.experimental import pallas as pl
from jax.experimental.pallas import tpu as pltpu
from jax.sharding import PartitionSpec as P

HEADS = 8
DEPTH = 32
C = 256
T = 256
PATCHES = 2
Z = 16
HALF = 128
QUAD = 4
LINES = 4
NEG = -1e30

BF = jnp.bfloat16
F32 = jnp.float32


def nn(a, b):
    return lax.dot_general(a, b, (((1,), (0,)), ((), ())), preferred_element_type=F32)


def nt(a, b):
    return lax.dot_general(a, b, (((1,), (1,)), ((), ())), preferred_element_type=F32)


def down(n):
    return lax.broadcasted_iota(jnp.int32, (n, 1), 0)


def along(n):
    return lax.broadcasted_iota(jnp.int32, (1, n), 1)


def x_source(r):
    peer = r >> 5
    return ((peer >> 2) << 7) + ((r & 7) << 4) + ((peer & 3) << 2) + ((r >> 3) & 3)


def x_sorted(t):
    return (((t & 63) >> 3) << 5) + ((t >> 6) << 3) + (t & 7)


def y_row(t):
    at = t & 127
    return ((at >> 1) << 3) + ((t >> 7) << 1) + (at & 1)


def y_sorted(t):
    at = t & 63
    return ((t >> 7) << 8) + ((at >> 1) << 3) + ((at & 1) << 1) + ((t >> 6) & 1)


def z_line(r):
    return r >> 4


def long_line(r):
    return r >> 6


def onehot(a, b):
    return jnp.where(a == b, 1.0, 0.0).astype(BF)


def pack_body(feat_hbm, cot_hbm, send_x, feat, cot, sorted_rows, sem):
    copies = [
        pltpu.make_async_copy(feat_hbm, feat, sem.at[0]),
        pltpu.make_async_copy(cot_hbm, cot, sem.at[1]),
    ]
    for copy in copies:
        copy.start()
    pick = onehot(x_source(down(T)), along(T))
    outs = []
    for at, (copy, rows) in enumerate(zip(copies, (feat, cot))):
        copy.wait()
        cols = slice(at * C, (at + 1) * C)
        sorted_rows[:, cols] = nn(pick, rows[...]).astype(BF)
        outs.append(
            pltpu.make_async_copy(sorted_rows.at[:, cols], send_x.at[:, cols], sem.at[2 + at])
        )
        outs[at].start()
    for out in outs:
        out.wait()


def axis_math(line, feat, cot, w_qkv, w_qkv_t, w_out):
    scale = 1.0 / math.sqrt(DEPTH)
    feat_t = nt(onehot(down(T), along(T)), feat).astype(BF)
    proj = nn(feat, w_qkv[...]).astype(BF)
    proj_t = nt(w_qkv_t[...], feat).astype(BF)
    gmix = nt(cot, w_out[...]).astype(BF)
    gmix_t = nt(w_out[...], cot).astype(BF)
    q, k, v = proj[:, :C], proj[:, C : 2 * C], proj[:, 2 * C :]
    q_t, k_t, v_t = proj_t[:C], proj_t[C : 2 * C], proj_t[2 * C :]
    bias = jnp.where(line(down(HALF)) == line(along(QUAD * HALF) & (HALF - 1)), 0.0, NEG)
    head_of_lane = jnp.broadcast_to(along(HALF) >> 5, (HALF, HALF))
    blank = jnp.zeros((HALF, HALF), BF)
    strip = jnp.zeros((DEPTH, HALF), BF)

    def spread(a_t):
        return jnp.concatenate(
            [
                jnp.concatenate(
                    [a_t[i * DEPTH : (i + 1) * DEPTH] if i == j else strip for i in range(QUAD)],
                    axis=0,
                )
                for j in range(QUAD)
            ],
            axis=1,
        )

    def stack(a):
        return jnp.concatenate(
            [jnp.where(head_of_lane == j, a, blank) for j in range(QUAD)], axis=0
        )

    def per_head(a_t, m):
        return jnp.concatenate(
            [
                nn(a_t[j * DEPTH : (j + 1) * DEPTH], m[:, j * HALF : (j + 1) * HALF])
                for j in range(QUAD)
            ],
            axis=0,
        )

    blocks = [
        (slice(half * HALF, (half + 1) * HALF), slice(quad * HALF, (quad + 1) * HALF))
        for half in range(2)
        for quad in range(2)
    ]
    all_scores = [nn(k[t, c], spread(q_t[c, t])) + bias for t, c in blocks]
    all_dprobs = [nn(v[t, c], spread(gmix_t[c, t])) for t, c in blocks]
    soft = []
    for scores, dprobs in zip(all_scores, all_dprobs):
        top = jnp.max(scores, axis=0, keepdims=True)
        e = jnp.exp((scores - top) * scale)
        probs = e * (1.0 / jnp.sum(e, axis=0, keepdims=True))
        mean = jnp.sum(dprobs * probs, axis=0, keepdims=True)
        soft.append((probs.astype(BF), (probs * (dprobs - mean) * scale).astype(BF)))
    parts = []
    for (t, c), (rounded, dround) in zip(blocks, soft):
        out_t = per_head(v_t[c, t], rounded)
        dv = nn(rounded, stack(gmix[t, c]))
        dq_t = per_head(k_t[c, t], dround)
        dk = nn(dround, stack(q[t, c]))
        parts.append([m.astype(BF) for m in (out_t, dq_t, dk, dv)])

    def whole(at, transposed):
        p = [[parts[2 * half + quad][at] for quad in range(2)] for half in range(2)]
        if transposed:
            p = [[p[j][i] for j in range(2)] for i in range(2)]
        return jnp.concatenate([jnp.concatenate(r, axis=1) for r in p], axis=0)

    out_t, dq_t = whole(0, True), whole(1, True)
    dk, dv = whole(2, False), whole(3, False)
    grads = (nt(feat_t, dq_t), nn(feat_t, dk), nn(feat_t, dv), nn(out_t, cot))
    return (out_t, dq_t, dk, dv), grads


def results(out_t, dq_t, dk, dv, w_qkv):
    dfeat_t = nn(w_qkv[:, :C], dq_t) + nt(w_qkv[:, C : 2 * C], dk) + nt(w_qkv[:, 2 * C :], dv)
    return out_t, dfeat_t.astype(BF)


def z_body(feat, cot, w_qkv, w_qkv_t, w_out, back, grad, send_y):
    row, at_row = y_row(along(T)), down(2 * T)
    send_y[...] = (
        nn(onehot(at_row, row), feat[...]) + nn(onehot(at_row, row + 4), cot[...])
    ).astype(BF)
    parts, terms = axis_math(z_line, feat[...], cot[...], w_qkv, w_qkv_t, w_out)
    eye = onehot(down(T), along(T))
    for at, part_t in enumerate(results(*parts, w_qkv)):
        back[:, at * C : (at + 1) * C] = nt(eye, part_t).astype(BF)
    for at, term in enumerate(terms):
        grad[:, at * C : (at + 1) * C] = term.astype(BF)


def x_body(got, w_qkv, w_qkv_t, w_out, grad_so_far, back, grad):
    sort = onehot(x_sorted(down(T)), along(T))
    feat = nn(sort, got[:, :C]).astype(BF)
    cot = nn(sort, got[:, C:]).astype(BF)
    parts, terms = axis_math(long_line, feat, cot, w_qkv, w_qkv_t, w_out)
    unsort = onehot(down(T), x_sorted(along(T)))
    for at, part_t in enumerate(results(*parts, w_qkv)):
        back[:, at * C : (at + 1) * C] = nt(unsort, part_t).astype(BF)
    for at, term in enumerate(terms):
        cols = slice(at * C, (at + 1) * C)
        grad[:, cols] = (grad_so_far[:, cols].astype(F32) + term).astype(BF)


def core():
    return lax.rem(lax.axis_index("row"), 2)


def y_body(got, w_qkv, w_qkv_t, w_out, grad_so_far, out_t, dq_t, dk, dv, keep, give, total):
    row = y_sorted(down(T))
    feat = nn(onehot(row, along(2 * T)), got[...]).astype(BF)
    cot = nn(onehot(row + 4, along(2 * T)), got[...]).astype(BF)
    parts, terms = axis_math(long_line, feat, cot, w_qkv, w_qkv_t, w_out)
    for ref, part in zip((out_t, dq_t, dk, dv), parts):
        ref[...] = part
    for at, term in enumerate(terms):
        cols = slice(at * C, (at + 1) * C)
        total[:, cols] = grad_so_far[:, cols].astype(F32) + term
    mine = core()
    keep[...] = total[pl.ds(pl.multiple_of(mine * 128, 128), 128)]
    give[...] = total[pl.ds(pl.multiple_of((1 - mine) * 128, 128), 128)].astype(BF)


def y_back_body(out_t, dq_t, dk, dv, w_qkv, back):
    row, at_row = y_sorted(along(T)), down(2 * T)
    low, high = onehot(at_row, row), onehot(at_row, row + 4)
    for at, part_t in enumerate(results(out_t[...], dq_t[...], dk[...], dv[...], w_qkv)):
        back[:, at * 128 : (at + 1) * 128] = (
            nt(low, part_t[:128]) + nt(high, part_t[128:])
        ).astype(BF)


def col_pack_body(back_y, keep, took, send_col):
    send_col[:, :128] = back_y[:, :128]
    half = (keep[...] + took[...].astype(F32)).astype(BF)
    for at in range(4):
        send_col[at * 128 : (at + 1) * 128, 128:] = half[:, at * C : (at + 1) * C]


def row_pack_body(got_col, back_x, send_row):
    send_row[:, : 2 * C] = back_x[...]
    block = jnp.sum(got_col[:, 128:].astype(F32).reshape(64, 8, C), axis=0)
    block = jnp.concatenate([block[:, :128], block[:, 128:]], axis=0)
    send_row[:, 2 * C :] = jnp.concatenate([block] * 16, axis=0).astype(BF)


def last_pack_body(factor, got_row, back_y, send):
    mine = core()
    block = jnp.zeros((16, 128), F32)
    for peer in range(4):
        at = pl.multiple_of((2 * peer + mine) * 32, 32)
        block += got_row[pl.ds(at, 16), 2 * C :].astype(F32)
    block = jnp.concatenate([block[:8], block[8:]], axis=1) * factor
    send[:, :128] = back_y[:, 128:]
    send[:, 128:] = jnp.concatenate([block] * 64, axis=0).astype(BF)


def final_body(back_z, got_col, got_row, got_last, w_out, update, grad_in):
    row = y_row(down(T))
    low, high = onehot(row, along(2 * T)), onehot(row + 4, along(2 * T))
    put_x = onehot(down(T), x_source(along(T)))
    sums = []
    for at, rows in enumerate((got_col[:, :128], got_last[:, :128])):
        cols = slice(at * C, (at + 1) * C)
        from_y = jnp.concatenate([nn(low, rows), nn(high, rows)], axis=1)
        sums.append((back_z[:, cols].astype(F32) + from_y + nn(put_x, got_row[:, cols])).astype(BF))
    update[...] = nn(sums[0], w_out[...]).astype(BF)
    grad_in[...] = sums[1]


def unpack_body(mine, other, grad_qkv, grad_out):
    for src, half in ((mine, core()), (other, 1 - core())):
        rows = pl.ds(pl.multiple_of(half * 128, 128), 128)
        for at in range(3):
            grad_qkv[rows, at * C : (at + 1) * C] = src[at * 128 : (at + 1) * 128, 128:].astype(F32)
        grad_out[rows, :] = src[3 * 128 :, 128:].astype(F32)


def call(body, outs, flops, *args, space=pltpu.VMEM, scratch=(), grant=40 * 2**20):
    return pl.pallas_call(
        body,
        out_shape=outs,
        in_specs=[pl.BlockSpec(memory_space=space)] * len(args),
        scratch_shapes=scratch,
        out_specs=[pl.BlockSpec(memory_space=space)] * len(outs),
        compiler_params=pltpu.CompilerParams(vmem_limit_bytes=grant),
        cost_estimate=pl.CostEstimate(flops=flops, bytes_accessed=2**20, transcendentals=2**19),
    )(*args)


def shape(rows, cols, dtype):
    return jax.ShapeDtypeStruct((rows, cols), dtype)


def exchange(rows, axis):
    return lax.all_to_all(rows, axis, split_axis=0, concat_axis=0, tiled=True)


def swap(rows):
    return lax.ppermute(rows, "row", [(i, i ^ 1) for i in range(8)])


def body(features, w_qkv, w_out, cotangent):
    local_shape = features.shape
    feat = features.reshape(T, C)
    cot = cotangent.reshape(T, C)
    weights = (w_qkv, w_qkv.T, w_out)
    cube = 2 * T * T * C
    back_shape = shape(T, 2 * C, BF)
    grad_shape = shape(C, 4 * C, BF)
    (send_x,) = call(
        pack_body,
        [back_shape],
        cube * 2,
        feat,
        cot,
        space=pltpu.HBM,
        scratch=[
            pltpu.VMEM((T, C), BF),
            pltpu.VMEM((T, C), BF),
            pltpu.VMEM((T, 2 * C), BF),
            pltpu.SemaphoreType.DMA((4,)),
        ],
        grant=None,
    )
    got_x = exchange(send_x, "row")
    back_z, grad, send_y = call(
        z_body, [back_shape, grad_shape, shape(2 * T, C, BF)], cube * 70, feat, cot, *weights
    )
    got_y = exchange(send_y, ("dp", "col"))
    back_x, grad = call(x_body, [back_shape, grad_shape], cube * 70, got_x, *weights, grad)
    *parts, keep, give = call(
        y_body,
        [shape(T, C, BF)] * 4 + [shape(128, 4 * C, F32), shape(128, 4 * C, BF)],
        cube * 70,
        got_y,
        *weights,
        grad,
        scratch=[pltpu.VMEM((C, 4 * C), F32)],
    )
    took = swap(give)
    (back_y,) = call(y_back_body, [shape(2 * T, C, BF)], cube * 8, *parts, w_qkv)
    (send_col,) = call(col_pack_body, [shape(2 * T, 3 * 128, BF)], 2**20, back_y, keep, took)
    got_col = exchange(send_col, ("dp", "col"))
    (send_row,) = call(row_pack_body, [shape(T, 2 * C + 128, BF)], 2**20, got_col, back_x)
    got_row = exchange(send_row, "row")
    factor = 1.0 / math.sqrt(PATCHES * 64 * 64 * 16)
    (send_last,) = call(
        functools.partial(last_pack_body, factor),
        [shape(2 * T, 3 * 128, BF)],
        2**20,
        got_row,
        back_y,
    )
    mine = exchange(send_last, ("dp", "col"))
    update, grad_in = call(
        final_body, [shape(T, C, BF)] * 2, cube * 6, back_z, got_col, got_row, mine, w_out
    )
    grad_qkv, grad_out = call(
        unpack_body, [shape(C, 3 * C, F32), shape(C, C, F32)], 2**20, mine, swap(mine)
    )
    return (update.reshape(local_shape), grad_in.reshape(local_shape), grad_qkv, grad_out)


def solution(mesh):
    placed = (P("dp", "col", "row", None, None), P(), P(), P("dp", "col", "row", None, None))
    return jax.shard_map(
        body,
        mesh=mesh,
        in_specs=placed,
        out_specs=(P("dp", "col", "row", None, None), P("dp", "col", "row", None, None), P(), P()),
        check_vma=False,
    )
```

```python
import functools
import math

import jax
import jax.numpy as jnp
from jax import lax
from jax.experimental import pallas as pl
from jax.experimental.pallas import tpu as pltpu
from jax.sharding import PartitionSpec as P

HEADS = 8
DEPTH = 32
C = 256
T = 256
PATCHES = 2
Z = 16
HALF = 128
QUAD = 4
NEG = -1e30

BF = jnp.bfloat16
F32 = jnp.float32


def nn(a, b):
    return lax.dot_general(a, b, (((1,), (0,)), ((), ())), preferred_element_type=F32)


def nt(a, b):
    return lax.dot_general(a, b, (((1,), (1,)), ((), ())), preferred_element_type=F32)


def down(n):
    return lax.broadcasted_iota(jnp.int32, (n, 1), 0)


def along(n):
    return lax.broadcasted_iota(jnp.int32, (1, n), 1)


def core():
    return lax.rem(lax.axis_index("row"), 2)


def by_core(first, second):
    mine = core()
    return first * (1 - mine) + second * mine


def y_source(r):
    return (((r >> 2) & 1) << 7) + ((r >> 3) << 2) + (r & 3)


def x_source(r):
    return ((r >> 7) << 7) + ((r & 7) << 4) + ((r >> 3) & 15)


def place(t, part):
    line, at = t >> 6, t & 63
    y_place = (part << 8) + ((at >> 1) << 3) + ((at & 1) << 2) + line
    x_peer = ((at >> 4) << 3) + (part << 2) + line
    x_place = (((at >> 3) & 1) << 8) + (x_peer << 3) + (at & 7)
    return by_core(y_place, x_place)


def z_line(r):
    return r >> 4


def long_line(r):
    return r >> 6


def onehot(a, b):
    return jnp.where(a == b, 1.0, 0.0).astype(BF)


def pack_body(feat_hbm, cot_hbm, keep, give, feat, cot, mine, theirs, sem):
    copies = [
        pltpu.make_async_copy(feat_hbm, feat, sem.at[0]),
        pltpu.make_async_copy(cot_hbm, cot, sem.at[1]),
    ]
    for copy in copies:
        copy.start()
    r = down(T)
    pick_mine = onehot(by_core(y_source(r), x_source(r)), along(T))
    pick_theirs = onehot(by_core(x_source(r), y_source(r)), along(T))
    for copy in copies:
        copy.wait()
    for pick, rows in ((pick_theirs, theirs), (pick_mine, mine)):
        rows[:, :C] = nn(pick, feat[...]).astype(BF)
        rows[:, C:] = nn(pick, cot[...]).astype(BF)
    outs = [
        pltpu.make_async_copy(theirs, give, sem.at[2]),
        pltpu.make_async_copy(mine, keep, sem.at[3]),
    ]
    for out in outs:
        out.start()
    for out in outs:
        out.wait()


def merge_body(mine, took, send):
    send[:, : 2 * C] = mine[...]
    send[:, 2 * C :] = took[...]


def axis_math(line, feat, cot, w_qkv, w_qkv_t, w_out):
    scale = 1.0 / math.sqrt(DEPTH)
    feat_t = nt(onehot(down(T), along(T)), feat).astype(BF)
    proj = nn(feat, w_qkv[...]).astype(BF)
    proj_t = nt(w_qkv_t[...], feat).astype(BF)
    gmix = nt(cot, w_out[...]).astype(BF)
    gmix_t = nt(w_out[...], cot).astype(BF)
    q, k, v = proj[:, :C], proj[:, C : 2 * C], proj[:, 2 * C :]
    q_t, k_t, v_t = proj_t[:C], proj_t[C : 2 * C], proj_t[2 * C :]
    bias = jnp.where(line(down(HALF)) == line(along(QUAD * HALF) & (HALF - 1)), 0.0, NEG)
    head_of_lane = jnp.broadcast_to(along(HALF) >> 5, (HALF, HALF))
    blank = jnp.zeros((HALF, HALF), BF)
    strip = jnp.zeros((DEPTH, HALF), BF)

    def spread(a_t):
        return jnp.concatenate(
            [
                jnp.concatenate(
                    [a_t[i * DEPTH : (i + 1) * DEPTH] if i == j else strip for i in range(QUAD)],
                    axis=0,
                )
                for j in range(QUAD)
            ],
            axis=1,
        )

    def stack(a):
        return jnp.concatenate(
            [jnp.where(head_of_lane == j, a, blank) for j in range(QUAD)], axis=0
        )

    def per_head(a_t, m):
        return jnp.concatenate(
            [
                nn(a_t[j * DEPTH : (j + 1) * DEPTH], m[:, j * HALF : (j + 1) * HALF])
                for j in range(QUAD)
            ],
            axis=0,
        )

    blocks = [
        (slice(half * HALF, (half + 1) * HALF), slice(quad * HALF, (quad + 1) * HALF))
        for half in range(2)
        for quad in range(2)
    ]
    all_scores = [nn(k[t, c], spread(q_t[c, t])) + bias for t, c in blocks]
    all_dprobs = [nn(v[t, c], spread(gmix_t[c, t])) for t, c in blocks]
    soft = []
    for scores, dprobs in zip(all_scores, all_dprobs):
        top = jnp.max(scores, axis=0, keepdims=True)
        e = jnp.exp((scores - top) * scale)
        probs = e * (1.0 / jnp.sum(e, axis=0, keepdims=True))
        mean = jnp.sum(dprobs * probs, axis=0, keepdims=True)
        soft.append((probs.astype(BF), (probs * (dprobs - mean) * scale).astype(BF)))
    parts = []
    for (t, c), (rounded, dround) in zip(blocks, soft):
        out_t = per_head(v_t[c, t], rounded)
        dv = nn(rounded, stack(gmix[t, c]))
        dq_t = per_head(k_t[c, t], dround)
        dk = nn(dround, stack(q[t, c]))
        parts.append([m.astype(BF) for m in (out_t, dq_t, dk, dv)])

    def whole(at, transposed):
        p = [[parts[2 * half + quad][at] for quad in range(2)] for half in range(2)]
        if transposed:
            p = [[p[j][i] for j in range(2)] for i in range(2)]
        return jnp.concatenate([jnp.concatenate(r, axis=1) for r in p], axis=0)

    out_t, dq_t = whole(0, True), whole(1, True)
    dk, dv = whole(2, False), whole(3, False)
    grads = (nt(feat_t, dq_t), nn(feat_t, dk), nn(feat_t, dv), nn(out_t, cot))
    return (out_t, dq_t, dk, dv), grads


def results(out_t, dq_t, dk, dv, w_qkv):
    dfeat_t = nn(w_qkv[:, :C], dq_t) + nt(w_qkv[:, C : 2 * C], dk) + nt(w_qkv[:, 2 * C :], dv)
    return out_t, dfeat_t.astype(BF)


def z_body(feat, cot, w_qkv, w_qkv_t, w_out, back, grad):
    parts, terms = axis_math(z_line, feat[...], cot[...], w_qkv, w_qkv_t, w_out)
    eye = onehot(down(T), along(T))
    for at, part_t in enumerate(results(*parts, w_qkv)):
        back[:, at * C : (at + 1) * C] = nt(eye, part_t).astype(BF)
    for at, term in enumerate(terms):
        grad[:, at * C : (at + 1) * C] = term.astype(BF)


def lines_body(got, w_qkv, w_qkv_t, w_out, grad_z, *refs):
    keep, give, total = refs[8:]
    for part in range(2):
        t = place(down(T), part)
        first, second = onehot(t, along(T)), onehot(t, along(T) + T)
        feat = (nn(first, got[:, :C]) + nn(second, got[:, 2 * C : 3 * C])).astype(BF)
        cot = (nn(first, got[:, C : 2 * C]) + nn(second, got[:, 3 * C :])).astype(BF)
        held, terms = axis_math(long_line, feat, cot, w_qkv, w_qkv_t, w_out)
        for ref, value in zip(refs[part * 4 : part * 4 + 4], held):
            ref[...] = value
        for at, term in enumerate(terms):
            cols = slice(at * C, (at + 1) * C)
            total[:, cols] = (total[:, cols] if part else grad_z[:, cols].astype(F32)) + term
    mine = core()
    keep[...] = total[pl.ds(pl.multiple_of(mine * 128, 128), 128)]
    give[...] = total[pl.ds(pl.multiple_of((1 - mine) * 128, 128), 128)].astype(BF)


def back_body(*refs):
    w_qkv, back_out, back_feat = refs[8:]
    sums = [jnp.zeros((T, C), F32)] * 4
    for part in range(2):
        t = place(along(T), part)
        first, second = onehot(down(T), t), onehot(down(T) + T, t)
        out_t, feat_t = results(*[ref[...] for ref in refs[part * 4 : part * 4 + 4]], w_qkv)
        new = (nt(first, out_t), nt(second, out_t), nt(first, feat_t), nt(second, feat_t))
        sums = [a + b for a, b in zip(sums, new)]
    back_out[:, :C], back_out[:, C:] = sums[0].astype(BF), sums[1].astype(BF)
    back_feat[:, :C], back_feat[:, C:] = sums[2].astype(BF), sums[3].astype(BF)


def first_pack_body(back_out, keep, took, send):
    send[:, : 2 * C] = back_out[...]
    half = (keep[...] + took[...].astype(F32)).astype(BF)
    send[:128, 2 * C :] = half[:, : 2 * C]
    send[128:, 2 * C :] = half[:, 2 * C :]


def block_body(got, send):
    block = jnp.sum(got[:, 2 * C :].astype(F32).reshape(32, 8, 2 * C), axis=0)
    send[...] = jnp.concatenate([block] * 8, axis=0).astype(BF)


def last_pack_body(factor, got, back_feat, send):
    block = jnp.sum(got[...].astype(F32).reshape(8, 8, 2 * C), axis=0) * factor
    send[:, : 2 * C] = back_feat[...]
    send[:, 2 * C :] = jnp.concatenate([block] * 32, axis=0).astype(BF)


def give_body(got_first, got_last, give):
    give[:, :C] = got_first[:, C : 2 * C]
    give[:, C : 2 * C] = got_last[:, C : 2 * C]
    give[:, 2 * C :] = got_last[:, 2 * C :]


def final_body(back_z, got_first, got_last, took, w_out, update, grad_in, grad_qkv, grad_out):
    r = along(T)
    put_mine = onehot(down(T), by_core(y_source(r), x_source(r)))
    put_theirs = onehot(down(T), by_core(x_source(r), y_source(r)))
    sums = []
    for at, rows in enumerate((got_first[:, :C], got_last[:, :C])):
        cols = slice(at * C, (at + 1) * C)
        sums.append(
            (
                back_z[:, cols].astype(F32) + nn(put_mine, rows) + nn(put_theirs, took[:, cols])
            ).astype(BF)
        )
    update[...] = nn(sums[0], w_out[...]).astype(BF)
    grad_in[...] = sums[1]
    for src, half in ((got_last, core()), (took, 1 - core())):
        rows = pl.ds(pl.multiple_of(half * 128, 128), 128)
        grad_qkv[rows, : 2 * C] = src[:128, 2 * C :].astype(F32)
        grad_qkv[rows, 2 * C :] = src[128:, 2 * C : 3 * C].astype(F32)
        grad_out[rows, :] = src[128:, 3 * C :].astype(F32)


def call(body, outs, flops, *args, space=pltpu.VMEM, scratch=(), grant=40 * 2**20):
    return pl.pallas_call(
        body,
        out_shape=outs,
        in_specs=[pl.BlockSpec(memory_space=space)] * len(args),
        out_specs=[pl.BlockSpec(memory_space=space)] * len(outs),
        scratch_shapes=scratch,
        compiler_params=pltpu.CompilerParams(vmem_limit_bytes=grant),
        cost_estimate=pl.CostEstimate(flops=flops, bytes_accessed=2**20, transcendentals=2**19),
    )(*args)


def shape(rows, cols, dtype):
    return jax.ShapeDtypeStruct((rows, cols), dtype)


AXES = ("dp", "row", "col")


def device(x, mine, y, z):
    return z % 2 * 256 + (x * 2 + mine) * 32 + y * 4 + z // 2


X, Y, ZS = range(4), range(8), range(8)
LONG = [[device(x, 0, y, z) for y in Y for z in ZS[dp::2]] for x in X for dp in range(2)] + [
    [device(x, 1, y, z) for x in X for z in ZS] for y in Y
]
SHORT = [
    [device(x, 0, y, 2 * z + dp) for x in X for dp in range(2)] for y in Y for z in range(4)
] + [[device(x, 1, y, z) for y in Y] for x in X for z in ZS]


def exchange(rows, groups):
    return lax.all_to_all(
        rows, AXES, split_axis=0, concat_axis=0, axis_index_groups=groups, tiled=True
    )


def swap(rows):
    return lax.ppermute(rows, "row", [(i, i ^ 1) for i in range(8)])


def body(features, w_qkv, w_out, cotangent):
    local_shape = features.shape
    feat = features.reshape(T, C)
    cot = cotangent.reshape(T, C)
    weights = (w_qkv, w_qkv.T, w_out)
    cube = 2 * T * T * C
    pair = shape(T, 2 * C, BF)
    quad = shape(T, 4 * C, BF)
    mine, give = call(
        pack_body,
        [pair, pair],
        cube * 4,
        feat,
        cot,
        space=pltpu.HBM,
        scratch=[
            pltpu.VMEM((T, C), BF),
            pltpu.VMEM((T, C), BF),
            pltpu.VMEM((T, 2 * C), BF),
            pltpu.VMEM((T, 2 * C), BF),
            pltpu.SemaphoreType.DMA((4,)),
        ],
        grant=None,
    )
    (send,) = call(merge_body, [quad], 2**20, mine, swap(give))
    got = exchange(send, LONG)
    back_z, grad_z = call(z_body, [pair, shape(C, 4 * C, BF)], cube * 70, feat, cot, *weights)
    *held, keep, give = call(
        lines_body,
        [shape(T, C, BF)] * 8 + [shape(128, 4 * C, F32), shape(128, 4 * C, BF)],
        cube * 140,
        got,
        *weights,
        grad_z,
        scratch=[pltpu.VMEM((C, 4 * C), F32)],
    )
    took = swap(give)
    back_out, back_feat = call(back_body, [pair] * 2, cube * 20, *held, w_qkv)
    (send,) = call(first_pack_body, [quad], 2**20, back_out, keep, took)
    got_first = exchange(send, LONG)
    (send,) = call(block_body, [shape(64, 2 * C, BF)], 2**20, got_first)
    blocks = exchange(send, SHORT)
    factor = 1.0 / math.sqrt(PATCHES * 64 * 64 * 16)
    (send,) = call(functools.partial(last_pack_body, factor), [quad], 2**20, blocks, back_feat)
    got_last = exchange(send, LONG)
    (give,) = call(give_body, [quad], 2**20, got_first, got_last)
    update, grad_in, grad_qkv, grad_out = call(
        final_body,
        [shape(T, C, BF)] * 2 + [shape(C, 3 * C, F32), shape(C, C, F32)],
        cube * 6,
        back_z,
        got_first,
        got_last,
        swap(give),
        w_out,
    )
    return (update.reshape(local_shape), grad_in.reshape(local_shape), grad_qkv, grad_out)


def solution(mesh):
    placed = (P("dp", "col", "row", None, None), P(), P(), P("dp", "col", "row", None, None))
    return jax.shard_map(
        body,
        mesh=mesh,
        in_specs=placed,
        out_specs=(P("dp", "col", "row", None, None), P("dp", "col", "row", None, None), P(), P()),
        check_vma=False,
    )
```

```python
import functools
import math

import jax
import jax.numpy as jnp
from jax import lax
from jax.experimental import pallas as pl
from jax.experimental.pallas import tpu as pltpu
from jax.sharding import PartitionSpec as P

HEADS = 8
DEPTH = 32
C = 256
T = 256
PATCHES = 2
Z = 16
HALF = 128
QUAD = 4
NEG = -1e30

BF = jnp.bfloat16
F32 = jnp.float32


def nn(a, b):
    return lax.dot_general(a, b, (((1,), (0,)), ((), ())), preferred_element_type=F32)


def nt(a, b):
    return lax.dot_general(a, b, (((1,), (1,)), ((), ())), preferred_element_type=F32)


def down(n):
    return lax.broadcasted_iota(jnp.int32, (n, 1), 0)


def along(n):
    return lax.broadcasted_iota(jnp.int32, (1, n), 1)


def core():
    return lax.rem(lax.axis_index("row"), 2)


def by_core(first, second):
    mine = core()
    return first * (1 - mine) + second * mine


def y_source(r):
    return (((r >> 2) & 1) << 7) + ((r >> 3) << 2) + (r & 3)


def x_source(r):
    return ((r >> 7) << 7) + ((r & 7) << 4) + ((r >> 3) & 15)


def place(t, part):
    line, at = t >> 6, t & 63
    y_place = (part << 8) + ((at >> 1) << 3) + ((at & 1) << 2) + line
    x_peer = ((at >> 4) << 3) + (part << 2) + line
    x_place = (((at >> 3) & 1) << 8) + (x_peer << 3) + (at & 7)
    return by_core(y_place, x_place)


def z_line(r):
    return r >> 4


def long_line(r):
    return r >> 6


def onehot(a, b):
    return jnp.where(a == b, 1.0, 0.0).astype(BF)


def pack_body(feat, cot, mine, theirs):
    r = down(T)
    for out, source in (
        (theirs, by_core(x_source(r), y_source(r))),
        (mine, by_core(y_source(r), x_source(r))),
    ):
        pick = onehot(source, along(T))
        out[:, :C] = nn(pick, feat[...]).astype(BF)
        out[:, C:] = nn(pick, cot[...]).astype(BF)


def merge_body(mine, took, send):
    send[:, : 2 * C] = mine[...]
    send[:, 2 * C :] = took[...]


def axis_math(line, feat, cot, w_qkv, w_qkv_t, w_out):
    scale = 1.0 / math.sqrt(DEPTH)
    feat_t = nt(onehot(down(T), along(T)), feat).astype(BF)
    proj = nn(feat, w_qkv[...]).astype(BF)
    proj_t = nt(w_qkv_t[...], feat).astype(BF)
    gmix = nt(cot, w_out[...]).astype(BF)
    gmix_t = nt(w_out[...], cot).astype(BF)
    q, k, v = proj[:, :C], proj[:, C : 2 * C], proj[:, 2 * C :]
    q_t, k_t, v_t = proj_t[:C], proj_t[C : 2 * C], proj_t[2 * C :]
    bias = jnp.where(line(down(HALF)) == line(along(QUAD * HALF) & (HALF - 1)), 0.0, NEG)
    head_of_lane = jnp.broadcast_to(along(HALF) >> 5, (HALF, HALF))
    blank = jnp.zeros((HALF, HALF), BF)
    strip = jnp.zeros((DEPTH, HALF), BF)

    def spread(a_t):
        return jnp.concatenate(
            [
                jnp.concatenate(
                    [a_t[i * DEPTH : (i + 1) * DEPTH] if i == j else strip for i in range(QUAD)],
                    axis=0,
                )
                for j in range(QUAD)
            ],
            axis=1,
        )

    def stack(a):
        return jnp.concatenate(
            [jnp.where(head_of_lane == j, a, blank) for j in range(QUAD)], axis=0
        )

    def per_head(a_t, m):
        return jnp.concatenate(
            [
                nn(a_t[j * DEPTH : (j + 1) * DEPTH], m[:, j * HALF : (j + 1) * HALF])
                for j in range(QUAD)
            ],
            axis=0,
        )

    blocks = [
        (slice(half * HALF, (half + 1) * HALF), slice(quad * HALF, (quad + 1) * HALF))
        for half in range(2)
        for quad in range(2)
    ]
    all_scores = [nn(k[t, c], spread(q_t[c, t])) + bias for t, c in blocks]
    all_dprobs = [nn(v[t, c], spread(gmix_t[c, t])) for t, c in blocks]
    soft = []
    for scores, dprobs in zip(all_scores, all_dprobs):
        top = jnp.max(scores, axis=0, keepdims=True)
        e = jnp.exp((scores - top) * scale)
        probs = e * (1.0 / jnp.sum(e, axis=0, keepdims=True))
        mean = jnp.sum(dprobs * probs, axis=0, keepdims=True)
        soft.append((probs.astype(BF), (probs * (dprobs - mean) * scale).astype(BF)))
    parts = []
    for (t, c), (rounded, dround) in zip(blocks, soft):
        out_t = per_head(v_t[c, t], rounded)
        dv = nn(rounded, stack(gmix[t, c]))
        dq_t = per_head(k_t[c, t], dround)
        dk = nn(dround, stack(q[t, c]))
        parts.append([m.astype(BF) for m in (out_t, dq_t, dk, dv)])

    def whole(at, transposed):
        p = [[parts[2 * half + quad][at] for quad in range(2)] for half in range(2)]
        if transposed:
            p = [[p[j][i] for j in range(2)] for i in range(2)]
        return jnp.concatenate([jnp.concatenate(r, axis=1) for r in p], axis=0)

    out_t, dq_t = whole(0, True), whole(1, True)
    dk, dv = whole(2, False), whole(3, False)
    grads = (nt(feat_t, dq_t), nn(feat_t, dk), nn(feat_t, dv), nn(out_t, cot))
    return (out_t, dq_t, dk, dv), grads


def results(out_t, dq_t, dk, dv, w_qkv):
    dfeat_t = nn(w_qkv[:, :C], dq_t) + nt(w_qkv[:, C : 2 * C], dk) + nt(w_qkv[:, 2 * C :], dv)
    return out_t, dfeat_t.astype(BF)


def z_body(feat, cot, w_qkv, w_qkv_t, w_out, back, grad):
    parts, terms = axis_math(z_line, feat[...], cot[...], w_qkv, w_qkv_t, w_out)
    eye = onehot(down(T), along(T))
    for at, part_t in enumerate(results(*parts, w_qkv)):
        back[:, at * C : (at + 1) * C] = nt(eye, part_t).astype(BF)
    for at, term in enumerate(terms):
        grad[:, at * C : (at + 1) * C] = term.astype(BF)


def lines_body(got, w_qkv, w_qkv_t, w_out, grad_z, *refs):
    keep, give, total = refs[8:]
    for part in range(2):
        t = place(down(T), part)
        first, second = onehot(t, along(T)), onehot(t, along(T) + T)
        feat = (nn(first, got[:, :C]) + nn(second, got[:, 2 * C : 3 * C])).astype(BF)
        cot = (nn(first, got[:, C : 2 * C]) + nn(second, got[:, 3 * C :])).astype(BF)
        held, terms = axis_math(long_line, feat, cot, w_qkv, w_qkv_t, w_out)
        for ref, value in zip(refs[part * 4 : part * 4 + 4], held):
            ref[...] = value
        for at, term in enumerate(terms):
            cols = slice(at * C, (at + 1) * C)
            total[:, cols] = (total[:, cols] if part else grad_z[:, cols].astype(F32)) + term
    mine = core()
    keep[...] = total[pl.ds(pl.multiple_of(mine * 128, 128), 128)]
    give[...] = total[pl.ds(pl.multiple_of((1 - mine) * 128, 128), 128)].astype(BF)


def back_body(*refs):
    w_qkv, back_out, back_feat = refs[8:]
    sums = [jnp.zeros((T, C), F32)] * 4
    for part in range(2):
        t = place(along(T), part)
        first, second = onehot(down(T), t), onehot(down(T) + T, t)
        out_t, feat_t = results(*[ref[...] for ref in refs[part * 4 : part * 4 + 4]], w_qkv)
        new = (nt(first, out_t), nt(second, out_t), nt(first, feat_t), nt(second, feat_t))
        sums = [a + b for a, b in zip(sums, new)]
    back_out[:, :C], back_out[:, C:] = sums[0].astype(BF), sums[1].astype(BF)
    back_feat[:, :C], back_feat[:, C:] = sums[2].astype(BF), sums[3].astype(BF)


def first_pack_body(back_out, keep, took, send):
    send[:, : 2 * C] = back_out[...]
    half = (keep[...] + took[...].astype(F32)).astype(BF)
    send[:128, 2 * C :] = half[:, : 2 * C]
    send[128:, 2 * C :] = half[:, 2 * C :]


def block_body(got, send):
    block = jnp.sum(got[:, 2 * C :].astype(F32).reshape(32, 8, 2 * C), axis=0)
    send[...] = jnp.concatenate([block] * 8, axis=0).astype(BF)


def last_pack_body(factor, got, back_feat, send):
    block = jnp.sum(got[...].astype(F32).reshape(8, 8, 2 * C), axis=0) * factor
    send[:, : 2 * C] = back_feat[...]
    send[:, 2 * C :] = jnp.concatenate([block] * 32, axis=0).astype(BF)


def give_body(got_first, got_last, give):
    give[:, :C] = got_first[:, C : 2 * C]
    give[:, C : 2 * C] = got_last[:, C : 2 * C]
    give[:, 2 * C :] = got_last[:, 2 * C :]


def final_body(back_z, got_first, got_last, took, w_out, update, grad_in, grad_qkv, grad_out):
    r = along(T)
    put_mine = onehot(down(T), by_core(y_source(r), x_source(r)))
    put_theirs = onehot(down(T), by_core(x_source(r), y_source(r)))
    sums = []
    for at, rows in enumerate((got_first[:, :C], got_last[:, :C])):
        cols = slice(at * C, (at + 1) * C)
        sums.append(
            (
                back_z[:, cols].astype(F32) + nn(put_mine, rows) + nn(put_theirs, took[:, cols])
            ).astype(BF)
        )
    update[...] = nn(sums[0], w_out[...]).astype(BF)
    grad_in[...] = sums[1]
    for src, half in ((got_last, core()), (took, 1 - core())):
        rows = pl.ds(pl.multiple_of(half * 128, 128), 128)
        grad_qkv[rows, : 2 * C] = src[:128, 2 * C :].astype(F32)
        grad_qkv[rows, 2 * C :] = src[128:, 2 * C : 3 * C].astype(F32)
        grad_out[rows, :] = src[128:, 3 * C :].astype(F32)


def call(body, outs, flops, *args, scratch=()):
    return pl.pallas_call(
        body,
        out_shape=outs,
        in_specs=[pl.BlockSpec(memory_space=pltpu.VMEM)] * len(args),
        out_specs=[pl.BlockSpec(memory_space=pltpu.VMEM)] * len(outs),
        scratch_shapes=scratch,
        compiler_params=pltpu.CompilerParams(vmem_limit_bytes=40 * 2**20),
        cost_estimate=pl.CostEstimate(flops=flops, bytes_accessed=2**20, transcendentals=2**19),
    )(*args)


def shape(rows, cols, dtype):
    return jax.ShapeDtypeStruct((rows, cols), dtype)


AXES = ("dp", "row", "col")


def device(x, mine, y, z):
    return z % 2 * 256 + (x * 2 + mine) * 32 + y * 4 + z // 2


X, Y, ZS = range(4), range(8), range(8)
LONG = [[device(x, 0, y, z) for y in Y for z in ZS[dp::2]] for x in X for dp in range(2)] + [
    [device(x, 1, y, z) for x in X for z in ZS] for y in Y
]
SHORT = [
    [device(x, 0, y, 2 * z + dp) for x in X for dp in range(2)] for y in Y for z in range(4)
] + [[device(x, 1, y, z) for y in Y] for x in X for z in ZS]


def exchange(rows, groups):
    return lax.all_to_all(
        rows, AXES, split_axis=0, concat_axis=0, axis_index_groups=groups, tiled=True
    )


def swap(rows):
    return lax.ppermute(rows, "row", [(i, i ^ 1) for i in range(8)])


def body(features, w_qkv, w_out, cotangent):
    local_shape = features.shape
    feat = features.reshape(T, C)
    cot = cotangent.reshape(T, C)
    weights = (w_qkv, w_qkv.T, w_out)
    cube = 2 * T * T * C
    pair = shape(T, 2 * C, BF)
    quad = shape(T, 4 * C, BF)
    mine, give = call(pack_body, [pair, pair], cube * 4, feat, cot)
    (send,) = call(merge_body, [quad], 2**20, mine, swap(give))
    got = exchange(send, LONG)
    back_z, grad_z = call(z_body, [pair, shape(C, 4 * C, BF)], cube * 70, feat, cot, *weights)
    *held, keep, give = call(
        lines_body,
        [shape(T, C, BF)] * 8 + [shape(128, 4 * C, F32), shape(128, 4 * C, BF)],
        cube * 140,
        got,
        *weights,
        grad_z,
        scratch=[pltpu.VMEM((C, 4 * C), F32)],
    )
    took = swap(give)
    back_out, back_feat = call(back_body, [pair] * 2, cube * 20, *held, w_qkv)
    (send,) = call(first_pack_body, [quad], 2**20, back_out, keep, took)
    got_first = exchange(send, LONG)
    (send,) = call(block_body, [shape(64, 2 * C, BF)], 2**20, got_first)
    blocks = exchange(send, SHORT)
    factor = 1.0 / math.sqrt(PATCHES * 64 * 64 * 16)
    (send,) = call(functools.partial(last_pack_body, factor), [quad], 2**20, blocks, back_feat)
    got_last = exchange(send, LONG)
    (give,) = call(give_body, [quad], 2**20, got_first, got_last)
    update, grad_in, grad_qkv, grad_out = call(
        final_body,
        [shape(T, C, BF)] * 2 + [shape(C, 3 * C, F32), shape(C, C, F32)],
        cube * 6,
        back_z,
        got_first,
        got_last,
        swap(give),
        w_out,
    )
    return (update.reshape(local_shape), grad_in.reshape(local_shape), grad_qkv, grad_out)


def solution(mesh):
    placed = (P("dp", "col", "row", None, None), P(), P(), P("dp", "col", "row", None, None))
    return jax.shard_map(
        body,
        mesh=mesh,
        in_specs=placed,
        out_specs=(P("dp", "col", "row", None, None), P("dp", "col", "row", None, None), P(), P()),
        check_vma=False,
    )
```

```python
import functools
import math

import jax
import jax.numpy as jnp
from jax import lax
from jax.experimental import pallas as pl
from jax.experimental.pallas import tpu as pltpu
from jax.sharding import PartitionSpec as P

HEADS = 8
DEPTH = 32
C = 256
T = 256
PATCHES = 2
Z = 16
HALF = 128
QUAD = 4
NEG = -1e30

BF = jnp.bfloat16
F32 = jnp.float32


def nn(a, b):
    return lax.dot_general(a, b, (((1,), (0,)), ((), ())), preferred_element_type=F32)


def nt(a, b):
    return lax.dot_general(a, b, (((1,), (1,)), ((), ())), preferred_element_type=F32)


def down(n):
    return lax.broadcasted_iota(jnp.int32, (n, 1), 0)


def along(n):
    return lax.broadcasted_iota(jnp.int32, (1, n), 1)


def core():
    return lax.rem(lax.axis_index("row"), 2)


def by_core(first, second):
    mine = core()
    return first * (1 - mine) + second * mine


def y_source(r):
    return (((r >> 2) & 1) << 7) + ((r >> 3) << 2) + (r & 3)


def x_source(r):
    return ((r >> 7) << 7) + ((r & 7) << 4) + ((r >> 3) & 15)


def place(t):
    line, at = t >> 6, t & 63
    y_place = ((line >> 2) << 8) + ((at >> 1) << 3) + ((at & 1) << 2) + (line & 3)
    x_place = (((at >> 3) & 1) << 8) + ((at >> 4) << 6) + (line << 3) + (at & 7)
    return by_core(y_place, x_place)


def z_line(r):
    return r >> 4


def long_line(r):
    return r >> 6


def onehot(a, b):
    return jnp.where(a == b, 1.0, 0.0).astype(BF)


def pack_body(feat, cot, mine, theirs):
    r = down(T)
    for out, source in (
        (theirs, by_core(x_source(r), y_source(r))),
        (mine, by_core(y_source(r), x_source(r))),
    ):
        pick = onehot(source, along(T))
        out[:, :C] = nn(pick, feat[...]).astype(BF)
        out[:, C:] = nn(pick, cot[...]).astype(BF)


def merge_body(mine, took, send):
    send[:, : 2 * C] = mine[...]
    send[:, 2 * C :] = took[...]


def axis_math(line, feat, cot, w_qkv, w_qkv_t, w_out):
    scale = 1.0 / math.sqrt(DEPTH)
    feat_t = nt(onehot(down(T), along(T)), feat).astype(BF)
    proj = nn(feat, w_qkv[...]).astype(BF)
    proj_t = nt(w_qkv_t[...], feat).astype(BF)
    gmix = nt(cot, w_out[...]).astype(BF)
    gmix_t = nt(w_out[...], cot).astype(BF)
    q, k, v = proj[:, :C], proj[:, C : 2 * C], proj[:, 2 * C :]
    q_t, k_t, v_t = proj_t[:C], proj_t[C : 2 * C], proj_t[2 * C :]
    bias = jnp.where(line(down(HALF)) == line(along(QUAD * HALF) & (HALF - 1)), 0.0, NEG)
    head_of_lane = jnp.broadcast_to(along(HALF) >> 5, (HALF, HALF))
    blank = jnp.zeros((HALF, HALF), BF)
    strip = jnp.zeros((DEPTH, HALF), BF)

    def spread(a_t):
        return jnp.concatenate(
            [
                jnp.concatenate(
                    [a_t[i * DEPTH : (i + 1) * DEPTH] if i == j else strip for i in range(QUAD)],
                    axis=0,
                )
                for j in range(QUAD)
            ],
            axis=1,
        )

    def stack(a):
        return jnp.concatenate(
            [jnp.where(head_of_lane == j, a, blank) for j in range(QUAD)], axis=0
        )

    def per_head(a_t, m):
        return jnp.concatenate(
            [
                nn(a_t[j * DEPTH : (j + 1) * DEPTH], m[:, j * HALF : (j + 1) * HALF])
                for j in range(QUAD)
            ],
            axis=0,
        )

    halves = feat.shape[0] // HALF
    blocks = [
        (slice(half * HALF, (half + 1) * HALF), slice(quad * HALF, (quad + 1) * HALF))
        for half in range(halves)
        for quad in range(2)
    ]
    all_scores = [nn(k[t, c], spread(q_t[c, t])) + bias for t, c in blocks]
    all_dprobs = [nn(v[t, c], spread(gmix_t[c, t])) for t, c in blocks]
    soft = []
    for scores, dprobs in zip(all_scores, all_dprobs):
        top = jnp.max(scores, axis=0, keepdims=True)
        e = jnp.exp((scores - top) * scale)
        probs = e * (1.0 / jnp.sum(e, axis=0, keepdims=True))
        mean = jnp.sum(dprobs * probs, axis=0, keepdims=True)
        soft.append((probs.astype(BF), (probs * (dprobs - mean) * scale).astype(BF)))
    parts = []
    for (t, c), (rounded, dround) in zip(blocks, soft):
        out_t = per_head(v_t[c, t], rounded)
        dv = nn(rounded, stack(gmix[t, c]))
        dq_t = per_head(k_t[c, t], dround)
        dk = nn(dround, stack(q[t, c]))
        parts.append([m.astype(BF) for m in (out_t, dq_t, dk, dv)])

    def whole(at, transposed):
        p = [[parts[2 * half + quad][at] for quad in range(2)] for half in range(halves)]
        if transposed:
            p = [list(row) for row in zip(*p)]
        return jnp.concatenate([jnp.concatenate(r, axis=1) for r in p], axis=0)

    out_t, dq_t = whole(0, True), whole(1, True)
    dk, dv = whole(2, False), whole(3, False)
    grads = (nt(feat_t, dq_t), nn(feat_t, dk), nn(feat_t, dv), nn(out_t, cot))
    return (out_t, dq_t, dk, dv), grads


def results(out_t, dq_t, dk, dv, w_qkv):
    dfeat_t = nn(w_qkv[:, :C], dq_t) + nt(w_qkv[:, C : 2 * C], dk) + nt(w_qkv[:, 2 * C :], dv)
    return out_t, dfeat_t.astype(BF)


def z_body(feat, cot, w_qkv, w_qkv_t, w_out, back, grad):
    parts, terms = axis_math(z_line, feat[...], cot[...], w_qkv, w_qkv_t, w_out)
    eye = onehot(down(T), along(T))
    for at, part_t in enumerate(results(*parts, w_qkv)):
        back[:, at * C : (at + 1) * C] = nt(eye, part_t).astype(BF)
    for at, term in enumerate(terms):
        grad[:, at * C : (at + 1) * C] = term.astype(BF)


def lines_body(got, w_qkv, w_qkv_t, w_out, grad_z, out_t, dq_t, dk, dv, keep, give, total):
    sort = onehot(place(down(2 * T)), along(2 * T))
    feat = nn(sort, jnp.concatenate([got[:, :C], got[:, 2 * C : 3 * C]], axis=0)).astype(BF)
    cot = nn(sort, jnp.concatenate([got[:, C : 2 * C], got[:, 3 * C :]], axis=0)).astype(BF)
    held, terms = axis_math(long_line, feat, cot, w_qkv, w_qkv_t, w_out)
    for ref, value in zip((out_t, dq_t, dk, dv), held):
        ref[...] = value
    for at, term in enumerate(terms):
        cols = slice(at * C, (at + 1) * C)
        total[:, cols] = grad_z[:, cols].astype(F32) + term
    mine = core()
    keep[...] = total[pl.ds(pl.multiple_of(mine * 128, 128), 128)]
    give[...] = total[pl.ds(pl.multiple_of((1 - mine) * 128, 128), 128)].astype(BF)


def back_body(out_t, dq_t, dk, dv, w_qkv, back_out, back_feat):
    unsort = onehot(down(2 * T), place(along(2 * T)))
    parts = results(out_t[...], dq_t[...], dk[...], dv[...], w_qkv)
    for part_t, back in zip(parts, (back_out, back_feat)):
        rows = nt(unsort, part_t).astype(BF)
        back[:, :C], back[:, C:] = rows[:T], rows[T:]


def first_pack_body(back_out, keep, took, send):
    send[:, : 2 * C] = back_out[...]
    half = (keep[...] + took[...].astype(F32)).astype(BF)
    send[:128, 2 * C :] = half[:, : 2 * C]
    send[128:, 2 * C :] = half[:, 2 * C :]


def block_body(got, send):
    block = jnp.sum(got[:, 2 * C :].astype(F32).reshape(32, 8, 2 * C), axis=0)
    send[...] = jnp.concatenate([block] * 8, axis=0).astype(BF)


def last_pack_body(factor, got, back_feat, send):
    block = jnp.sum(got[...].astype(F32).reshape(8, 8, 2 * C), axis=0) * factor
    send[:, : 2 * C] = back_feat[...]
    send[:, 2 * C :] = jnp.concatenate([block] * 32, axis=0).astype(BF)


def give_body(got_first, got_last, give):
    give[:, :C] = got_first[:, C : 2 * C]
    give[:, C : 2 * C] = got_last[:, C : 2 * C]
    give[:, 2 * C :] = got_last[:, 2 * C :]


def final_body(back_z, got_first, got_last, took, w_out, update, grad_in, grad_qkv, grad_out):
    r = along(T)
    put_mine = onehot(down(T), by_core(y_source(r), x_source(r)))
    put_theirs = onehot(down(T), by_core(x_source(r), y_source(r)))
    sums = []
    for at, rows in enumerate((got_first[:, :C], got_last[:, :C])):
        cols = slice(at * C, (at + 1) * C)
        sums.append(
            (
                back_z[:, cols].astype(F32) + nn(put_mine, rows) + nn(put_theirs, took[:, cols])
            ).astype(BF)
        )
    update[...] = nn(sums[0], w_out[...]).astype(BF)
    grad_in[...] = sums[1]
    for src, half in ((got_last, core()), (took, 1 - core())):
        rows = pl.ds(pl.multiple_of(half * 128, 128), 128)
        grad_qkv[rows, : 2 * C] = src[:128, 2 * C :].astype(F32)
        grad_qkv[rows, 2 * C :] = src[128:, 2 * C : 3 * C].astype(F32)
        grad_out[rows, :] = src[128:, 3 * C :].astype(F32)


def call(body, outs, flops, *args, scratch=()):
    return pl.pallas_call(
        body,
        out_shape=outs,
        in_specs=[pl.BlockSpec(memory_space=pltpu.VMEM)] * len(args),
        out_specs=[pl.BlockSpec(memory_space=pltpu.VMEM)] * len(outs),
        scratch_shapes=scratch,
        compiler_params=pltpu.CompilerParams(vmem_limit_bytes=40 * 2**20),
        cost_estimate=pl.CostEstimate(flops=flops, bytes_accessed=2**20, transcendentals=2**19),
    )(*args)


def shape(rows, cols, dtype):
    return jax.ShapeDtypeStruct((rows, cols), dtype)


AXES = ("dp", "row", "col")


def device(x, mine, y, z):
    return z % 2 * 256 + (x * 2 + mine) * 32 + y * 4 + z // 2


X, Y, ZS = range(4), range(8), range(8)
LONG = [[device(x, 0, y, z) for y in Y for z in ZS[dp::2]] for x in X for dp in range(2)] + [
    [device(x, 1, y, z) for x in X for z in ZS] for y in Y
]
SHORT = [
    [device(x, 0, y, 2 * z + dp) for x in X for dp in range(2)] for y in Y for z in range(4)
] + [[device(x, 1, y, z) for y in Y] for x in X for z in ZS]


def exchange(rows, groups):
    return lax.all_to_all(
        rows, AXES, split_axis=0, concat_axis=0, axis_index_groups=groups, tiled=True
    )


def swap(rows):
    return lax.ppermute(rows, "row", [(i, i ^ 1) for i in range(8)])


def body(features, w_qkv, w_out, cotangent):
    local_shape = features.shape
    feat = features.reshape(T, C)
    cot = cotangent.reshape(T, C)
    weights = (w_qkv, w_qkv.T, w_out)
    cube = 2 * T * T * C
    pair = shape(T, 2 * C, BF)
    quad = shape(T, 4 * C, BF)
    mine, give = call(pack_body, [pair, pair], cube * 4, feat, cot)
    (send,) = call(merge_body, [quad], 2**20, mine, swap(give))
    got = exchange(send, LONG)
    back_z, grad_z = call(z_body, [pair, shape(C, 4 * C, BF)], cube * 70, feat, cot, *weights)
    *held, keep, give = call(
        lines_body,
        [shape(C, 2 * T, BF)] * 2
        + [shape(2 * T, C, BF)] * 2
        + [shape(128, 4 * C, F32), shape(128, 4 * C, BF)],
        cube * 140,
        got,
        *weights,
        grad_z,
        scratch=[pltpu.VMEM((C, 4 * C), F32)],
    )
    took = swap(give)
    back_out, back_feat = call(back_body, [pair] * 2, cube * 20, *held, w_qkv)
    (send,) = call(first_pack_body, [quad], 2**20, back_out, keep, took)
    got_first = exchange(send, LONG)
    (send,) = call(block_body, [shape(64, 2 * C, BF)], 2**20, got_first)
    blocks = exchange(send, SHORT)
    factor = 1.0 / math.sqrt(PATCHES * 64 * 64 * 16)
    (send,) = call(functools.partial(last_pack_body, factor), [quad], 2**20, blocks, back_feat)
    got_last = exchange(send, LONG)
    (give,) = call(give_body, [quad], 2**20, got_first, got_last)
    update, grad_in, grad_qkv, grad_out = call(
        final_body,
        [shape(T, C, BF)] * 2 + [shape(C, 3 * C, F32), shape(C, C, F32)],
        cube * 6,
        back_z,
        got_first,
        got_last,
        swap(give),
        w_out,
    )
    return (update.reshape(local_shape), grad_in.reshape(local_shape), grad_qkv, grad_out)


def solution(mesh):
    placed = (P("dp", "col", "row", None, None), P(), P(), P("dp", "col", "row", None, None))
    return jax.shard_map(
        body,
        mesh=mesh,
        in_specs=placed,
        out_specs=(P("dp", "col", "row", None, None), P("dp", "col", "row", None, None), P(), P()),
        check_vma=False,
    )
```

```python
import functools
import math

import jax
import jax.numpy as jnp
from jax import lax
from jax.experimental import pallas as pl
from jax.experimental.pallas import tpu as pltpu
from jax.sharding import PartitionSpec as P

HEADS = 8
DEPTH = 32
C = 256
T = 256
PATCHES = 2
Z = 16
HALF = 128
QUAD = 4
NEG = -1e30

BF = jnp.bfloat16
F32 = jnp.float32


def nn(a, b):
    return lax.dot_general(a, b, (((1,), (0,)), ((), ())), preferred_element_type=F32)


def nt(a, b):
    return lax.dot_general(a, b, (((1,), (1,)), ((), ())), preferred_element_type=F32)


def down(n):
    return lax.broadcasted_iota(jnp.int32, (n, 1), 0)


def along(n):
    return lax.broadcasted_iota(jnp.int32, (1, n), 1)


def core():
    return lax.rem(lax.axis_index("row"), 2)


def by_core(first, second):
    mine = core()
    return first * (1 - mine) + second * mine


def y_source(r):
    return (((r >> 2) & 1) << 7) + ((r >> 3) << 2) + (r & 3)


def x_source(r):
    return ((r >> 7) << 7) + ((r & 7) << 4) + ((r >> 3) & 15)


def place(t):
    line, at = t >> 6, t & 63
    y_place = ((line >> 2) << 8) + ((at >> 1) << 3) + ((at & 1) << 2) + (line & 3)
    x_place = (((at >> 3) & 1) << 8) + ((at >> 4) << 6) + (line << 3) + (at & 7)
    return by_core(y_place, x_place)


def z_line(r):
    return r >> 4


def long_line(r):
    return r >> 6


def onehot(a, b):
    return jnp.where(a == b, 1.0, 0.0).astype(BF)


def pack_body(first, second, feat, cot, out):
    pick = onehot(by_core(first(down(T)), second(down(T))), along(T))
    out[:, :C] = nn(pick, feat[...]).astype(BF)
    out[:, C:] = nn(pick, cot[...]).astype(BF)


def merge_body(mine, took, send):
    send[:, : 2 * C] = mine[...]
    send[:, 2 * C :] = took[...]


def axis_math(line, feat, cot, w_qkv, w_qkv_t, w_out):
    scale = 1.0 / math.sqrt(DEPTH)
    feat_t = nt(onehot(down(T), along(T)), feat).astype(BF)
    proj = nn(feat, w_qkv[...]).astype(BF)
    proj_t = nt(w_qkv_t[...], feat).astype(BF)
    gmix = nt(cot, w_out[...]).astype(BF)
    gmix_t = nt(w_out[...], cot).astype(BF)
    q, k, v = proj[:, :C], proj[:, C : 2 * C], proj[:, 2 * C :]
    q_t, k_t, v_t = proj_t[:C], proj_t[C : 2 * C], proj_t[2 * C :]
    bias = jnp.where(line(down(HALF)) == line(along(QUAD * HALF) & (HALF - 1)), 0.0, NEG)
    head_of_lane = jnp.broadcast_to(along(HALF) >> 5, (HALF, HALF))
    blank = jnp.zeros((HALF, HALF), BF)
    strip = jnp.zeros((DEPTH, HALF), BF)

    def spread(a_t):
        return jnp.concatenate(
            [
                jnp.concatenate(
                    [a_t[i * DEPTH : (i + 1) * DEPTH] if i == j else strip for i in range(QUAD)],
                    axis=0,
                )
                for j in range(QUAD)
            ],
            axis=1,
        )

    def stack(a):
        return jnp.concatenate(
            [jnp.where(head_of_lane == j, a, blank) for j in range(QUAD)], axis=0
        )

    def per_head(a_t, m):
        return jnp.concatenate(
            [
                nn(a_t[j * DEPTH : (j + 1) * DEPTH], m[:, j * HALF : (j + 1) * HALF])
                for j in range(QUAD)
            ],
            axis=0,
        )

    halves = feat.shape[0] // HALF
    blocks = [
        (slice(half * HALF, (half + 1) * HALF), slice(quad * HALF, (quad + 1) * HALF))
        for half in range(halves)
        for quad in range(2)
    ]
    all_scores = [nn(k[t, c], spread(q_t[c, t])) + bias for t, c in blocks]
    all_dprobs = [nn(v[t, c], spread(gmix_t[c, t])) for t, c in blocks]
    soft = []
    for scores, dprobs in zip(all_scores, all_dprobs):
        top = jnp.max(scores, axis=0, keepdims=True)
        e = jnp.exp((scores - top) * scale)
        probs = e * (1.0 / jnp.sum(e, axis=0, keepdims=True))
        mean = jnp.sum(dprobs * probs, axis=0, keepdims=True)
        soft.append((probs.astype(BF), (probs * (dprobs - mean) * scale).astype(BF)))
    parts = []
    for (t, c), (rounded, dround) in zip(blocks, soft):
        out_t = per_head(v_t[c, t], rounded)
        dv = nn(rounded, stack(gmix[t, c]))
        dq_t = per_head(k_t[c, t], dround)
        dk = nn(dround, stack(q[t, c]))
        parts.append([m.astype(BF) for m in (out_t, dq_t, dk, dv)])

    def whole(at, transposed):
        p = [[parts[2 * half + quad][at] for quad in range(2)] for half in range(halves)]
        if transposed:
            p = [list(row) for row in zip(*p)]
        return jnp.concatenate([jnp.concatenate(r, axis=1) for r in p], axis=0)

    out_t, dq_t = whole(0, True), whole(1, True)
    dk, dv = whole(2, False), whole(3, False)
    grads = (nt(feat_t, dq_t), nn(feat_t, dk), nn(feat_t, dv), nn(out_t, cot))
    return (out_t, dq_t, dk, dv), grads


def results(out_t, dq_t, dk, dv, w_qkv):
    dfeat_t = nn(w_qkv[:, :C], dq_t) + nt(w_qkv[:, C : 2 * C], dk) + nt(w_qkv[:, 2 * C :], dv)
    return out_t, dfeat_t.astype(BF)


def z_body(feat, cot, w_qkv, w_qkv_t, w_out, back, grad):
    parts, terms = axis_math(z_line, feat[...], cot[...], w_qkv, w_qkv_t, w_out)
    eye = onehot(down(T), along(T))
    for at, part_t in enumerate(results(*parts, w_qkv)):
        back[:, at * C : (at + 1) * C] = nt(eye, part_t).astype(BF)
    for at, term in enumerate(terms):
        grad[:, at * C : (at + 1) * C] = term.astype(BF)


def lines_body(got, w_qkv, w_qkv_t, w_out, grad_z, out_t, dq_t, dk, dv, keep, give, total):
    sort = onehot(place(down(2 * T)), along(2 * T))
    feat = nn(sort, jnp.concatenate([got[:, :C], got[:, 2 * C : 3 * C]], axis=0)).astype(BF)
    cot = nn(sort, jnp.concatenate([got[:, C : 2 * C], got[:, 3 * C :]], axis=0)).astype(BF)
    held, terms = axis_math(long_line, feat, cot, w_qkv, w_qkv_t, w_out)
    for ref, value in zip((out_t, dq_t, dk, dv), held):
        ref[...] = value
    for at, term in enumerate(terms):
        cols = slice(at * C, (at + 1) * C)
        total[:, cols] = grad_z[:, cols].astype(F32) + term
    mine = core()
    keep[...] = total[pl.ds(pl.multiple_of(mine * 128, 128), 128)]
    give[...] = total[pl.ds(pl.multiple_of((1 - mine) * 128, 128), 128)].astype(BF)


def back_body(out_t, dq_t, dk, dv, w_qkv, back_out, back_feat):
    unsort = onehot(down(2 * T), place(along(2 * T)))
    parts = results(out_t[...], dq_t[...], dk[...], dv[...], w_qkv)
    for part_t, back in zip(parts, (back_out, back_feat)):
        rows = nt(unsort, part_t).astype(BF)
        back[:, :C], back[:, C:] = rows[:T], rows[T:]


def first_pack_body(back_out, keep, took, send):
    send[:, : 2 * C] = back_out[...]
    half = (keep[...] + took[...].astype(F32)).astype(BF)
    send[:128, 2 * C :] = half[:, : 2 * C]
    send[128:, 2 * C :] = half[:, 2 * C :]


def block_body(got, send):
    block = jnp.sum(got[:, 2 * C :].astype(F32).reshape(32, 8, 2 * C), axis=0)
    send[...] = jnp.concatenate([block] * 8, axis=0).astype(BF)


def last_pack_body(factor, got, back_feat, send):
    block = jnp.sum(got[...].astype(F32).reshape(8, 8, 2 * C), axis=0) * factor
    send[:, : 2 * C] = back_feat[...]
    send[:, 2 * C :] = jnp.concatenate([block] * 32, axis=0).astype(BF)


def give_body(got_first, got_last, give):
    give[:, :C] = got_first[:, C : 2 * C]
    give[:, C : 2 * C] = got_last[:, C : 2 * C]
    give[:, 2 * C :] = got_last[:, 2 * C :]


def final_body(
    back_z, got_first, got_last, took, w_out, update, grad_in, grad_qkv, grad_out, qkv, out, rows, sem
):
    copies = []

    def send_home(src, dst):
        copies.append(pltpu.make_async_copy(src, dst, sem.at[len(copies)]))
        copies[-1].start()

    for at, (src, half) in enumerate(((got_last, core()), (took, 1 - core()))):
        place_of = pl.ds(pl.multiple_of(half * 128, 128), 128)
        qkv[at, :, : 2 * C] = src[:128, 2 * C :].astype(F32)
        qkv[at, :, 2 * C :] = src[128:, 2 * C : 3 * C].astype(F32)
        out[at] = src[128:, 3 * C :].astype(F32)
        send_home(qkv.at[at], grad_qkv.at[place_of])
        send_home(out.at[at], grad_out.at[place_of])
    r = along(T)
    put_mine = onehot(down(T), by_core(y_source(r), x_source(r)))
    put_theirs = onehot(down(T), by_core(x_source(r), y_source(r)))
    for at, (got, home) in enumerate(((got_last, grad_in), (got_first, update))):
        cols = slice((1 - at) * C, (2 - at) * C)
        total = (
            back_z[:, cols].astype(F32)
            + nn(put_mine, got[:, :C])
            + nn(put_theirs, took[:, cols])
        ).astype(BF)
        rows[at] = nn(total, w_out[...]).astype(BF) if at else total
        send_home(rows.at[at], home)
    for copy in copies:
        copy.wait()


def call(body, outs, flops, *args, out_space=pltpu.VMEM, scratch=()):
    return pl.pallas_call(
        body,
        out_shape=outs,
        in_specs=[pl.BlockSpec(memory_space=pltpu.VMEM)] * len(args),
        out_specs=[pl.BlockSpec(memory_space=out_space)] * len(outs),
        scratch_shapes=scratch,
        compiler_params=pltpu.CompilerParams(vmem_limit_bytes=40 * 2**20),
        cost_estimate=pl.CostEstimate(flops=flops, bytes_accessed=2**20, transcendentals=2**19),
    )(*args)


def shape(rows, cols, dtype):
    return jax.ShapeDtypeStruct((rows, cols), dtype)


AXES = ("dp", "row", "col")


def device(x, mine, y, z):
    return z % 2 * 256 + (x * 2 + mine) * 32 + y * 4 + z // 2


X, Y, ZS = range(4), range(8), range(8)
LONG = [[device(x, 0, y, z) for y in Y for z in ZS[dp::2]] for x in X for dp in range(2)] + [
    [device(x, 1, y, z) for x in X for z in ZS] for y in Y
]
SHORT = [
    [device(x, 0, y, 2 * z + dp) for x in X for dp in range(2)] for y in Y for z in range(4)
] + [[device(x, 1, y, z) for y in Y] for x in X for z in ZS]


def exchange(rows, groups):
    return lax.all_to_all(
        rows, AXES, split_axis=0, concat_axis=0, axis_index_groups=groups, tiled=True
    )


def swap(rows):
    return lax.ppermute(rows, "row", [(i, i ^ 1) for i in range(8)])


def body(features, w_qkv, w_out, cotangent):
    local_shape = features.shape
    feat = features.reshape(T, C)
    cot = cotangent.reshape(T, C)
    weights = (w_qkv, w_qkv.T, w_out)
    cube = 2 * T * T * C
    pair = shape(T, 2 * C, BF)
    quad = shape(T, 4 * C, BF)
    (give,) = call(
        functools.partial(pack_body, x_source, y_source), [pair], cube * 2, feat, cot
    )
    took = swap(give)
    (mine,) = call(functools.partial(pack_body, y_source, x_source), [pair], cube * 2, feat, cot)
    (send,) = call(merge_body, [quad], 2**20, mine, took)
    got = exchange(send, LONG)
    back_z, grad_z = call(z_body, [pair, shape(C, 4 * C, BF)], cube * 70, feat, cot, *weights)
    *held, keep, give = call(
        lines_body,
        [shape(C, 2 * T, BF)] * 2
        + [shape(2 * T, C, BF)] * 2
        + [shape(128, 4 * C, F32), shape(128, 4 * C, BF)],
        cube * 140,
        got,
        *weights,
        grad_z,
        scratch=[pltpu.VMEM((C, 4 * C), F32)],
    )
    took = swap(give)
    back_out, back_feat = call(back_body, [pair] * 2, cube * 20, *held, w_qkv)
    (send,) = call(first_pack_body, [quad], 2**20, back_out, keep, took)
    got_first = exchange(send, LONG)
    (send,) = call(block_body, [shape(64, 2 * C, BF)], 2**20, got_first)
    blocks = exchange(send, SHORT)
    factor = 1.0 / math.sqrt(PATCHES * 64 * 64 * 16)
    (send,) = call(functools.partial(last_pack_body, factor), [quad], 2**20, blocks, back_feat)
    got_last = exchange(send, LONG)
    (give,) = call(give_body, [quad], 2**20, got_first, got_last)
    update, grad_in, grad_qkv, grad_out = call(
        final_body,
        [shape(T, C, BF)] * 2 + [shape(C, 3 * C, F32), shape(C, C, F32)],
        cube * 6,
        back_z,
        got_first,
        got_last,
        swap(give),
        w_out,
        out_space=pl.ANY,
        scratch=[
            pltpu.VMEM((2, 128, 3 * C), F32),
            pltpu.VMEM((2, 128, C), F32),
            pltpu.VMEM((2, T, C), BF),
            pltpu.SemaphoreType.DMA((6,)),
        ],
    )
    return (update.reshape(local_shape), grad_in.reshape(local_shape), grad_qkv, grad_out)


def solution(mesh):
    placed = (P("dp", "col", "row", None, None), P(), P(), P("dp", "col", "row", None, None))
    return jax.shard_map(
        body,
        mesh=mesh,
        in_specs=placed,
        out_specs=(P("dp", "col", "row", None, None), P("dp", "col", "row", None, None), P(), P()),
        check_vma=False,
    )
```

```python
import functools
import math

import jax
import jax.numpy as jnp
from jax import lax
from jax.experimental import pallas as pl
from jax.experimental.pallas import tpu as pltpu
from jax.sharding import PartitionSpec as P

HEADS = 8
DEPTH = 32
C = 256
T = 256
PATCHES = 2
Z = 16
HALF = 128
QUAD = 4
NEG = -1e30

BF = jnp.bfloat16
F32 = jnp.float32


def nn(a, b):
    return lax.dot_general(a, b, (((1,), (0,)), ((), ())), preferred_element_type=F32)


def nt(a, b):
    return lax.dot_general(a, b, (((1,), (1,)), ((), ())), preferred_element_type=F32)


def down(n):
    return lax.broadcasted_iota(jnp.int32, (n, 1), 0)


def along(n):
    return lax.broadcasted_iota(jnp.int32, (1, n), 1)


def core():
    return lax.rem(lax.axis_index("row"), 2)


def by_core(first, second):
    mine = core()
    return first * (1 - mine) + second * mine


def y_source(r):
    return (((r >> 2) & 1) << 7) + ((r >> 3) << 2) + (r & 3)


def x_source(r):
    return ((r >> 7) << 7) + ((r & 7) << 4) + ((r >> 3) & 15)


def place(t):
    line, at = t >> 6, t & 63
    y_place = ((line >> 2) << 8) + ((at >> 1) << 3) + ((at & 1) << 2) + (line & 3)
    x_place = (((at >> 3) & 1) << 8) + (line << 5) + ((at >> 4) << 3) + (at & 7)
    return by_core(y_place, x_place)


def z_line(r):
    return r >> 4


def long_line(r):
    return r >> 6


def onehot(a, b):
    return jnp.where(a == b, 1.0, 0.0).astype(BF)


def pack_body(first, second, feat, cot, out):
    pick = onehot(by_core(first(down(T)), second(down(T))), along(T))
    out[:, :C] = nn(pick, feat[...]).astype(BF)
    out[:, C:] = nn(pick, cot[...]).astype(BF)


def merge_body(mine, took, send):
    send[:, : 2 * C] = mine[...]
    send[:, 2 * C :] = took[...]


def axis_math(line, feat, cot, w_qkv, w_qkv_t, w_out):
    scale = 1.0 / math.sqrt(DEPTH)
    feat_t = nt(onehot(down(T), along(T)), feat).astype(BF)
    proj = nn(feat, w_qkv[...]).astype(BF)
    proj_t = nt(w_qkv_t[...], feat).astype(BF)
    gmix = nt(cot, w_out[...]).astype(BF)
    gmix_t = nt(w_out[...], cot).astype(BF)
    q, k, v = proj[:, :C], proj[:, C : 2 * C], proj[:, 2 * C :]
    q_t, k_t, v_t = proj_t[:C], proj_t[C : 2 * C], proj_t[2 * C :]
    bias = jnp.where(line(down(HALF)) == line(along(QUAD * HALF) & (HALF - 1)), 0.0, NEG)
    head_of_lane = jnp.broadcast_to(along(HALF) >> 5, (HALF, HALF))
    blank = jnp.zeros((HALF, HALF), BF)
    strip = jnp.zeros((DEPTH, HALF), BF)

    def spread(a_t):
        return jnp.concatenate(
            [
                jnp.concatenate(
                    [a_t[i * DEPTH : (i + 1) * DEPTH] if i == j else strip for i in range(QUAD)],
                    axis=0,
                )
                for j in range(QUAD)
            ],
            axis=1,
        )

    def stack(a):
        return jnp.concatenate(
            [jnp.where(head_of_lane == j, a, blank) for j in range(QUAD)], axis=0
        )

    def per_head(a_t, m):
        return jnp.concatenate(
            [
                nn(a_t[j * DEPTH : (j + 1) * DEPTH], m[:, j * HALF : (j + 1) * HALF])
                for j in range(QUAD)
            ],
            axis=0,
        )

    halves = feat.shape[0] // HALF
    blocks = [
        (slice(half * HALF, (half + 1) * HALF), slice(quad * HALF, (quad + 1) * HALF))
        for half in range(halves)
        for quad in range(2)
    ]
    all_scores = [nn(k[t, c], spread(q_t[c, t])) + bias for t, c in blocks]
    all_dprobs = [nn(v[t, c], spread(gmix_t[c, t])) for t, c in blocks]
    soft = []
    for scores, dprobs in zip(all_scores, all_dprobs):
        top = jnp.max(scores, axis=0, keepdims=True)
        e = jnp.exp((scores - top) * scale)
        probs = e * (1.0 / jnp.sum(e, axis=0, keepdims=True))
        mean = jnp.sum(dprobs * probs, axis=0, keepdims=True)
        soft.append((probs.astype(BF), (probs * (dprobs - mean) * scale).astype(BF)))
    parts = []
    for (t, c), (rounded, dround) in zip(blocks, soft):
        out_t = per_head(v_t[c, t], rounded)
        dv = nn(rounded, stack(gmix[t, c]))
        dq_t = per_head(k_t[c, t], dround)
        dk = nn(dround, stack(q[t, c]))
        parts.append([m.astype(BF) for m in (out_t, dq_t, dk, dv)])

    def whole(at, transposed):
        p = [[parts[2 * half + quad][at] for quad in range(2)] for half in range(halves)]
        if transposed:
            p = [list(row) for row in zip(*p)]
        return jnp.concatenate([jnp.concatenate(r, axis=1) for r in p], axis=0)

    out_t, dq_t = whole(0, True), whole(1, True)
    dk, dv = whole(2, False), whole(3, False)
    grads = (nt(feat_t, dq_t), nn(feat_t, dk), nn(feat_t, dv), nn(out_t, cot))
    return (out_t, dq_t, dk, dv), grads


def results(out_t, dq_t, dk, dv, w_qkv):
    dfeat_t = nn(w_qkv[:, :C], dq_t) + nt(w_qkv[:, C : 2 * C], dk) + nt(w_qkv[:, 2 * C :], dv)
    return out_t, dfeat_t.astype(BF)


def z_body(feat, cot, w_qkv, w_qkv_t, w_out, back, grad):
    parts, terms = axis_math(z_line, feat[...], cot[...], w_qkv, w_qkv_t, w_out)
    eye = onehot(down(T), along(T))
    for at, part_t in enumerate(results(*parts, w_qkv)):
        back[:, at * C : (at + 1) * C] = nt(eye, part_t).astype(BF)
    for at, term in enumerate(terms):
        grad[:, at * C : (at + 1) * C] = term.astype(BF)


def lines_body(got, w_qkv, w_qkv_t, w_out, grad_z, out_t, dq_t, dk, dv, keep, give, total):
    sort = onehot(place(down(2 * T)), along(2 * T))
    feat = nn(sort, jnp.concatenate([got[:, :C], got[:, 2 * C : 3 * C]], axis=0)).astype(BF)
    cot = nn(sort, jnp.concatenate([got[:, C : 2 * C], got[:, 3 * C :]], axis=0)).astype(BF)
    held, terms = axis_math(long_line, feat, cot, w_qkv, w_qkv_t, w_out)
    for ref, value in zip((out_t, dq_t, dk, dv), held):
        ref[...] = value
    for at, term in enumerate(terms):
        cols = slice(at * C, (at + 1) * C)
        total[:, cols] = grad_z[:, cols].astype(F32) + term
    mine = core()
    keep[...] = total[pl.ds(pl.multiple_of(mine * 128, 128), 128)]
    give[...] = total[pl.ds(pl.multiple_of((1 - mine) * 128, 128), 128)].astype(BF)


def back_body(out_t, dq_t, dk, dv, w_qkv, back_out, back_feat):
    unsort = onehot(down(2 * T), place(along(2 * T)))
    parts = results(out_t[...], dq_t[...], dk[...], dv[...], w_qkv)
    for part_t, back in zip(parts, (back_out, back_feat)):
        rows = nt(unsort, part_t).astype(BF)
        back[:, :C], back[:, C:] = rows[:T], rows[T:]


def first_pack_body(back_out, keep, took, send):
    send[:, : 2 * C] = back_out[...]
    half = (keep[...] + took[...].astype(F32)).astype(BF)
    send[:128, 2 * C :] = half[:, : 2 * C]
    send[128:, 2 * C :] = half[:, 2 * C :]


def block_body(got, send):
    block = jnp.sum(got[:, 2 * C :].astype(F32).reshape(32, 8, 2 * C), axis=0)
    send[...] = jnp.concatenate([block] * 8, axis=0).astype(BF)


def last_pack_body(factor, got, back_feat, send):
    block = jnp.sum(got[...].astype(F32).reshape(8, 8, 2 * C), axis=0) * factor
    send[:, : 2 * C] = back_feat[...]
    send[:, 2 * C :] = jnp.concatenate([block] * 32, axis=0).astype(BF)


def give_body(got_first, got_last, give):
    give[:, :C] = got_first[:, C : 2 * C]
    give[:, C : 2 * C] = got_last[:, C : 2 * C]
    give[:, 2 * C :] = got_last[:, 2 * C :]


def final_body(back_z, got_first, got_last, took, w_out, update, grad_in, grad_qkv, grad_out):
    r = along(T)
    put_mine = onehot(down(T), by_core(y_source(r), x_source(r)))
    put_theirs = onehot(down(T), by_core(x_source(r), y_source(r)))
    sums = []
    for at, rows in enumerate((got_first[:, :C], got_last[:, :C])):
        cols = slice(at * C, (at + 1) * C)
        sums.append(
            (
                back_z[:, cols].astype(F32) + nn(put_mine, rows) + nn(put_theirs, took[:, cols])
            ).astype(BF)
        )
    update[...] = nn(sums[0], w_out[...]).astype(BF)
    grad_in[...] = sums[1]
    for src, half in ((got_last, core()), (took, 1 - core())):
        rows = pl.ds(pl.multiple_of(half * 128, 128), 128)
        grad_qkv[rows, : 2 * C] = src[:128, 2 * C :].astype(F32)
        grad_qkv[rows, 2 * C :] = src[128:, 2 * C : 3 * C].astype(F32)
        grad_out[rows, :] = src[128:, 3 * C :].astype(F32)


def call(body, outs, flops, *args, scratch=()):
    return pl.pallas_call(
        body,
        out_shape=outs,
        in_specs=[pl.BlockSpec(memory_space=pltpu.VMEM)] * len(args),
        out_specs=[pl.BlockSpec(memory_space=pltpu.VMEM)] * len(outs),
        scratch_shapes=scratch,
        compiler_params=pltpu.CompilerParams(vmem_limit_bytes=40 * 2**20),
        cost_estimate=pl.CostEstimate(flops=flops, bytes_accessed=2**20, transcendentals=2**19),
    )(*args)


def shape(rows, cols, dtype):
    return jax.ShapeDtypeStruct((rows, cols), dtype)


AXES = ("dp", "row", "col")


def device(x, mine, y, z):
    return z % 2 * 256 + (x * 2 + mine) * 32 + y * 4 + z // 2


X, Y, ZS = range(4), range(8), range(8)
LONG = [[device(x, 0, y, z) for z in ZS[dp::2] for y in Y] for x in X for dp in range(2)] + [
    [device(x, 1, y, z) for z in ZS for x in X] for y in Y
]
SHORT = [
    [device(x, 0, y, 2 * z + dp) for x in X for dp in range(2)] for y in Y for z in range(4)
] + [[device(x, 1, y, z) for y in Y] for x in X for z in ZS]


def exchange(rows, groups):
    return lax.all_to_all(
        rows, AXES, split_axis=0, concat_axis=0, axis_index_groups=groups, tiled=True
    )


def swap(rows):
    return lax.ppermute(rows, "row", [(i, i ^ 1) for i in range(8)])


def body(features, w_qkv, w_out, cotangent):
    local_shape = features.shape
    feat = features.reshape(T, C)
    cot = cotangent.reshape(T, C)
    weights = (w_qkv, w_qkv.T, w_out)
    cube = 2 * T * T * C
    pair = shape(T, 2 * C, BF)
    quad = shape(T, 4 * C, BF)
    (give,) = call(
        functools.partial(pack_body, x_source, y_source), [pair], cube * 2, feat, cot
    )
    took = swap(give)
    (mine,) = call(functools.partial(pack_body, y_source, x_source), [pair], cube * 2, feat, cot)
    (send,) = call(merge_body, [quad], 2**20, mine, took)
    got = exchange(send, LONG)
    back_z, grad_z = call(z_body, [pair, shape(C, 4 * C, BF)], cube * 70, feat, cot, *weights)
    *held, keep, give = call(
        lines_body,
        [shape(C, 2 * T, BF)] * 2
        + [shape(2 * T, C, BF)] * 2
        + [shape(128, 4 * C, F32), shape(128, 4 * C, BF)],
        cube * 140,
        got,
        *weights,
        grad_z,
        scratch=[pltpu.VMEM((C, 4 * C), F32)],
    )
    took = swap(give)
    back_out, back_feat = call(back_body, [pair] * 2, cube * 20, *held, w_qkv)
    (send,) = call(first_pack_body, [quad], 2**20, back_out, keep, took)
    got_first = exchange(send, LONG)
    (send,) = call(block_body, [shape(64, 2 * C, BF)], 2**20, got_first)
    blocks = exchange(send, SHORT)
    factor = 1.0 / math.sqrt(PATCHES * 64 * 64 * 16)
    (send,) = call(functools.partial(last_pack_body, factor), [quad], 2**20, blocks, back_feat)
    got_last = exchange(send, LONG)
    (give,) = call(give_body, [quad], 2**20, got_first, got_last)
    update, grad_in, grad_qkv, grad_out = call(
        final_body,
        [shape(T, C, BF)] * 2 + [shape(C, 3 * C, F32), shape(C, C, F32)],
        cube * 6,
        back_z,
        got_first,
        got_last,
        swap(give),
        w_out,
    )
    return (update.reshape(local_shape), grad_in.reshape(local_shape), grad_qkv, grad_out)


def solution(mesh):
    placed = (P("dp", "col", "row", None, None), P(), P(), P("dp", "col", "row", None, None))
    return jax.shard_map(
        body,
        mesh=mesh,
        in_specs=placed,
        out_specs=(P("dp", "col", "row", None, None), P("dp", "col", "row", None, None), P(), P()),
        check_vma=False,
    )
```

```python
import functools
import math

import jax
import jax.numpy as jnp
from jax import lax
from jax.experimental import pallas as pl
from jax.experimental.pallas import tpu as pltpu
from jax.sharding import PartitionSpec as P

HEADS = 8
DEPTH = 32
C = 256
T = 256
PATCHES = 2
Z = 16
HALF = 128
QUAD = 4
NEG = -1e30

BF = jnp.bfloat16
F32 = jnp.float32


def nn(a, b):
    return lax.dot_general(a, b, (((1,), (0,)), ((), ())), preferred_element_type=F32)


def nt(a, b):
    return lax.dot_general(a, b, (((1,), (1,)), ((), ())), preferred_element_type=F32)


def down(n):
    return lax.broadcasted_iota(jnp.int32, (n, 1), 0)


def along(n):
    return lax.broadcasted_iota(jnp.int32, (1, n), 1)


def core():
    return lax.rem(lax.axis_index("row"), 2)


def by_core(first, second):
    mine = core()
    return first * (1 - mine) + second * mine


def y_source(r):
    return (((r >> 2) & 1) << 7) + ((r >> 3) << 2) + (r & 3)


def x_source(r):
    return ((r >> 7) << 7) + ((r & 7) << 4) + ((r >> 3) & 15)


def place(t):
    line, at = t >> 6, t & 63
    y_place = ((line >> 2) << 8) + ((at >> 1) << 3) + ((at & 1) << 2) + (line & 3)
    x_place = (((at >> 3) & 1) << 8) + ((at >> 4) << 6) + (line << 3) + (at & 7)
    return by_core(y_place, x_place)


def z_line(r):
    return r >> 4


def long_line(r):
    return r >> 6


def onehot(a, b):
    return jnp.where(a == b, 1.0, 0.0).astype(BF)


def pack_body(first, second, feat, cot, out):
    pick = onehot(by_core(first(down(T)), second(down(T))), along(T))
    out[:, :C] = nn(pick, feat[...]).astype(BF)
    out[:, C:] = nn(pick, cot[...]).astype(BF)


def merge_body(mine, took, send):
    send[:, : 2 * C] = mine[...]
    send[:, 2 * C :] = took[...]


def axis_math(line, feat, cot, w_qkv, w_qkv_t, w_out):
    scale = 1.0 / math.sqrt(DEPTH)
    feat_t = nt(onehot(down(T), along(T)), feat).astype(BF)
    proj = nn(feat, w_qkv[...]).astype(BF)
    proj_t = nt(w_qkv_t[...], feat).astype(BF)
    gmix = nt(cot, w_out[...]).astype(BF)
    gmix_t = nt(w_out[...], cot).astype(BF)
    q, k, v = proj[:, :C], proj[:, C : 2 * C], proj[:, 2 * C :]
    q_t, k_t, v_t = proj_t[:C], proj_t[C : 2 * C], proj_t[2 * C :]
    bias = jnp.where(line(down(HALF)) == line(along(QUAD * HALF) & (HALF - 1)), 0.0, NEG)
    head_of_lane = jnp.broadcast_to(along(HALF) >> 5, (HALF, HALF))
    blank = jnp.zeros((HALF, HALF), BF)
    strip = jnp.zeros((DEPTH, HALF), BF)

    def spread(a_t):
        return jnp.concatenate(
            [
                jnp.concatenate(
                    [a_t[i * DEPTH : (i + 1) * DEPTH] if i == j else strip for i in range(QUAD)],
                    axis=0,
                )
                for j in range(QUAD)
            ],
            axis=1,
        )

    def stack(a):
        return jnp.concatenate(
            [jnp.where(head_of_lane == j, a, blank) for j in range(QUAD)], axis=0
        )

    def per_head(a_t, m):
        return jnp.concatenate(
            [
                nn(a_t[j * DEPTH : (j + 1) * DEPTH], m[:, j * HALF : (j + 1) * HALF])
                for j in range(QUAD)
            ],
            axis=0,
        )

    halves = feat.shape[0] // HALF
    blocks = [
        (slice(half * HALF, (half + 1) * HALF), slice(quad * HALF, (quad + 1) * HALF))
        for half in range(halves)
        for quad in range(2)
    ]
    all_scores = [nn(k[t, c], spread(q_t[c, t])) + bias for t, c in blocks]
    all_dprobs = [nn(v[t, c], spread(gmix_t[c, t])) for t, c in blocks]
    soft = []
    for scores, dprobs in zip(all_scores, all_dprobs):
        top = jnp.max(scores, axis=0, keepdims=True)
        e = jnp.exp((scores - top) * scale)
        probs = e * (1.0 / jnp.sum(e, axis=0, keepdims=True))
        mean = jnp.sum(dprobs * probs, axis=0, keepdims=True)
        soft.append((probs.astype(BF), (probs * (dprobs - mean) * scale).astype(BF)))
    parts = []
    for (t, c), (rounded, dround) in zip(blocks, soft):
        out_t = per_head(v_t[c, t], rounded)
        dv = nn(rounded, stack(gmix[t, c]))
        dq_t = per_head(k_t[c, t], dround)
        dk = nn(dround, stack(q[t, c]))
        parts.append([m.astype(BF) for m in (out_t, dq_t, dk, dv)])

    def whole(at, transposed):
        p = [[parts[2 * half + quad][at] for quad in range(2)] for half in range(halves)]
        if transposed:
            p = [list(row) for row in zip(*p)]
        return jnp.concatenate([jnp.concatenate(r, axis=1) for r in p], axis=0)

    out_t, dq_t = whole(0, True), whole(1, True)
    dk, dv = whole(2, False), whole(3, False)
    return out_t, dq_t, dk, dv, feat_t


def gradients(feat_t, out_t, dq_t, dk, dv, cot):
    return nt(feat_t, dq_t), nn(feat_t, dk), nn(feat_t, dv), nn(out_t, cot)


def results(out_t, dq_t, dk, dv, w_qkv):
    dfeat_t = nn(w_qkv[:, :C], dq_t) + nt(w_qkv[:, C : 2 * C], dk) + nt(w_qkv[:, 2 * C :], dv)
    return out_t, dfeat_t.astype(BF)


def z_body(feat, cot, w_qkv, w_qkv_t, w_out, back, grad):
    *parts, feat_t = axis_math(z_line, feat[...], cot[...], w_qkv, w_qkv_t, w_out)
    eye = onehot(down(T), along(T))
    for at, part_t in enumerate(results(*parts, w_qkv)):
        back[:, at * C : (at + 1) * C] = nt(eye, part_t).astype(BF)
    for at, term in enumerate(gradients(feat_t, *parts, cot[...])):
        grad[:, at * C : (at + 1) * C] = term.astype(BF)


def half_gradient(half, grad_z, feat_t, out_t, dq_t, dk, dv, cot, grad):
    rows = pl.ds(pl.multiple_of(half * 128, 128), 128)
    terms = gradients(feat_t[rows, :], out_t[rows, :], dq_t[...], dk[...], dv[...], cot[...])
    for at, term in enumerate(terms):
        cols = slice(at * C, (at + 1) * C)
        grad[:, cols] = (grad_z[rows, cols].astype(F32) + term).astype(grad.dtype)


def lines_body(
    got, w_qkv, w_qkv_t, w_out, grad_z, feat_t, out_t, dq_t, dk, dv, cot, give
):
    sort = onehot(place(down(2 * T)), along(2 * T))
    feat = nn(sort, jnp.concatenate([got[:, :C], got[:, 2 * C : 3 * C]], axis=0)).astype(BF)
    cot[...] = nn(sort, jnp.concatenate([got[:, C : 2 * C], got[:, 3 * C :]], axis=0)).astype(BF)
    held = axis_math(long_line, feat, cot[...], w_qkv, w_qkv_t, w_out)
    for ref, value in zip((out_t, dq_t, dk, dv, feat_t), held):
        ref[...] = value
    half_gradient(1 - core(), grad_z, feat_t, out_t, dq_t, dk, dv, cot, give)


def back_body(grad_z, feat_t, out_t, dq_t, dk, dv, cot, w_qkv, back_out, back_feat, keep):
    unsort = onehot(down(2 * T), place(along(2 * T)))
    parts = results(out_t[...], dq_t[...], dk[...], dv[...], w_qkv)
    for part_t, back in zip(parts, (back_out, back_feat)):
        rows = nt(unsort, part_t).astype(BF)
        back[:, :C], back[:, C:] = rows[:T], rows[T:]
    half_gradient(core(), grad_z, feat_t, out_t, dq_t, dk, dv, cot, keep)


def first_pack_body(back_out, keep, took, send):
    send[:, : 2 * C] = back_out[...]
    half = (keep[...] + took[...].astype(F32)).astype(BF)
    send[:128, 2 * C :] = half[:, : 2 * C]
    send[128:, 2 * C :] = half[:, 2 * C :]


def block_body(got, send):
    block = jnp.sum(got[:, 2 * C :].astype(F32).reshape(32, 8, 2 * C), axis=0)
    send[...] = jnp.concatenate([block] * 8, axis=0).astype(BF)


def last_pack_body(factor, got, back_feat, send):
    block = jnp.sum(got[...].astype(F32).reshape(8, 8, 2 * C), axis=0) * factor
    send[:, : 2 * C] = back_feat[...]
    send[:, 2 * C :] = jnp.concatenate([block] * 32, axis=0).astype(BF)


def give_body(got_first, got_last, give):
    give[:, :C] = got_first[:, C : 2 * C]
    give[:, C : 2 * C] = got_last[:, C : 2 * C]
    give[:, 2 * C :] = got_last[:, 2 * C :]


def final_body(back_z, got_first, got_last, took, w_out, update, grad_in, grad_qkv, grad_out):
    r = along(T)
    put_mine = onehot(down(T), by_core(y_source(r), x_source(r)))
    put_theirs = onehot(down(T), by_core(x_source(r), y_source(r)))
    sums = []
    for at, rows in enumerate((got_first[:, :C], got_last[:, :C])):
        cols = slice(at * C, (at + 1) * C)
        sums.append(
            (
                back_z[:, cols].astype(F32) + nn(put_mine, rows) + nn(put_theirs, took[:, cols])
            ).astype(BF)
        )
    update[...] = nn(sums[0], w_out[...]).astype(BF)
    grad_in[...] = sums[1]
    for src, half in ((got_last, core()), (took, 1 - core())):
        rows = pl.ds(pl.multiple_of(half * 128, 128), 128)
        grad_qkv[rows, : 2 * C] = src[:128, 2 * C :].astype(F32)
        grad_qkv[rows, 2 * C :] = src[128:, 2 * C : 3 * C].astype(F32)
        grad_out[rows, :] = src[128:, 3 * C :].astype(F32)


def call(body, outs, flops, *args, scratch=()):
    return pl.pallas_call(
        body,
        out_shape=outs,
        in_specs=[pl.BlockSpec(memory_space=pltpu.VMEM)] * len(args),
        out_specs=[pl.BlockSpec(memory_space=pltpu.VMEM)] * len(outs),
        scratch_shapes=scratch,
        compiler_params=pltpu.CompilerParams(vmem_limit_bytes=40 * 2**20),
        cost_estimate=pl.CostEstimate(flops=flops, bytes_accessed=2**20, transcendentals=2**19),
    )(*args)


def shape(rows, cols, dtype):
    return jax.ShapeDtypeStruct((rows, cols), dtype)


AXES = ("dp", "row", "col")


def device(x, mine, y, z):
    return z % 2 * 256 + (x * 2 + mine) * 32 + y * 4 + z // 2


X, Y, ZS = range(4), range(8), range(8)
LONG = [[device(x, 0, y, z) for y in Y for z in ZS[dp::2]] for x in X for dp in range(2)] + [
    [device(x, 1, y, z) for x in X for z in ZS] for y in Y
]
SHORT = [
    [device(x, 0, y, 2 * z + dp) for x in X for dp in range(2)] for y in Y for z in range(4)
] + [[device(x, 1, y, z) for y in Y] for x in X for z in ZS]


def exchange(rows, groups):
    return lax.all_to_all(
        rows, AXES, split_axis=0, concat_axis=0, axis_index_groups=groups, tiled=True
    )


def swap(rows):
    return lax.ppermute(rows, "row", [(i, i ^ 1) for i in range(8)])


def body(features, w_qkv, w_out, cotangent):
    local_shape = features.shape
    feat = features.reshape(T, C)
    cot = cotangent.reshape(T, C)
    weights = (w_qkv, w_qkv.T, w_out)
    cube = 2 * T * T * C
    pair = shape(T, 2 * C, BF)
    quad = shape(T, 4 * C, BF)
    (give,) = call(
        functools.partial(pack_body, x_source, y_source), [pair], cube * 2, feat, cot
    )
    took = swap(give)
    (mine,) = call(functools.partial(pack_body, y_source, x_source), [pair], cube * 2, feat, cot)
    (send,) = call(merge_body, [quad], 2**20, mine, took)
    got = exchange(send, LONG)
    back_z, grad_z = call(z_body, [pair, shape(C, 4 * C, BF)], cube * 70, feat, cot, *weights)
    *held, give = call(
        lines_body,
        [shape(C, 2 * T, BF)] * 3 + [shape(2 * T, C, BF)] * 3 + [shape(128, 4 * C, BF)],
        cube * 140,
        got,
        *weights,
        grad_z,
    )
    took = swap(give)
    back_out, back_feat, keep = call(
        back_body, [pair, pair, shape(128, 4 * C, F32)], cube * 20, grad_z, *held, w_qkv
    )
    (send,) = call(first_pack_body, [quad], 2**20, back_out, keep, took)
    got_first = exchange(send, LONG)
    (send,) = call(block_body, [shape(64, 2 * C, BF)], 2**20, got_first)
    blocks = exchange(send, SHORT)
    factor = 1.0 / math.sqrt(PATCHES * 64 * 64 * 16)
    (send,) = call(functools.partial(last_pack_body, factor), [quad], 2**20, blocks, back_feat)
    got_last = exchange(send, LONG)
    (give,) = call(give_body, [quad], 2**20, got_first, got_last)
    update, grad_in, grad_qkv, grad_out = call(
        final_body,
        [shape(T, C, BF)] * 2 + [shape(C, 3 * C, F32), shape(C, C, F32)],
        cube * 6,
        back_z,
        got_first,
        got_last,
        swap(give),
        w_out,
    )
    return (update.reshape(local_shape), grad_in.reshape(local_shape), grad_qkv, grad_out)


def solution(mesh):
    placed = (P("dp", "col", "row", None, None), P(), P(), P("dp", "col", "row", None, None))
    return jax.shard_map(
        body,
        mesh=mesh,
        in_specs=placed,
        out_specs=(P("dp", "col", "row", None, None), P("dp", "col", "row", None, None), P(), P()),
        check_vma=False,
    )
```

```python
import functools
import math

import jax
import jax.numpy as jnp
from jax import lax
from jax.experimental import pallas as pl
from jax.experimental.pallas import tpu as pltpu
from jax.sharding import PartitionSpec as P

HEADS = 8
DEPTH = 32
C = 256
T = 256
PATCHES = 2
Z = 16
HALF = 128
QUAD = 4
NEG = -1e30

BF = jnp.bfloat16
F32 = jnp.float32


def nn(a, b):
    return lax.dot_general(a, b, (((1,), (0,)), ((), ())), preferred_element_type=F32)


def nt(a, b):
    return lax.dot_general(a, b, (((1,), (1,)), ((), ())), preferred_element_type=F32)


def down(n):
    return lax.broadcasted_iota(jnp.int32, (n, 1), 0)


def along(n):
    return lax.broadcasted_iota(jnp.int32, (1, n), 1)


def core():
    return lax.rem(lax.axis_index("row"), 2)


def by_core(first, second):
    mine = core()
    return first * (1 - mine) + second * mine


def y_source(r):
    return (((r >> 2) & 1) << 7) + ((r >> 3) << 2) + (r & 3)


def x_source(r):
    return ((r >> 7) << 7) + ((r & 7) << 4) + ((r >> 3) & 15)


def place(t):
    line, at = t >> 6, t & 63
    y_place = ((line >> 2) << 8) + ((at >> 1) << 3) + ((at & 1) << 2) + (line & 3)
    x_place = (((at >> 3) & 1) << 8) + ((at >> 4) << 6) + (line << 3) + (at & 7)
    return by_core(y_place, x_place)


def z_line(r):
    return r >> 4


def long_line(r):
    return r >> 6


def onehot(a, b):
    return jnp.where(a == b, 1.0, 0.0).astype(BF)


def pack_body(first, second, feat, cot, out):
    pick = onehot(by_core(first(down(T)), second(down(T))), along(T))
    out[:, :C] = nn(pick, feat[...]).astype(BF)
    out[:, C:] = nn(pick, cot[...]).astype(BF)


def merge_body(mine, took, send):
    send[:, : 2 * C] = mine[...]
    send[:, 2 * C :] = took[...]


def axis_math(line, feat, cot, w_qkv, w_out):
    scale = 1.0 / math.sqrt(DEPTH)
    feat_t = feat.T
    proj = nn(feat, w_qkv[...]).astype(BF)
    proj_t = proj.T
    gmix = nt(cot, w_out[...]).astype(BF)
    gmix_t = gmix.T
    q, k, v = proj[:, :C], proj[:, C : 2 * C], proj[:, 2 * C :]
    q_t, k_t, v_t = proj_t[:C], proj_t[C : 2 * C], proj_t[2 * C :]
    bias = jnp.where(line(down(HALF)) == line(along(QUAD * HALF) & (HALF - 1)), 0.0, NEG)
    head_of_lane = jnp.broadcast_to(along(HALF) >> 5, (HALF, HALF))
    blank = jnp.zeros((HALF, HALF), BF)
    strip = jnp.zeros((DEPTH, HALF), BF)

    def spread(a_t):
        return jnp.concatenate(
            [
                jnp.concatenate(
                    [a_t[i * DEPTH : (i + 1) * DEPTH] if i == j else strip for i in range(QUAD)],
                    axis=0,
                )
                for j in range(QUAD)
            ],
            axis=1,
        )

    def stack(a):
        return jnp.concatenate(
            [jnp.where(head_of_lane == j, a, blank) for j in range(QUAD)], axis=0
        )

    def per_head(a_t, m):
        return jnp.concatenate(
            [
                nn(a_t[j * DEPTH : (j + 1) * DEPTH], m[:, j * HALF : (j + 1) * HALF])
                for j in range(QUAD)
            ],
            axis=0,
        )

    halves = feat.shape[0] // HALF
    blocks = [
        (slice(half * HALF, (half + 1) * HALF), slice(quad * HALF, (quad + 1) * HALF))
        for half in range(halves)
        for quad in range(2)
    ]
    def softmax(scores, dprobs):
        top = jnp.max(scores, axis=0, keepdims=True)
        e = jnp.exp((scores - top) * scale)
        probs = e * (1.0 / jnp.sum(e, axis=0, keepdims=True))
        mean = jnp.sum(dprobs * probs, axis=0, keepdims=True)
        return probs.astype(BF), (probs * (dprobs - mean) * scale).astype(BF)

    def score(block):
        t, c = block
        scores = nn(k[t, c], spread(q_t[c, t])) + bias
        return scores, nn(v[t, c], spread(gmix_t[c, t]))

    def products(block, rounded, dround):
        t, c = block
        out_t = per_head(v_t[c, t], rounded)
        dv = nn(rounded, stack(gmix[t, c]))
        dq_t = per_head(k_t[c, t], dround)
        dk = nn(dround, stack(q[t, c]))
        return [m.astype(BF) for m in (out_t, dq_t, dk, dv)]

    parts = []
    scored, soft = [score(blocks[0])], []
    for at in range(len(blocks) + 1):
        if at + 1 < len(blocks):
            scored.append(score(blocks[at + 1]))
        if at < len(blocks):
            soft.append(softmax(*scored[at]))
        if at:
            parts.append(products(blocks[at - 1], *soft[at - 1]))

    def whole(at, transposed):
        p = [[parts[2 * half + quad][at] for quad in range(2)] for half in range(halves)]
        if transposed:
            p = [list(row) for row in zip(*p)]
        return jnp.concatenate([jnp.concatenate(r, axis=1) for r in p], axis=0)

    out_t, dq_t = whole(0, True), whole(1, True)
    dk, dv = whole(2, False), whole(3, False)
    grads = (nt(feat_t, dq_t), nn(feat_t, dk), nn(feat_t, dv), nn(out_t, cot))
    return (out_t, dq_t, dk, dv), grads


def results(out_t, dq_t, dk, dv, w_qkv):
    dfeat_t = nn(w_qkv[:, :C], dq_t) + nt(w_qkv[:, C : 2 * C], dk) + nt(w_qkv[:, 2 * C :], dv)
    return out_t, dfeat_t.astype(BF)


def z_body(feat, cot, w_qkv, w_out, back, grad):
    parts, terms = axis_math(z_line, feat[...], cot[...], w_qkv, w_out)
    eye = onehot(down(T), along(T))
    for at, part_t in enumerate(results(*parts, w_qkv)):
        back[:, at * C : (at + 1) * C] = nt(eye, part_t).astype(BF)
    for at, term in enumerate(terms):
        grad[:, at * C : (at + 1) * C] = term.astype(BF)


def lines_body(got, w_qkv, w_out, grad_z, out_t, dq_t, dk, dv, keep, give, total):
    sort = onehot(place(down(2 * T)), along(2 * T))
    feat = nn(sort, jnp.concatenate([got[:, :C], got[:, 2 * C : 3 * C]], axis=0)).astype(BF)
    cot = nn(sort, jnp.concatenate([got[:, C : 2 * C], got[:, 3 * C :]], axis=0)).astype(BF)
    held, terms = axis_math(long_line, feat, cot, w_qkv, w_out)
    for ref, value in zip((out_t, dq_t, dk, dv), held):
        ref[...] = value
    for at, term in enumerate(terms):
        cols = slice(at * C, (at + 1) * C)
        total[:, cols] = grad_z[:, cols].astype(F32) + term
    mine = core()
    keep[...] = total[pl.ds(pl.multiple_of(mine * 128, 128), 128)]
    give[...] = total[pl.ds(pl.multiple_of((1 - mine) * 128, 128), 128)].astype(BF)


def back_body(out_t, dq_t, dk, dv, w_qkv, back_out, back_feat):
    unsort = onehot(down(2 * T), place(along(2 * T)))
    parts = results(out_t[...], dq_t[...], dk[...], dv[...], w_qkv)
    for part_t, back in zip(parts, (back_out, back_feat)):
        rows = nt(unsort, part_t).astype(BF)
        back[:, :C], back[:, C:] = rows[:T], rows[T:]


def first_pack_body(back_out, keep, took, send):
    send[:, : 2 * C] = back_out[...]
    half = (keep[...] + took[...].astype(F32)).astype(BF)
    send[:128, 2 * C :] = half[:, : 2 * C]
    send[128:, 2 * C :] = half[:, 2 * C :]


def block_body(got, send):
    block = jnp.sum(got[:, 2 * C :].astype(F32).reshape(32, 8, 2 * C), axis=0)
    send[...] = jnp.concatenate([block] * 8, axis=0).astype(BF)


def last_pack_body(factor, got, back_feat, send):
    block = jnp.sum(got[...].astype(F32).reshape(8, 8, 2 * C), axis=0) * factor
    send[:, : 2 * C] = back_feat[...]
    send[:, 2 * C :] = jnp.concatenate([block] * 32, axis=0).astype(BF)


def give_body(got_first, got_last, give):
    give[:, :C] = got_first[:, C : 2 * C]
    give[:, C : 2 * C] = got_last[:, C : 2 * C]
    give[:, 2 * C :] = got_last[:, 2 * C :]


def final_body(back_z, got_first, got_last, took, w_out, update, grad_in, grad_qkv, grad_out):
    r = along(T)
    put_mine = onehot(down(T), by_core(y_source(r), x_source(r)))
    put_theirs = onehot(down(T), by_core(x_source(r), y_source(r)))
    sums = []
    for at, rows in enumerate((got_first[:, :C], got_last[:, :C])):
        cols = slice(at * C, (at + 1) * C)
        sums.append(
            (
                back_z[:, cols].astype(F32) + nn(put_mine, rows) + nn(put_theirs, took[:, cols])
            ).astype(BF)
        )
    update[...] = nn(sums[0], w_out[...]).astype(BF)
    grad_in[...] = sums[1]
    for src, half in ((got_last, core()), (took, 1 - core())):
        rows = pl.ds(pl.multiple_of(half * 128, 128), 128)
        grad_qkv[rows, : 2 * C] = src[:128, 2 * C :].astype(F32)
        grad_qkv[rows, 2 * C :] = src[128:, 2 * C : 3 * C].astype(F32)
        grad_out[rows, :] = src[128:, 3 * C :].astype(F32)


def call(body, outs, flops, *args, scratch=()):
    return pl.pallas_call(
        body,
        out_shape=outs,
        in_specs=[pl.BlockSpec(memory_space=pltpu.VMEM)] * len(args),
        out_specs=[pl.BlockSpec(memory_space=pltpu.VMEM)] * len(outs),
        scratch_shapes=scratch,
        compiler_params=pltpu.CompilerParams(vmem_limit_bytes=40 * 2**20),
        cost_estimate=pl.CostEstimate(flops=flops, bytes_accessed=2**20, transcendentals=2**19),
    )(*args)


def shape(rows, cols, dtype):
    return jax.ShapeDtypeStruct((rows, cols), dtype)


AXES = ("dp", "row", "col")


def device(x, mine, y, z):
    return z % 2 * 256 + (x * 2 + mine) * 32 + y * 4 + z // 2


X, Y, ZS = range(4), range(8), range(8)
LONG = [[device(x, 0, y, z) for y in Y for z in ZS[dp::2]] for x in X for dp in range(2)] + [
    [device(x, 1, y, z) for x in X for z in ZS] for y in Y
]
SHORT = [
    [device(x, 0, y, 2 * z + dp) for x in X for dp in range(2)] for y in Y for z in range(4)
] + [[device(x, 1, y, z) for y in Y] for x in X for z in ZS]


def exchange(rows, groups):
    return lax.all_to_all(
        rows, AXES, split_axis=0, concat_axis=0, axis_index_groups=groups, tiled=True
    )


def swap(rows):
    return lax.ppermute(rows, "row", [(i, i ^ 1) for i in range(8)])


def body(features, w_qkv, w_out, cotangent):
    local_shape = features.shape
    feat = features.reshape(T, C)
    cot = cotangent.reshape(T, C)
    weights = (w_qkv, w_out)
    cube = 2 * T * T * C
    pair = shape(T, 2 * C, BF)
    quad = shape(T, 4 * C, BF)
    (give,) = call(
        functools.partial(pack_body, x_source, y_source), [pair], cube * 2, feat, cot
    )
    took = swap(give)
    (mine,) = call(functools.partial(pack_body, y_source, x_source), [pair], cube * 2, feat, cot)
    (send,) = call(merge_body, [quad], 2**20, mine, took)
    got = exchange(send, LONG)
    back_z, grad_z = call(z_body, [pair, shape(C, 4 * C, BF)], cube * 70, feat, cot, *weights)
    *held, keep, give = call(
        lines_body,
        [shape(C, 2 * T, BF)] * 2
        + [shape(2 * T, C, BF)] * 2
        + [shape(128, 4 * C, F32), shape(128, 4 * C, BF)],
        cube * 140,
        got,
        *weights,
        grad_z,
        scratch=[pltpu.VMEM((C, 4 * C), F32)],
    )
    took = swap(give)
    back_out, back_feat = call(back_body, [pair] * 2, cube * 20, *held, w_qkv)
    (send,) = call(first_pack_body, [quad], 2**20, back_out, keep, took)
    got_first = exchange(send, LONG)
    (send,) = call(block_body, [shape(64, 2 * C, BF)], 2**20, got_first)
    blocks = exchange(send, SHORT)
    factor = 1.0 / math.sqrt(PATCHES * 64 * 64 * 16)
    (send,) = call(functools.partial(last_pack_body, factor), [quad], 2**20, blocks, back_feat)
    got_last = exchange(send, LONG)
    (give,) = call(give_body, [quad], 2**20, got_first, got_last)
    update, grad_in, grad_qkv, grad_out = call(
        final_body,
        [shape(T, C, BF)] * 2 + [shape(C, 3 * C, F32), shape(C, C, F32)],
        cube * 6,
        back_z,
        got_first,
        got_last,
        swap(give),
        w_out,
    )
    return (update.reshape(local_shape), grad_in.reshape(local_shape), grad_qkv, grad_out)


def solution(mesh):
    placed = (P("dp", "col", "row", None, None), P(), P(), P("dp", "col", "row", None, None))
    return jax.shard_map(
        body,
        mesh=mesh,
        in_specs=placed,
        out_specs=(P("dp", "col", "row", None, None), P("dp", "col", "row", None, None), P(), P()),
        check_vma=False,
    )
```

```python
import functools
import math

import jax
import jax.numpy as jnp
from jax import lax
from jax.experimental import pallas as pl
from jax.experimental.pallas import tpu as pltpu
from jax.sharding import PartitionSpec as P

HEADS = 8
DEPTH = 32
C = 256
T = 256
PATCHES = 2
Z = 16
HALF = 128
QUAD = 4
NEG = -1e30

BF = jnp.bfloat16
F32 = jnp.float32


def nn(a, b):
    return lax.dot_general(a, b, (((1,), (0,)), ((), ())), preferred_element_type=F32)


def nt(a, b):
    return lax.dot_general(a, b, (((1,), (1,)), ((), ())), preferred_element_type=F32)


def down(n):
    return lax.broadcasted_iota(jnp.int32, (n, 1), 0)


def along(n):
    return lax.broadcasted_iota(jnp.int32, (1, n), 1)


def core():
    return lax.rem(lax.axis_index("row"), 2)


def by_core(first, second):
    mine = core()
    return first * (1 - mine) + second * mine


def y_source(r):
    return (((r >> 2) & 1) << 7) + ((r >> 3) << 2) + (r & 3)


def x_source(r):
    return ((r >> 7) << 7) + ((r & 7) << 4) + ((r >> 3) & 15)


def place(t):
    line, at = t >> 6, t & 63
    y_place = ((line >> 2) << 8) + ((at >> 1) << 3) + ((at & 1) << 2) + (line & 3)
    x_place = (((at >> 3) & 1) << 8) + ((at >> 4) << 6) + (line << 3) + (at & 7)
    return by_core(y_place, x_place)


def z_line(r):
    return r >> 4


def long_line(r):
    return r >> 6


def onehot(a, b):
    return jnp.where(a == b, 1.0, 0.0).astype(BF)


def pack_body(first, second, feat, cot, out):
    pick = onehot(by_core(first(down(T)), second(down(T))), along(T))
    out[:, :C] = nn(pick, feat[...]).astype(BF)
    out[:, C:] = nn(pick, cot[...]).astype(BF)


def merge_body(mine, took, send):
    send[:, : 2 * C] = mine[...]
    send[:, 2 * C :] = took[...]


def axis_math(line, feat, cot, w_qkv, w_out):
    scale = 1.0 / math.sqrt(DEPTH)
    feat_t = feat.T
    proj = nn(feat, w_qkv[...]).astype(BF)
    proj_t = proj.T
    gmix = nt(cot, w_out[...]).astype(BF)
    gmix_t = gmix.T
    q, k, v = proj[:, :C], proj[:, C : 2 * C], proj[:, 2 * C :]
    q_t, k_t, v_t = proj_t[:C], proj_t[C : 2 * C], proj_t[2 * C :]
    bias = jnp.where(line(down(HALF)) == line(along(QUAD * HALF) & (HALF - 1)), 0.0, NEG)
    head_of_lane = jnp.broadcast_to(along(HALF) >> 5, (HALF, HALF))
    blank = jnp.zeros((HALF, HALF), BF)
    strip = jnp.zeros((DEPTH, HALF), BF)

    def spread(a_t):
        return jnp.concatenate(
            [
                jnp.concatenate(
                    [a_t[i * DEPTH : (i + 1) * DEPTH] if i == j else strip for i in range(QUAD)],
                    axis=0,
                )
                for j in range(QUAD)
            ],
            axis=1,
        )

    def stack(a):
        return jnp.concatenate(
            [jnp.where(head_of_lane == j, a, blank) for j in range(QUAD)], axis=0
        )

    def per_head(a_t, m):
        return jnp.concatenate(
            [
                nn(a_t[j * DEPTH : (j + 1) * DEPTH], m[:, j * HALF : (j + 1) * HALF])
                for j in range(QUAD)
            ],
            axis=0,
        )

    halves = feat.shape[0] // HALF
    blocks = [
        (slice(half * HALF, (half + 1) * HALF), slice(quad * HALF, (quad + 1) * HALF))
        for half in range(halves)
        for quad in range(2)
    ]
    def softmax(scores, dprobs):
        top = jnp.max(scores, axis=0, keepdims=True)
        e = jnp.exp((scores - top) * scale)
        probs = e * (1.0 / jnp.sum(e, axis=0, keepdims=True))
        mean = jnp.sum(dprobs * probs, axis=0, keepdims=True)
        return probs.astype(BF), (probs * (dprobs - mean) * scale).astype(BF)

    def score(block):
        t, c = block
        scores = nn(k[t, c], spread(q_t[c, t])) + bias
        return scores, nn(v[t, c], spread(gmix_t[c, t]))

    def products(block, rounded, dround):
        t, c = block
        out_t = per_head(v_t[c, t], rounded)
        dv = nn(rounded, stack(gmix[t, c]))
        dq_t = per_head(k_t[c, t], dround)
        dk = nn(dround, stack(q[t, c]))
        return [m.astype(BF) for m in (out_t, dq_t, dk, dv)]

    parts = []
    scored, soft = [score(blocks[0])], []
    for at in range(len(blocks) + 1):
        if at + 1 < len(blocks):
            scored.append(score(blocks[at + 1]))
        if at < len(blocks):
            soft.append(softmax(*scored[at]))
        if at:
            parts.append(products(blocks[at - 1], *soft[at - 1]))

    def whole(at, transposed):
        p = [[parts[2 * half + quad][at] for quad in range(2)] for half in range(halves)]
        if transposed:
            p = [list(row) for row in zip(*p)]
        return jnp.concatenate([jnp.concatenate(r, axis=1) for r in p], axis=0)

    out_t, dq_t = whole(0, True), whole(1, True)
    dk, dv = whole(2, False), whole(3, False)
    grads = (nt(feat_t, dq_t), nn(feat_t, dk), nn(feat_t, dv), nn(out_t, cot))
    return (out_t, dq_t, dk, dv), grads


def results(out_t, dq_t, dk, dv, w_qkv):
    dfeat_t = nn(w_qkv[:, :C], dq_t) + nt(w_qkv[:, C : 2 * C], dk) + nt(w_qkv[:, 2 * C :], dv)
    return out_t, dfeat_t.astype(BF)


def z_body(feat, cot, w_qkv, w_out, back, grad):
    parts, terms = axis_math(z_line, feat[...], cot[...], w_qkv, w_out)
    eye = onehot(down(T), along(T))
    for at, part_t in enumerate(results(*parts, w_qkv)):
        back[:, at * C : (at + 1) * C] = nt(eye, part_t).astype(BF)
    for at, term in enumerate(terms):
        grad[:, at * C : (at + 1) * C] = term.astype(BF)


def lines_body(got, w_qkv, w_out, grad_z, out_t, dq_t, dk, dv, keep, give, total):
    sort = onehot(place(down(2 * T)), along(2 * T))
    feat = nn(sort, jnp.concatenate([got[:, :C], got[:, 2 * C : 3 * C]], axis=0)).astype(BF)
    cot = nn(sort, jnp.concatenate([got[:, C : 2 * C], got[:, 3 * C :]], axis=0)).astype(BF)
    held, terms = axis_math(long_line, feat, cot, w_qkv, w_out)
    for ref, value in zip((out_t, dq_t, dk, dv), held):
        ref[...] = value
    for at, term in enumerate(terms):
        cols = slice(at * C, (at + 1) * C)
        total[:, cols] = grad_z[:, cols].astype(F32) + term
    mine = core()
    keep[...] = total[pl.ds(pl.multiple_of(mine * 128, 128), 128)]
    give[...] = total[pl.ds(pl.multiple_of((1 - mine) * 128, 128), 128)].astype(BF)


def back_body(out_t, dq_t, dk, dv, w_qkv, back_out, back_feat):
    unsort = onehot(down(2 * T), place(along(2 * T)))
    parts = results(out_t[...], dq_t[...], dk[...], dv[...], w_qkv)
    for part_t, back in zip(parts, (back_out, back_feat)):
        rows = nt(unsort, part_t).astype(BF)
        back[:, :C], back[:, C:] = rows[:T], rows[T:]


def first_pack_body(back_out, keep, took, send):
    send[:, : 2 * C] = back_out[...]
    half = (keep[...] + took[...].astype(F32)).astype(BF)
    send[:128, 2 * C :] = half[:, : 2 * C]
    send[128:, 2 * C :] = half[:, 2 * C :]


def block_body(got, send):
    block = jnp.sum(got[:, 2 * C :].astype(F32).reshape(32, 8, 2 * C), axis=0)
    send[...] = jnp.concatenate([block] * 8, axis=0).astype(BF)


def last_pack_body(factor, got, back_feat, send):
    block = jnp.sum(got[...].astype(F32).reshape(8, 8, 2 * C), axis=0) * factor
    send[:, : 2 * C] = back_feat[...]
    send[:, 2 * C :] = jnp.concatenate([block] * 32, axis=0).astype(BF)


def give_body(got_first, got_last, give):
    give[:, :C] = got_first[:, C : 2 * C]
    give[:, C : 2 * C] = got_last[:, C : 2 * C]
    give[:, 2 * C :] = got_last[:, 2 * C :]


def own_sum_body(back_z, got_first, got_last, part):
    put = onehot(down(T), by_core(y_source(along(T)), x_source(along(T))))
    for at, got in enumerate((got_first, got_last)):
        cols = slice(at * C, (at + 1) * C)
        part[:, cols] = back_z[:, cols].astype(F32) + nn(put, got[:, :C])


def final_body(part, got_last, took, w_out, update, grad_in, grad_qkv, grad_out):
    put = onehot(down(T), by_core(x_source(along(T)), y_source(along(T))))
    sums = (part[...] + nn(put, took[:, : 2 * C])).astype(BF)
    update[...] = nn(sums[:, :C], w_out[...]).astype(BF)
    grad_in[...] = sums[:, C:]
    for src, half in ((got_last, core()), (took, 1 - core())):
        rows = pl.ds(pl.multiple_of(half * 128, 128), 128)
        grad_qkv[rows, : 2 * C] = src[:128, 2 * C :].astype(F32)
        grad_qkv[rows, 2 * C :] = src[128:, 2 * C : 3 * C].astype(F32)
        grad_out[rows, :] = src[128:, 3 * C :].astype(F32)


def call(body, outs, flops, *args, scratch=()):
    return pl.pallas_call(
        body,
        out_shape=outs,
        in_specs=[pl.BlockSpec(memory_space=pltpu.VMEM)] * len(args),
        out_specs=[pl.BlockSpec(memory_space=pltpu.VMEM)] * len(outs),
        scratch_shapes=scratch,
        compiler_params=pltpu.CompilerParams(vmem_limit_bytes=40 * 2**20),
        cost_estimate=pl.CostEstimate(flops=flops, bytes_accessed=2**20, transcendentals=2**19),
    )(*args)


def shape(rows, cols, dtype):
    return jax.ShapeDtypeStruct((rows, cols), dtype)


AXES = ("dp", "row", "col")


def device(x, mine, y, z):
    return z % 2 * 256 + (x * 2 + mine) * 32 + y * 4 + z // 2


X, Y, ZS = range(4), range(8), range(8)
LONG = [[device(x, 0, y, z) for y in Y for z in ZS[dp::2]] for x in X for dp in range(2)] + [
    [device(x, 1, y, z) for x in X for z in ZS] for y in Y
]
SHORT = [
    [device(x, 0, y, 2 * z + dp) for x in X for dp in range(2)] for y in Y for z in range(4)
] + [[device(x, 1, y, z) for y in Y] for x in X for z in ZS]


def exchange(rows, groups):
    return lax.all_to_all(
        rows, AXES, split_axis=0, concat_axis=0, axis_index_groups=groups, tiled=True
    )


def swap(rows):
    return lax.ppermute(rows, "row", [(i, i ^ 1) for i in range(8)])


def body(features, w_qkv, w_out, cotangent):
    local_shape = features.shape
    feat = features.reshape(T, C)
    cot = cotangent.reshape(T, C)
    weights = (w_qkv, w_out)
    cube = 2 * T * T * C
    pair = shape(T, 2 * C, BF)
    quad = shape(T, 4 * C, BF)
    (give,) = call(
        functools.partial(pack_body, x_source, y_source), [pair], cube * 2, feat, cot
    )
    took = swap(give)
    (mine,) = call(functools.partial(pack_body, y_source, x_source), [pair], cube * 2, feat, cot)
    (send,) = call(merge_body, [quad], 2**20, mine, took)
    got = exchange(send, LONG)
    back_z, grad_z = call(z_body, [pair, shape(C, 4 * C, BF)], cube * 70, feat, cot, *weights)
    *held, keep, give = call(
        lines_body,
        [shape(C, 2 * T, BF)] * 2
        + [shape(2 * T, C, BF)] * 2
        + [shape(128, 4 * C, F32), shape(128, 4 * C, BF)],
        cube * 140,
        got,
        *weights,
        grad_z,
        scratch=[pltpu.VMEM((C, 4 * C), F32)],
    )
    took = swap(give)
    back_out, back_feat = call(back_body, [pair] * 2, cube * 20, *held, w_qkv)
    (send,) = call(first_pack_body, [quad], 2**20, back_out, keep, took)
    got_first = exchange(send, LONG)
    (send,) = call(block_body, [shape(64, 2 * C, BF)], 2**20, got_first)
    blocks = exchange(send, SHORT)
    factor = 1.0 / math.sqrt(PATCHES * 64 * 64 * 16)
    (send,) = call(functools.partial(last_pack_body, factor), [quad], 2**20, blocks, back_feat)
    got_last = exchange(send, LONG)
    (give,) = call(give_body, [quad], 2**20, got_first, got_last)
    took = swap(give)
    (part,) = call(
        own_sum_body, [shape(T, 2 * C, F32)], cube * 2, back_z, got_first, got_last
    )
    update, grad_in, grad_qkv, grad_out = call(
        final_body,
        [shape(T, C, BF)] * 2 + [shape(C, 3 * C, F32), shape(C, C, F32)],
        cube * 6,
        part,
        got_last,
        took,
        w_out,
    )
    return (update.reshape(local_shape), grad_in.reshape(local_shape), grad_qkv, grad_out)


def solution(mesh):
    placed = (P("dp", "col", "row", None, None), P(), P(), P("dp", "col", "row", None, None))
    return jax.shard_map(
        body,
        mesh=mesh,
        in_specs=placed,
        out_specs=(P("dp", "col", "row", None, None), P("dp", "col", "row", None, None), P(), P()),
        check_vma=False,
    )
```
